512 devices in a mesh: skyy: 16 (over y, x_hi), skyx: 32 (over x_lo, z, core).
Axes of the slice: x: 4 (x_hi: 2, x_lo: 2; x = x_hi * 2 + x_lo), y: 8, z: 8, core: 2. Of those that a mesh axis runs over, the one named last changes fastest.
Arguments:
- cube: float32 [256, 512, 512], P('skyy', 'skyx'), may hold values from -8 to 8
- level_table: float32 [16], replicated, may hold values from 0.05 to 0.6
- level_index: int32 [4, 512], replicated, may hold values from 0 to 15
- amplitude: float32 [8, 256, 512], P(None, 'skyy', 'skyx'), may hold values from 0.3 to 2
- centre_index: int32 [8, 256, 512], P(None, 'skyy', 'skyx'), may hold values from 0 to 511
- spread: float32 [8, 256, 512], P(None, 'skyy', 'skyx'), may hold values from 3 to 30
Outputs:
- denoised: float32 [256, 512, 512], P('skyy', 'skyx')
- fitted: float32 [3, 8, 256, 512], P(None, None, 'skyy', 'skyx')
The draws below stay inside these ranges and needn't reach their ends.
All inputs are finite; a program needn't handle non-finite values.
Results may differ from the reference program's by a relative error of at most 0.00002.
Values sent between devices are 32-bit elements; how exact they have to be, the bound alone decides.
No kernel may reach another device: no remote copies, remote signals or barrier semaphores. Data moves between devices by JAX's collectives and lax.ppermute only.
A program may use at most 64 MiB of HBM per device.

```python
import math
import jax
import jax.numpy as jnp
from jax import lax

NCH = 512
KG = 8
LEVELS = 4
TABLE = 16
NY = 256
NX = 512


def with_ends(entries, stream_key, least, high):
    index_at = [jax.random.randint(jax.random.fold_in(stream_key, axis), (), 0, length) for axis, length in enumerate(entries.shape)]
    main_axis = entries.shape.index(max(entries.shape))
    next_to = index_at[:main_axis] + [(index_at[main_axis] + 1) % entries.shape[main_axis]] + index_at[main_axis + 1:]
    return entries.at[tuple(index_at)].set(least).at[tuple(next_to)].set(high)


def level_of(rng, shape, shards, least, largest):
    def one(position, parts):
        heights = jax.random.uniform(jax.random.fold_in(jax.random.fold_in(rng, 6), position), (parts,), jnp.float32, least / len(shards), largest / len(shards))
        return jnp.repeat(jnp.exp(heights), shape[position] // parts).reshape((-1,) + (1,) * (len(shape) - position - 1))

    gain = one(*shards[0])
    for cut in shards[1:]:
        gain = gain * one(*cut)
    return gain


def scatter_about(key, shape, scale, bound, pieces=(), kind=jnp.bfloat16):
    result = scale * jax.random.normal(key, shape, jnp.float32)
    if pieces:
        result = result * level_of(key, shape, pieces, -0.22, 0.18)
    return jnp.clip(result, -bound, bound).astype(kind)


def setup_inputs(seed: int = 0) -> dict:
    arg_keys = jax.random.split(jax.random.key(seed), 7)
    return {
        "cube": scatter_about(arg_keys[0], (NY, NX, NCH), 1.0, 8.0, ((0, 16), (1, 32)), jnp.float32),
        "level_table": jnp.clip(jnp.exp(jax.random.uniform(arg_keys[1], (TABLE,), jnp.float32, math.log(0.05), math.log(0.6))), 0.05, 0.6),
        "level_index": with_ends(jax.random.randint(arg_keys[2], (LEVELS, NCH), 0, TABLE), jax.random.fold_in(arg_keys[2], 1), 0, TABLE - 1).astype(jnp.int32),
        "amplitude": jnp.clip(jnp.exp(math.log(2.0) - 1.89712 * jax.random.uniform(arg_keys[3], (KG, NY, NX), jnp.float32) ** level_of(arg_keys[3], (KG, NY, NX), ((1, 16), (2, 32)), -0.2, 0.2)), 0.3, 2.0),
        "centre_index": with_ends(jax.random.randint(arg_keys[4], (KG, NY, NX), 0, NCH), jax.random.fold_in(arg_keys[4], 1), 0, NCH - 1).astype(jnp.int32),
        "spread": jnp.clip(jnp.exp(math.log(30.0) - 2.3025851 * jax.random.uniform(arg_keys[5], (KG, NY, NX), jnp.float32) ** level_of(arg_keys[5], (KG, NY, NX), ((1, 16), (2, 32)), -0.2, 0.2)), 3.0, 30.0),
    }


def smoothed_mirror_input(mirror_padded, target_axis, hole_spacing, axis_length):
    def gather_shifted(offset):
        return lax.slice_in_dim(mirror_padded, offset, offset + axis_length, axis=target_axis)
    return (gather_shifted(0) + gather_shifted(4 * hole_spacing) + 4.0 * (gather_shifted(hole_spacing) + gather_shifted(3 * hole_spacing)) + 6.0 * gather_shifted(2 * hole_spacing)) / 16.0


def starlet_smoother(image_plane, target_axis, hole_spacing):
    padding_widths = [(0, 0), (0, 0), (0, 0)]
    padding_widths[target_axis] = (2 * hole_spacing, 2 * hole_spacing)
    return smoothed_mirror_input(jnp.pad(image_plane, padding_widths), target_axis, hole_spacing, image_plane.shape[target_axis])


def laplace(params):
    mirror_padded = jnp.pad(params, ((0, 0), (0, 0), (1, 1), (1, 1)))
    inner = mirror_padded[:, :, 1:-1, 1:-1]
    return 4.0 * inner - (mirror_padded[:, :, :-2, 1:-1] + mirror_padded[:, :, 2:, 1:-1] + mirror_padded[:, :, 1:-1, :-2] + mirror_padded[:, :, 1:-1, 2:])


def reference(cube, level_table, level_index, amplitude, centre_index, spread):
    weight = level_table[level_index]
    present_plane = cube
    total = jnp.zeros_like(cube)
    for scale_level in range(LEVELS):
        hole_spacing = 2 ** scale_level
        next_plane = starlet_smoother(starlet_smoother(starlet_smoother(present_plane, 2, hole_spacing), 0, hole_spacing), 1, hole_spacing)
        total = total + weight[scale_level][None, None, :] * (present_plane - next_plane)
        present_plane = next_plane
    denoised = total + present_plane
    chans = jnp.arange(NCH, dtype=jnp.float32)
    frac = (centre_index.astype(jnp.float32) + 0.5) / NCH
    centre = frac * NCH

    def add_model(acc, item):
        amp, mu, sig = item
        diff = chans[None, None, :] - mu[:, :, None]
        bump = jnp.exp(-diff * diff / (2.0 * sig[:, :, None] * sig[:, :, None]))
        return acc + amp[:, :, None] * bump, None

    model, _ = lax.scan(add_model, jnp.zeros_like(cube), (amplitude, centre, spread))
    resid = model - denoised

    def grads(item):
        amp, mu, sig = item
        sig3 = sig[:, :, None]
        diff = chans[None, None, :] - mu[:, :, None]
        bump = jnp.exp(-diff * diff / (2.0 * sig3 * sig3))
        g_amp = jnp.sum(resid * bump, axis=2) / NCH
        term = resid * amp[:, :, None] * bump * diff / (sig3 * sig3)
        g_pos = jnp.sum(term, axis=2)
        g_sig = jnp.sum(term * diff / sig3, axis=2) / NCH
        return jnp.stack([g_amp, g_pos, g_sig])

    gathered = lax.map(grads, (amplitude, centre, spread))
    gradient = jnp.transpose(gathered, (1, 0, 2, 3))
    params = jnp.stack([amplitude, frac, spread])
    smoothing = laplace(laplace(params))
    steps = jnp.array([0.5, 0.002, 2.0], jnp.float32)[:, None, None, None]
    lams = jnp.array([0.2, 0.5, 0.05], jnp.float32)[:, None, None, None]
    fitted = params - steps * (gradient + lams * smoothing)
    return denoised, fitted
```

```python
import functools
import math

import jax
import jax.numpy as jnp
import numpy as np
from jax import lax
from jax.experimental import pallas as pl
from jax.experimental.pallas import tpu as pltpu
from jax.sharding import PartitionSpec as P

TILE = 16
LEVELS = 4
COMPS = 8
LANES = 128
TAPS = (1, 4, 6, 4, 1)
VMEM_LIMIT = 56 * 1024 * 1024
STEPS = (0.5, 0.002, 2.0)
LAMS = (0.2, 0.5, 0.05)


def blur_matrix(length, gap):
    out = np.zeros((length, length), np.float64)
    for tap, factor in enumerate(TAPS):
        offset = (tap - 2) * gap
        for i in range(max(0, -offset), min(length, length - offset)):
            out[i, i + offset] = factor
    return out


def composites(length):
    made, now = [], np.eye(length)
    for level in range(LEVELS):
        now = blur_matrix(length, 2**level) @ now
        made.append(now)
    return made


def halves(matrix):
    bf16 = jnp.bfloat16
    high = np.asarray(matrix, np.float32).astype(bf16)
    low = (np.asarray(matrix, np.float32) - high.astype(np.float32)).astype(bf16)
    return high, low


def channel_matrices(nch):
    return np.stack([np.stack(halves(m.T)) for m in composites(nch)])


def scatter_matrices(length):
    whole = composites(length)
    kinds = []
    for start in (0, TILE * (length // TILE // 2), length - TILE):
        parts = []
        for m in whole:
            block = np.zeros((5 * TILE, TILE))
            for k in range(5 * TILE):
                at = start - 2 * TILE + k
                if 0 <= at < length:
                    block[k] = m[at, start : start + TILE]
            parts.append(halves(block))
        high = np.concatenate([p[0] for p in parts], axis=1)
        low = np.concatenate([p[1] for p in parts[2:]], axis=1)
        kinds.append(np.concatenate([high, high, low], axis=1))
    return np.stack(kinds)


def sent(values, axis, by):
    size = lax.axis_size(axis)
    if by > 0:
        pairs = [(i, i + by) for i in range(size - by)]
    else:
        pairs = [(i, i + by) for i in range(-by, size)]
    return lax.ppermute(values, axis, pairs)


def five(v, flag=None):
    total = (v[0] + v[4]) + 4.0 * (v[1] + v[3]) + 6.0 * v[2]
    return total if flag is None else total * flag


def split(v):
    high = v.astype(jnp.bfloat16)
    return high, (v - high.astype(jnp.float32)).astype(jnp.bfloat16)


def wavelet_kernel(
    kind_ref, flag_ref, a_ref, m2, m1, x_ref, p1, p2, w_ref, k_ref,
    o_m2, o_m1, o_0, o_p1, o_p2, rows_ref, y_ref,
):
    nch = x_ref.shape[2]
    tiles = (m2, m1, x_ref, p1, p2)
    outs = (o_m2, o_m1, o_0, o_p1, o_p2)
    flags = [flag_ref[i] for i in range(5)]

    lane_tiles = nch // LANES

    def row_pass(step, carry):
        sub = pl.ds(pl.multiple_of((step // lane_tiles) * 8, 8), 8)
        lane = pl.ds(pl.multiple_of((step % lane_tiles) * LANES, LANES), LANES)

        @functools.cache
        def value(level, at):
            tile = (at + 2 * TILE) // TILE
            if level == 0:
                return tiles[tile][at % TILE, sub, lane]
            gap = 2 ** (level - 1)
            taps = [value(level - 1, at + (t - 2) * gap) for t in range(5)]
            return five(taps, None if tile == 2 else flags[tile])

        reach = {1: 28, 2: 24, 3: 16, 4: 0}
        lag = {1: 2, 2: 6, 3: 14, 4: 30}
        for at in range(-30, TILE + 30):
            value(0, at)
            for level in range(1, LEVELS + 1):
                row = at - lag[level]
                if -reach[level] <= row < TILE + reach[level]:
                    got = value(level, row)
                    if 0 <= row < TILE:
                        rows_ref[level - 1, row, sub, lane] = got
        return carry

    lax.fori_loop(0, 2 * lane_tiles, row_pass, 0)

    half = nch // 2
    pixels = TILE * TILE

    def channel_pass(step, carry):
        level = step // 2
        lane = pl.ds(pl.multiple_of((step % 2) * half, half), half)
        high, low = split(rows_ref[level].reshape(pixels, nch))
        w_high = w_ref[level, 0, :, lane]
        dot = functools.partial(jnp.dot, preferred_element_type=jnp.float32)
        got = dot(high, w_high) + dot(low, w_high) + dot(high, w_ref[level, 1, :, lane])
        got = got * a_ref[level + 1, :, lane]
        high, low = split(got)
        high = high.reshape(TILE, TILE, half)
        at = pl.ds(pl.multiple_of(level * TILE, TILE), TILE)
        y_ref[:, at, lane] = high
        at = pl.ds(pl.multiple_of((level + LEVELS) * TILE, TILE), TILE)
        y_ref[:, at, lane] = low.reshape(TILE, TILE, half)

        @pl.when(level >= 2)
        def _():
            at = pl.ds(pl.multiple_of((level + 6) * TILE, TILE), TILE)
            y_ref[:, at, lane] = high

        return carry

    lax.fori_loop(0, 2 * LEVELS, channel_pass, 0)

    columns = k_ref[kind_ref[0]]

    def column_pass(row, carry):
        got = jnp.dot(columns, y_ref[row], preferred_element_type=jnp.float32)
        for i, out in enumerate(outs):
            part = got[i * TILE : (i + 1) * TILE]
            if i == 2:
                part = part + a_ref[0] * x_ref[row]
            out[row] = part
        return carry

    lax.fori_loop(0, TILE, column_pass, 0)


def wavelet_parts(kind, flags, coeff, tiles, nch, length):
    w = jnp.asarray(channel_matrices(nch))
    k = jnp.asarray(scatter_matrices(length))
    smem = pl.BlockSpec(memory_space=pltpu.SMEM)
    vmem = pl.BlockSpec(memory_space=pltpu.VMEM)
    shape = jax.ShapeDtypeStruct(tiles[2].shape, jnp.float32)
    return pl.pallas_call(
        wavelet_kernel,
        out_shape=[shape] * 5,
        in_specs=[smem, smem] + [vmem] * 8,
        out_specs=[vmem] * 5,
        scratch_shapes=[
            pltpu.VMEM((LEVELS, TILE, TILE, nch), jnp.float32),
            pltpu.VMEM((TILE, 10 * TILE, nch), jnp.bfloat16),
        ],
        compiler_params=pltpu.CompilerParams(vmem_limit_bytes=VMEM_LIMIT),
        cost_estimate=pl.CostEstimate(flops=4_000_000_000, bytes_accessed=9_000_000, transcendentals=0),
        name="wavelet_parts",
    )(kind, flags, coeff, *tiles, w, k)


def model_kernel(amp_ref, mu_ref, s_ref, model_ref):
    nch, pixels = model_ref.shape

    def body(step, carry):
        base = pl.multiple_of(step * 8, 8)
        chan = (lax.broadcasted_iota(jnp.int32, (8, pixels), 0) + base).astype(jnp.float32)
        total = jnp.zeros((8, pixels), jnp.float32)
        for k in range(COMPS):
            diff = chan - mu_ref[k : k + 1, :]
            total += amp_ref[k : k + 1, :] * jnp.exp2(diff * diff * s_ref[k : k + 1, :])
        model_ref[pl.ds(base, 8), :] = total
        return carry

    lax.fori_loop(0, nch // 8, body, 0)


def model_of(amp, mu, s, nch):
    vmem = pl.BlockSpec(memory_space=pltpu.VMEM)
    return pl.pallas_call(
        model_kernel,
        out_shape=jax.ShapeDtypeStruct((nch, amp.shape[1]), jnp.float32),
        in_specs=[vmem] * 3,
        out_specs=vmem,
        compiler_params=pltpu.CompilerParams(vmem_limit_bytes=VMEM_LIMIT),
        cost_estimate=pl.CostEstimate(flops=10_000_000, bytes_accessed=600_000, transcendentals=1_100_000),
        name="gaussian_model",
    )(amp, mu, s)


def step_kernel(
    o_0, o_m2, o_m1, o_p1, o_p2, model_ref, amp_ref, mu_ref, s_ref, inv_ref, base_ref,
    den_ref, fit_ref, r_ref,
):
    nch, pixels = model_ref.shape
    for row in range(TILE):
        got = o_0[row] + ((o_m2[row] + o_m1[row]) + (o_p1[row] + o_p2[row]))
        den_ref[row] = got
    for part in range(pixels // LANES):
        rows = LANES // TILE
        block = den_ref[part * rows : (part + 1) * rows].reshape(LANES, nch)
        at = slice(part * LANES, (part + 1) * LANES)
        r_ref[:, at] = model_ref[:, at] - block.T

    for part in range(pixels // LANES):
        at = slice(part * LANES, (part + 1) * LANES)
        sums = [[] for _ in range(3)]
        for first in range(0, COMPS, 4):
            chosen = range(first, first + 4)
            mus = [jnp.broadcast_to(mu_ref[k : k + 1, at], (8, LANES)) for k in chosen]
            scales = [jnp.broadcast_to(s_ref[k : k + 1, at], (8, LANES)) for k in chosen]

            def body(step, carry):
                chan = (lax.broadcasted_iota(jnp.int32, (8, LANES), 0) + step * 8).astype(jnp.float32)
                r = r_ref[pl.ds(pl.multiple_of(step * 8, 8), 8), at]
                out = []
                for mu, scale, (a, b, c) in zip(mus, scales, carry):
                    diff = chan - mu
                    one = r * jnp.exp2(diff * diff * scale)
                    two = one * diff
                    out.append((a + one, b + two, c + two * diff))
                return tuple(out)

            zero = jnp.zeros((8, LANES), jnp.float32)
            done = lax.fori_loop(0, nch // 8, body, ((zero,) * 3,) * 4, unroll=4)
            for four in done:
                for t in range(3):
                    sums[t].append(jnp.sum(four[t], axis=0, keepdims=True))
        amp = amp_ref[:, at]
        inv = inv_ref[:, at]
        slope = amp * inv * inv
        grads = (
            jnp.concatenate(sums[0], axis=0) * (1.0 / nch),
            jnp.concatenate(sums[1], axis=0) * slope,
            jnp.concatenate(sums[2], axis=0) * (slope * inv * (1.0 / nch)),
        )
        for t in range(3):
            fit_ref[t, :, at] = base_ref[t, :, at] - STEPS[t] * grads[t]


def gradient_step(parts, model, amp, mu, s, inv, base):
    vmem = pl.BlockSpec(memory_space=pltpu.VMEM)
    return pl.pallas_call(
        step_kernel,
        out_shape=[
            jax.ShapeDtypeStruct(parts[0].shape, jnp.float32),
            jax.ShapeDtypeStruct(base.shape, jnp.float32),
        ],
        in_specs=[vmem] * 11,
        out_specs=[vmem] * 2,
        scratch_shapes=[pltpu.VMEM(model.shape, jnp.float32)],
        compiler_params=pltpu.CompilerParams(vmem_limit_bytes=VMEM_LIMIT),
        cost_estimate=pl.CostEstimate(flops=15_000_000, bytes_accessed=4_000_000, transcendentals=1_100_000),
        name="gradient_step",
    )(*parts, model, amp, mu, s, inv, base)


def stencil(p):
    return 4.0 * p[:, :, 1:-1, 1:-1] - (
        p[:, :, :-2, 1:-1] + p[:, :, 2:, 1:-1] + p[:, :, 1:-1, :-2] + p[:, :, 1:-1, 2:]
    )


def inside(axis, length, border):
    at = jnp.arange(-border, length + border) + lax.axis_index(axis) * length
    return ((at >= 0) & (at < length * lax.axis_size(axis))).astype(jnp.float32)


def on_device(cube, level_table, level_index, amplitude, centre_index, spread):
    nch = cube.shape[2]
    pixels = TILE * TILE

    up1, down1 = sent(cube, "skyy", 1), sent(cube, "skyy", -1)
    up2, down2 = sent(cube, "skyy", 2), sent(cube, "skyy", -2)
    frac = (centre_index.astype(jnp.float32) + 0.5) / nch
    params = jnp.stack([amplitude, frac, spread])
    above = sent(params[:, :, -2:, :], "skyy", 1)
    below = sent(params[:, :, :2, :], "skyy", -1)

    entries = jnp.arange(level_table.shape[0], dtype=jnp.int32)
    picks = (level_index[:, :, None] == entries).astype(jnp.float32)
    weight = jnp.sum(picks * level_table, axis=2)
    one = jnp.ones((1, nch), jnp.float32)
    coeff = jnp.concatenate([weight, one]) - jnp.concatenate([0.0 * one, weight])
    scale = jnp.array([16.0 ** (-3 * j) for j in range(LEVELS + 1)], jnp.float32)
    coeff = (coeff * scale[:, None])[:, None, :]

    amp = amplitude.reshape(COMPS, pixels)
    mu = (frac * nch).reshape(COMPS, pixels)
    inv = 1.0 / spread.reshape(COMPS, pixels)
    s = (-0.5 * math.log2(math.e)) * inv * inv
    model = model_of(amp, mu, s, nch)

    iy, ny = lax.axis_index("skyy"), lax.axis_size("skyy")
    ix, nx = lax.axis_index("skyx"), lax.axis_size("skyx")
    near = iy + jnp.arange(-2, 3)
    flags = ((near >= 0) & (near < ny)).astype(jnp.float32)
    kind = jnp.where(ix == 0, 0, jnp.where(ix == nx - 1, 2, 1)).astype(jnp.int32)[None]
    o_m2, o_m1, o_0, o_p1, o_p2 = wavelet_parts(
        kind, flags, coeff, (up2, up1, cube, down1, down2), nch, nx * TILE
    )

    from_left1, from_right1 = sent(o_p1, "skyx", 1), sent(o_m1, "skyx", -1)
    from_left2, from_right2 = sent(o_p2, "skyx", 2), sent(o_m2, "skyx", -2)
    tall = jnp.concatenate([above, params, below], axis=2)
    left = sent(tall[:, :, :, -2:], "skyx", 1)
    right = sent(tall[:, :, :, :2], "skyx", -1)
    wide = jnp.concatenate([left, tall, right], axis=3)
    first = stencil(wide) * (inside("skyy", TILE, 1)[:, None] * inside("skyx", TILE, 1))
    smoothing = stencil(first)
    rate = jnp.array([a * b for a, b in zip(STEPS, LAMS)], jnp.float32)[:, None, None, None]
    base = (params - rate * smoothing).reshape(3, COMPS, pixels)

    denoised, fitted = gradient_step(
        (o_0, from_left2, from_left1, from_right1, from_right2), model, amp, mu, s, inv, base
    )
    return denoised, fitted.reshape(3, COMPS, TILE, TILE)


def solution(mesh):
    placed = (
        P("skyy", "skyx", None),
        P(),
        P(),
        P(None, "skyy", "skyx"),
        P(None, "skyy", "skyx"),
        P(None, "skyy", "skyx"),
    )
    return jax.shard_map(
        on_device,
        mesh=mesh,
        in_specs=placed,
        out_specs=(P("skyy", "skyx", None), P(None, None, "skyy", "skyx")),
        check_vma=False,
    )
```

```python
import functools
import math

import jax
import jax.numpy as jnp
import numpy as np
from jax import lax
from jax.experimental import pallas as pl
from jax.experimental.pallas import tpu as pltpu
from jax.sharding import PartitionSpec as P

TILE = 16
LEVELS = 4
COMPS = 8
LANES = 128
TAPS = (1, 4, 6, 4, 1)
BEYOND = 2
W_ORDER = (0, 1, 2, 4, 3, 5)
VMEM_LIMIT = 20 * 1024 * 1024
PITCH = 32
EXT = 20 * PITCH
STEPS = (0.5, 0.002, 2.0)
LAMS = (0.2, 0.5, 0.05)


def blur_matrix(length, gap):
    out = np.zeros((length, length), np.float64)
    for tap, factor in enumerate(TAPS):
        offset = (tap - 2) * gap
        for i in range(max(0, -offset), min(length, length - offset)):
            out[i, i + offset] = factor
    return out


def composites(length):
    made, now = [], np.eye(length)
    for level in range(LEVELS):
        now = blur_matrix(length, 2**level) @ now
        made.append(now)
    return made


def halves(matrix):
    bf16 = jnp.bfloat16
    high = np.asarray(matrix, np.float32).astype(bf16)
    low = (np.asarray(matrix, np.float32) - high.astype(np.float32)).astype(bf16)
    return high, low


def channel_matrices(nch):
    parts = [halves(m.T) for m in composites(nch)]
    return np.stack([p[0] for p in parts] + [p[1] for p in parts[2:]])


def scatter_matrices(length):
    whole = composites(length)
    kinds = []
    for start in (0, TILE * (length // TILE // 2), length - TILE):
        parts = []
        for m in whole:
            block = np.zeros((5 * TILE, TILE))
            for k in range(5 * TILE):
                at = start - 2 * TILE + k
                if 0 <= at < length:
                    block[k] = m[at, start : start + TILE]
            parts.append(halves(block))
        high = np.concatenate([p[0] for p in parts], axis=1)
        low = np.concatenate([p[1] for p in parts[2:]], axis=1)
        kinds.append(np.concatenate([high, high, low], axis=1))
    return np.stack(kinds)


def sent(values, axis, by):
    size = lax.axis_size(axis)
    if by > 0:
        pairs = [(i, i + by) for i in range(size - by)]
    else:
        pairs = [(i, i + by) for i in range(-by, size)]
    return lax.ppermute(values, axis, pairs)


def own_row(t, row, amp_ref, index_ref, spread_ref, nch):
    if t == 0:
        return amp_ref[:, row, :]
    if t == 1:
        return (index_ref[:, row, :].astype(jnp.float32) + 0.5) * (1.0 / nch)
    return spread_ref[:, row, :]


def pack_kernel(x_ref, amp_ref, index_ref, spread_ref, up_ref, down_ref):
    nch = x_ref.shape[2]
    for out, first in ((up_ref, TILE - 2), (down_ref, 0)):
        for row in range(TILE):
            out[row] = x_ref[row]
        out[TILE] = jnp.zeros((TILE, nch), jnp.float32)
        for t in range(3):
            for r in range(2):
                lane = (2 * t + r) * TILE
                got = own_row(t, first + r, amp_ref, index_ref, spread_ref, nch)
                out[TILE, 0:COMPS, lane : lane + TILE] = got


def packed(cube, amplitude, centre_index, spread):
    vmem = pl.BlockSpec(memory_space=pltpu.VMEM)
    shape = (TILE + 1,) + cube.shape[1:]
    return pl.pallas_call(
        pack_kernel,
        out_shape=[pltpu.VMEM(shape, jnp.float32)] * 2,
        in_specs=[vmem] * 4,
        out_specs=[vmem] * 2,
        compiler_params=pltpu.CompilerParams(vmem_limit_bytes=VMEM_LIMIT),
        cost_estimate=pl.CostEstimate(flops=1000, bytes_accessed=1_000_000, transcendentals=0),
        name="pack",
    )(*[pltpu.with_memory_space_constraint(v, pltpu.HBM) for v in (cube, amplitude, centre_index, spread)])


def put_columns(out, ext_ref, shift):
    lane = lax.broadcasted_iota(jnp.int32, (COMPS, EXT), 1) % PITCH
    total = jnp.zeros((COMPS, EXT), jnp.float32)
    for t in range(3):
        moved = pltpu.roll(ext_ref[t], (2 * t - shift) % EXT, 1)
        total = jnp.where((lane >= 2 * t) & (lane < 2 * t + 2), moved, total)
    nch = out.shape[2]
    out[TILE] = jnp.zeros((TILE, nch), jnp.float32)
    out[TILE, 0:COMPS, :] = total[:, :nch]
    out[TILE, COMPS:, 0 : EXT - nch] = total[:, nch:]


def stencil(p):
    near = pltpu.roll(p, 1, 1) + pltpu.roll(p, EXT - 1, 1)
    return 4.0 * p - (near + (pltpu.roll(p, PITCH, 1) + pltpu.roll(p, EXT - PITCH, 1)))


def smoothed(ext_ref, left, right, place_ref):
    nch = left.shape[2]
    lane = lax.broadcasted_iota(jnp.int32, (COMPS, EXT), 1)
    row, column = lane // PITCH, lane % PITCH
    y = row + (place_ref[0] * TILE - 2)
    x = column + (place_ref[2] * TILE - 2)
    on_sky = (y >= 0) & (y < place_ref[1] * TILE) & (x >= 0) & (x < place_ref[3] * TILE)
    sides = [
        jnp.concatenate([ref[TILE, 0:COMPS, :], ref[TILE, COMPS:, 0 : EXT - nch]], axis=1)
        for ref in (left, right)
    ]
    out = []
    for t in range(3):
        p = ext_ref[t]
        p = jnp.where(column < 2, pltpu.roll(sides[0], (EXT - 2 * t) % EXT, 1), p)
        p = jnp.where(column >= TILE + 2, pltpu.roll(sides[1], (TILE + 2 - 2 * t) % EXT, 1), p)
        first = jnp.where(on_sky, stencil(p), 0.0)
        out.append(p - (STEPS[t] * LAMS[t]) * stencil(first))
    return out


def five(v, flag=None):
    total = (v[0] + v[4]) + 4.0 * (v[1] + v[3]) + 6.0 * v[2]
    return total if flag is None else total * flag


def split(v):
    high = v.astype(jnp.bfloat16)
    return high, (v - high.astype(jnp.float32)).astype(jnp.bfloat16)


def wavelet_kernel(
    place_ref, a_ref, m1, p1, m2, p2, x_ref, k_ref, own_ref, w_hbm,
    o_m2, o_m1, o_0, o_p1, o_p2, ext_ref, rows_ref, y_ref, w_ref, sems,
):
    nch = x_ref.shape[2]
    tiles = (m2, m1, x_ref, p1, p2)
    outs = (o_m2, o_m1, o_0, o_p1, o_p2)
    near = [place_ref[0] + i for i in (-2, -1, 0, 1, 2)]
    flags = [jnp.where((i >= 0) & (i < place_ref[1]), 1.0, 0.0) for i in near]
    loads = [pltpu.make_async_copy(w_hbm.at[i], w_ref.at[i], sems.at[i]) for i in range(LEVELS + 2)]
    for i in W_ORDER:
        loads[i].start()

    lane_tiles = nch // LANES

    def row_pass(step, carry):
        sub = pl.ds(pl.multiple_of((step // lane_tiles) * 8, 8), 8)
        lane = pl.ds(pl.multiple_of((step % lane_tiles) * LANES, LANES), LANES)

        @functools.cache
        def value(level, at):
            tile = (at + 2 * TILE) // TILE
            if level == 0:
                return tiles[tile][at % TILE - (BEYOND if tile == 0 else 0), sub, lane]
            gap = 2 ** (level - 1)
            taps = [value(level - 1, at + (t - 2) * gap) for t in range(5)]
            return five(taps, None if tile == 2 else flags[tile])

        reach = {1: 28, 2: 24, 3: 16, 4: 0}
        lag = {1: 2, 2: 6, 3: 14, 4: 30}
        for at in range(-30, TILE + 30):
            value(0, at)
            for level in range(1, LEVELS + 1):
                row = at - lag[level]
                if -reach[level] <= row < TILE + reach[level]:
                    got = value(level, row)
                    if 0 <= row < TILE:
                        rows_ref[level - 1, row, sub, lane] = got
        return carry

    lax.fori_loop(0, 2 * lane_tiles, row_pass, 0)

    pixels = TILE * TILE
    dot = functools.partial(jnp.dot, preferred_element_type=jnp.float32)
    for level in range(LEVELS):
        high, low = split(rows_ref[level].reshape(pixels, nch))
        loads[level].wait()
        got = dot(high, w_ref[level]) + dot(low, w_ref[level])
        if level >= 2:
            loads[level + 2].wait()
            got = got + dot(high, w_ref[level + 2])
        high, low = split(got * a_ref[level + 1])
        high = high.reshape(TILE, TILE, nch)
        y_ref[:, level * TILE : (level + 1) * TILE] = high
        at = (level + LEVELS) * TILE
        y_ref[:, at : at + TILE] = low.reshape(TILE, TILE, nch)
        if level >= 2:
            at = (level + 6) * TILE
            y_ref[:, at : at + TILE] = high

    kind = jnp.where(place_ref[2] == 0, 0, jnp.where(place_ref[2] == place_ref[3] - 1, 2, 1))
    columns = k_ref[kind]

    def column_pass(row, carry):
        got = dot(columns, y_ref[row])
        for i, out in enumerate(outs):
            part = got[i * TILE : (i + 1) * TILE]
            if i == 2:
                part = part + a_ref[0] * x_ref[row]
            out[row] = part
        return carry

    lax.fori_loop(0, TILE, column_pass, 0, unroll=4)

    ext_ref[...] = own_ref[...]
    for t in range(3):
        for r in range(2):
            lane = (2 * t + r) * TILE
            at = r * PITCH + 2
            ext_ref[t, :, at : at + TILE] = m1[TILE, 0:COMPS, lane : lane + TILE]
            at = (TILE + 2 + r) * PITCH + 2
            ext_ref[t, :, at : at + TILE] = p1[TILE, 0:COMPS, lane : lane + TILE]
    put_columns(o_p1, ext_ref, TILE)
    put_columns(o_m1, ext_ref, 2)


def kept(x):
    return pltpu.with_memory_space_constraint(x, pltpu.VMEM)


def wavelet_parts(place, coeff, tiles, own, nch, length):
    w = jnp.asarray(channel_matrices(nch))
    k = jnp.asarray(scatter_matrices(length))
    smem = pl.BlockSpec(memory_space=pltpu.SMEM)
    vmem = pl.BlockSpec(memory_space=pltpu.VMEM)
    plain = pltpu.VMEM(tiles[-1].shape, jnp.float32)
    taller = pltpu.VMEM(tiles[0].shape, jnp.float32)
    return pl.pallas_call(
        wavelet_kernel,
        out_shape=[plain, taller, plain, taller, plain, pltpu.VMEM(own.shape, jnp.float32)],
        in_specs=[smem] + [vmem] * 8 + [pl.BlockSpec(memory_space=pl.ANY)],
        out_specs=[vmem] * 6,
        scratch_shapes=[
            pltpu.VMEM((LEVELS, TILE, TILE, nch), jnp.float32),
            pltpu.VMEM((TILE, 10 * TILE, nch), jnp.bfloat16),
            pltpu.VMEM(w.shape, jnp.bfloat16),
            pltpu.SemaphoreType.DMA((LEVELS + 2,)),
        ],
        compiler_params=pltpu.CompilerParams(vmem_limit_bytes=VMEM_LIMIT),
        cost_estimate=pl.CostEstimate(flops=4_000_000_000, bytes_accessed=9_000_000, transcendentals=0),
        name="wavelet_parts",
    )(place, *[kept(x) for x in (coeff, *tiles, k, own)], pltpu.with_memory_space_constraint(w, pltpu.HBM))


def model_kernel(amp_ref, index_ref, spread_ref, model_ref, flat_ref, own_ref, scale_ref):
    nch, pixels = model_ref.shape
    own_ref[...] = jnp.zeros_like(own_ref)
    for t in range(3):
        for row in range(TILE):
            got = own_row(t, row, amp_ref, index_ref, spread_ref, nch)
            at = (row + 2) * PITCH + 2
            own_ref[t, :, at : at + TILE] = got
            flat_ref[t, :, row * TILE : (row + 1) * TILE] = got
    mu = flat_ref[1] * float(nch)
    inv = 1.0 / flat_ref[2]
    flat_ref[1] = mu
    flat_ref[2] = inv
    scale_ref[...] = (-0.5 * math.log2(math.e)) * inv * inv

    def body(step, carry):
        base = pl.multiple_of(step * 8, 8)
        chan = (lax.broadcasted_iota(jnp.int32, (8, pixels), 0) + base).astype(jnp.float32)
        total = jnp.zeros((8, pixels), jnp.float32)
        for k in range(COMPS):
            diff = chan - flat_ref[1, k : k + 1, :]
            bump = jnp.exp2(diff * diff * scale_ref[k : k + 1, :])
            total += flat_ref[0, k : k + 1, :] * bump
        model_ref[pl.ds(base, 8), :] = total
        return carry

    lax.fori_loop(0, nch // 8, body, 0, unroll=2)


def model_of(amplitude, centre_index, spread, nch):
    vmem = pl.BlockSpec(memory_space=pltpu.VMEM)
    pixels = TILE * TILE
    return pl.pallas_call(
        model_kernel,
        out_shape=[
            pltpu.VMEM((nch, pixels), jnp.float32),
            pltpu.VMEM((3, COMPS, pixels), jnp.float32),
            pltpu.VMEM((3, COMPS, EXT), jnp.float32),
        ],
        in_specs=[vmem] * 3,
        out_specs=[vmem] * 3,
        scratch_shapes=[pltpu.VMEM((COMPS, pixels), jnp.float32)],
        compiler_params=pltpu.CompilerParams(vmem_limit_bytes=VMEM_LIMIT),
        cost_estimate=pl.CostEstimate(flops=10_000_000, bytes_accessed=1_000_000, transcendentals=1_100_000),
        name="gaussian_model",
    )(amplitude, centre_index, spread)


def step_kernel(
    place_ref, o_0, o_m2, o_m1, o_p1, o_p2, model_ref, flat_ref, ext_ref,
    den_hbm, fit_ref, den_ref, r_ref, sem,
):
    nch, pixels = model_ref.shape
    rows = LANES // TILE
    parts = pixels // LANES
    copies = []
    bases = smoothed(ext_ref, o_m1, o_p1, place_ref)
    for part in range(parts):
        at = slice(part * rows, (part + 1) * rows)
        for row in range(part * rows, (part + 1) * rows):
            den_ref[row] = o_0[row] + ((o_m2[row] + o_m1[row]) + (o_p1[row] + o_p2[row]))
        copies.append(pltpu.make_async_copy(den_ref.at[at], den_hbm.at[at], sem.at[part]))
        copies[-1].start()

    for part in range(parts):
        block = den_ref[part * rows : (part + 1) * rows].reshape(LANES, nch)
        at = slice(part * LANES, (part + 1) * LANES)
        r_ref[:, at] = model_ref[:, at] - block.T

    for part in range(parts):
        at = slice(part * LANES, (part + 1) * LANES)
        sums = [[] for _ in range(3)]
        for first in range(0, COMPS, 4):
            chosen = range(first, first + 4)
            mus = [jnp.broadcast_to(flat_ref[1, k : k + 1, at], (8, LANES)) for k in chosen]
            inv = [jnp.broadcast_to(flat_ref[2, k : k + 1, at], (8, LANES)) for k in chosen]
            scales = [(-0.5 * math.log2(math.e)) * v * v for v in inv]

            def body(step, carry):
                base = pl.multiple_of(step * 8, 8)
                chan = (lax.broadcasted_iota(jnp.int32, (8, LANES), 0) + base).astype(jnp.float32)
                r = r_ref[pl.ds(base, 8), at]
                out = []
                for mu, scale, (a, b, c) in zip(mus, scales, carry):
                    diff = chan - mu
                    one = r * jnp.exp2(diff * diff * scale)
                    two = one * diff
                    out.append((a + one, b + two, c + two * diff))
                return tuple(out)

            zero = jnp.zeros((8, LANES), jnp.float32)
            done = lax.fori_loop(0, nch // 8, body, ((zero,) * 3,) * 4, unroll=8)
            for four in done:
                for t in range(3):
                    sums[t].append(jnp.sum(four[t], axis=0, keepdims=True))
        amp = flat_ref[0, :, at]
        inv = flat_ref[2, :, at]
        slope = amp * inv * inv
        grads = (
            jnp.concatenate(sums[0], axis=0) * (1.0 / nch),
            jnp.concatenate(sums[1], axis=0) * slope,
            jnp.concatenate(sums[2], axis=0) * (slope * inv * (1.0 / nch)),
        )
        for t in range(3):
            step = STEPS[t] * grads[t]
            for i in range(rows):
                row = part * rows + i
                lane = (row + 2) * PITCH + 2
                base = bases[t][:, lane : lane + TILE]
                fit_ref[t, :, row, :] = base - step[:, i * TILE : (i + 1) * TILE]

    for copy in copies:
        copy.wait()


def gradient_step(place, parts, model, flat, ext):
    vmem = pl.BlockSpec(memory_space=pltpu.VMEM)
    shape = parts[0].shape
    return pl.pallas_call(
        step_kernel,
        out_shape=[
            jax.ShapeDtypeStruct(shape, jnp.float32),
            jax.ShapeDtypeStruct((3, COMPS, TILE, TILE), jnp.float32),
        ],
        in_specs=[pl.BlockSpec(memory_space=pltpu.SMEM)] + [vmem] * 8,
        out_specs=[pl.BlockSpec(memory_space=pl.ANY), vmem],
        scratch_shapes=[
            pltpu.VMEM(shape, jnp.float32),
            pltpu.VMEM(model.shape, jnp.float32),
            pltpu.SemaphoreType.DMA((2,)),
        ],
        compiler_params=pltpu.CompilerParams(vmem_limit_bytes=VMEM_LIMIT),
        cost_estimate=pl.CostEstimate(flops=15_000_000, bytes_accessed=4_000_000, transcendentals=1_100_000),
        name="gradient_step",
    )(place, *[kept(x) for x in (*parts, model, flat, ext)])


def on_device(cube, level_table, level_index, amplitude, centre_index, spread):
    nch = cube.shape[2]
    places = [f(axis) for axis in ("skyy", "skyx") for f in (lax.axis_index, lax.axis_size)]
    place = jnp.stack([jnp.asarray(p, jnp.int32) for p in places])

    for_down, for_up = packed(cube, amplitude, centre_index, spread)
    up1, down1 = sent(for_down, "skyy", 1), sent(for_up, "skyy", -1)
    up2, down2 = sent(cube[BEYOND:], "skyy", 2), sent(cube[:-BEYOND], "skyy", -2)

    entries = jnp.arange(level_table.shape[0], dtype=jnp.int32)
    picks = (level_index[:, :, None] == entries).astype(jnp.float32)
    weight = jnp.sum(picks * level_table, axis=2)
    one = jnp.ones((1, nch), jnp.float32)
    coeff = jnp.concatenate([weight, one]) - jnp.concatenate([0.0 * one, weight])
    scale = jnp.array([16.0 ** (-3 * j) for j in range(LEVELS + 1)], jnp.float32)
    coeff = (coeff * scale[:, None])[:, None, :]
    model, flat, own = model_of(amplitude, centre_index, spread, nch)

    m2, m1, o_0, p1, p2, ext = wavelet_parts(
        place, coeff, (up1, down1, up2, down2, cube), own, nch, places[3] * TILE
    )

    left2, right2 = sent(p2, "skyx", 2), sent(m2, "skyx", -2)
    left1, right1 = sent(p1, "skyx", 1), sent(m1, "skyx", -1)
    return gradient_step(place, (o_0, left2, left1, right1, right2), model, flat, ext)


def solution(mesh):
    placed = (
        P("skyy", "skyx", None),
        P(),
        P(),
        P(None, "skyy", "skyx"),
        P(None, "skyy", "skyx"),
        P(None, "skyy", "skyx"),
    )
    return jax.shard_map(
        on_device,
        mesh=mesh,
        in_specs=placed,
        out_specs=(P("skyy", "skyx", None), P(None, None, "skyy", "skyx")),
        check_vma=False,
    )
```

```python
import functools
import math

import jax
import jax.numpy as jnp
import numpy as np
from jax import lax
from jax.experimental import pallas as pl
from jax.experimental.pallas import tpu as pltpu
from jax.sharding import PartitionSpec as P

TILE = 16
LEVELS = 4
COMPS = 8
LANES = 128
TAPS = (1, 4, 6, 4, 1)
BEYOND = 2
W_ORDER = (0, 1, 2, 4, 3, 5)
VMEM_LIMIT = 20 * 1024 * 1024
ROLES = ((2, 3, 4, 1, 0), (2, 1, 0, 3, 4))
PITCH = 32
EXT = 20 * PITCH
STEPS = (0.5, 0.002, 2.0)
LAMS = (0.2, 0.5, 0.05)


def blur_matrix(length, gap):
    out = np.zeros((length, length), np.float64)
    for tap, factor in enumerate(TAPS):
        offset = (tap - 2) * gap
        for i in range(max(0, -offset), min(length, length - offset)):
            out[i, i + offset] = factor
    return out


def composites(length):
    made, now = [], np.eye(length)
    for level in range(LEVELS):
        now = blur_matrix(length, 2**level) @ now
        made.append(now)
    return made


def halves(matrix):
    bf16 = jnp.bfloat16
    high = np.asarray(matrix, np.float32).astype(bf16)
    low = (np.asarray(matrix, np.float32) - high.astype(np.float32)).astype(bf16)
    return high, low


def channel_matrices(nch):
    parts = [halves(m.T) for m in composites(nch)]
    return np.stack([p[0] for p in parts] + [p[1] for p in parts[2:]])


def scatter_matrices(length):
    whole = composites(length)
    kinds = []
    for start in (0, TILE * (length // TILE // 2), length - TILE):
        parts = []
        for m in whole:
            block = np.zeros((5 * TILE, TILE))
            for k in range(5 * TILE):
                at = start - 2 * TILE + k
                if 0 <= at < length:
                    block[k] = m[at, start : start + TILE]
            parts.append(halves(block))
        high = np.concatenate([p[0] for p in parts], axis=1)
        low = np.concatenate([p[1] for p in parts[2:]], axis=1)
        columns = np.concatenate([high, high, low], axis=1).reshape(5, TILE, -1)
        for order in ROLES:
            kinds.append(np.concatenate([columns[i] for i in order]))
    return np.stack(kinds)


def sent(values, axis, by):
    size = lax.axis_size(axis)
    if by > 0:
        pairs = [(i, i + by) for i in range(size - by)]
    else:
        pairs = [(i, i + by) for i in range(-by, size)]
    return lax.ppermute(values, axis, pairs)


def away(values, axis, by):
    size = lax.axis_size(axis)
    pairs = [(i, i + by if i % 2 else i - by) for i in range(size)]
    return lax.ppermute(values, axis, [(i, j) for i, j in pairs if 0 <= j < size])


def own_row(t, row, amp_ref, index_ref, spread_ref, nch):
    if t == 0:
        return amp_ref[:, row, :]
    if t == 1:
        return (index_ref[:, row, :].astype(jnp.float32) + 0.5) * (1.0 / nch)
    return spread_ref[:, row, :]


def pack_kernel(x_ref, amp_ref, index_ref, spread_ref, up_ref, down_ref):
    nch = x_ref.shape[2]
    for out, first in ((up_ref, TILE - 2), (down_ref, 0)):
        for row in range(TILE):
            out[row] = x_ref[row]
        out[TILE] = jnp.zeros((TILE, nch), jnp.float32)
        for t in range(3):
            for r in range(2):
                lane = (2 * t + r) * TILE
                got = own_row(t, first + r, amp_ref, index_ref, spread_ref, nch)
                out[TILE, 0:COMPS, lane : lane + TILE] = got


def packed(cube, amplitude, centre_index, spread):
    vmem = pl.BlockSpec(memory_space=pltpu.VMEM)
    shape = (TILE + 1,) + cube.shape[1:]
    return pl.pallas_call(
        pack_kernel,
        out_shape=[pltpu.VMEM(shape, jnp.float32)] * 2,
        in_specs=[vmem] * 4,
        out_specs=[vmem] * 2,
        compiler_params=pltpu.CompilerParams(vmem_limit_bytes=VMEM_LIMIT),
        cost_estimate=pl.CostEstimate(flops=1000, bytes_accessed=1_000_000, transcendentals=0),
        name="pack",
    )(*[pltpu.with_memory_space_constraint(v, pltpu.HBM) for v in (cube, amplitude, centre_index, spread)])


def border_columns(ext_ref, shift):
    lane = lax.broadcasted_iota(jnp.int32, (COMPS, EXT), 1) % PITCH
    total = jnp.zeros((COMPS, EXT), jnp.float32)
    for t in range(3):
        moved = pltpu.roll(ext_ref[t], (2 * t - shift) % EXT, 1)
        total = jnp.where((lane >= 2 * t) & (lane < 2 * t + 2), moved, total)
    return total


def put_plane(out, index, lanes):
    nch = out.shape[2]
    out[index] = jnp.zeros((TILE, nch), jnp.float32)
    out[index, 0:COMPS, :] = lanes[:, :nch]
    out[index, COMPS:, 0 : EXT - nch] = lanes[:, nch:]


def from_plane(ref, index):
    nch = ref.shape[2]
    return jnp.concatenate([ref[index, 0:COMPS, :], ref[index, COMPS:, 0 : EXT - nch]], axis=1)


def stencil(p):
    near = pltpu.roll(p, 1, 1) + pltpu.roll(p, EXT - 1, 1)
    return 4.0 * p - (near + (pltpu.roll(p, PITCH, 1) + pltpu.roll(p, EXT - PITCH, 1)))


def smoothed(ext_ref, left, right, place_ref):
    lane = lax.broadcasted_iota(jnp.int32, (COMPS, EXT), 1)
    row, column = lane // PITCH, lane % PITCH
    y = row + (place_ref[0] * TILE - 2)
    x = column + (place_ref[2] * TILE - 2)
    on_sky = (y >= 0) & (y < place_ref[1] * TILE) & (x >= 0) & (x < place_ref[3] * TILE)
    out = []
    for t in range(3):
        p = ext_ref[t]
        p = jnp.where(column < 2, pltpu.roll(left, (EXT - 2 * t) % EXT, 1), p)
        p = jnp.where(column >= TILE + 2, pltpu.roll(right, (TILE + 2 - 2 * t) % EXT, 1), p)
        first = jnp.where(on_sky, stencil(p), 0.0)
        out.append(p - (STEPS[t] * LAMS[t]) * stencil(first))
    return out


def five(v, flag=None):
    total = (v[0] + v[4]) + 4.0 * (v[1] + v[3]) + 6.0 * v[2]
    return total if flag is None else total * flag


def split(v):
    high = v.astype(jnp.bfloat16)
    return high, (v - high.astype(jnp.float32)).astype(jnp.bfloat16)


def wavelet_kernel(
    place_ref, a_ref, m1, p1, m2, p2, x_ref, k_ref, own_ref, w_hbm,
    o_0, swap_ref, near_ref, far_ref, ext_ref, rows_ref, y_ref, w_ref, sems,
):
    nch = x_ref.shape[2]
    tiles = (m2, m1, x_ref, p1, p2)
    near = [place_ref[0] + i for i in (-2, -1, 0, 1, 2)]
    flags = [jnp.where((i >= 0) & (i < place_ref[1]), 1.0, 0.0) for i in near]
    loads = [pltpu.make_async_copy(w_hbm.at[i], w_ref.at[i], sems.at[i]) for i in range(LEVELS + 2)]
    for i in W_ORDER:
        loads[i].start()

    lane_tiles = nch // LANES

    def row_pass(step, carry):
        sub = pl.ds(pl.multiple_of((step // lane_tiles) * 8, 8), 8)
        lane = pl.ds(pl.multiple_of((step % lane_tiles) * LANES, LANES), LANES)

        @functools.cache
        def value(level, at):
            tile = (at + 2 * TILE) // TILE
            if level == 0:
                return tiles[tile][at % TILE - (BEYOND if tile == 0 else 0), sub, lane]
            gap = 2 ** (level - 1)
            taps = [value(level - 1, at + (t - 2) * gap) for t in range(5)]
            return five(taps, None if tile == 2 else flags[tile])

        reach = {1: 28, 2: 24, 3: 16, 4: 0}
        lag = {1: 2, 2: 6, 3: 14, 4: 30}
        for at in range(-30, TILE + 30):
            value(0, at)
            for level in range(1, LEVELS + 1):
                row = at - lag[level]
                if -reach[level] <= row < TILE + reach[level]:
                    got = value(level, row)
                    if 0 <= row < TILE:
                        rows_ref[level - 1, row, sub, lane] = got
        return carry

    lax.fori_loop(0, 2 * lane_tiles, row_pass, 0)

    pixels = TILE * TILE
    dot = functools.partial(jnp.dot, preferred_element_type=jnp.float32)
    for level in range(LEVELS):
        high, low = split(rows_ref[level].reshape(pixels, nch))
        loads[level].wait()
        got = dot(high, w_ref[level]) + dot(low, w_ref[level])
        if level >= 2:
            loads[level + 2].wait()
            got = got + dot(high, w_ref[level + 2])
        high, low = split(got * a_ref[level + 1])
        high = high.reshape(TILE, TILE, nch)
        y_ref[:, level * TILE : (level + 1) * TILE] = high
        at = (level + LEVELS) * TILE
        y_ref[:, at : at + TILE] = low.reshape(TILE, TILE, nch)
        if level >= 2:
            at = (level + 6) * TILE
            y_ref[:, at : at + TILE] = high

    kind = jnp.where(place_ref[2] == 0, 0, jnp.where(place_ref[2] == place_ref[3] - 1, 2, 1))
    odd = place_ref[2] % 2
    columns = k_ref[2 * kind + odd]

    def column_pass(row, carry):
        got = dot(columns, y_ref[row])
        o_0[row] = got[:TILE] + a_ref[0] * x_ref[row]
        swap_ref[row] = got[TILE : 2 * TILE]
        swap_ref[row + TILE] = got[2 * TILE : 3 * TILE]
        near_ref[row] = got[3 * TILE : 4 * TILE]
        far_ref[row] = got[4 * TILE :]
        return carry

    lax.fori_loop(0, TILE, column_pass, 0, unroll=4)

    ext_ref[...] = own_ref[...]
    for t in range(3):
        for r in range(2):
            lane = (2 * t + r) * TILE
            at = r * PITCH + 2
            ext_ref[t, :, at : at + TILE] = m1[TILE, 0:COMPS, lane : lane + TILE]
            at = (TILE + 2 + r) * PITCH + 2
            ext_ref[t, :, at : at + TILE] = p1[TILE, 0:COMPS, lane : lane + TILE]
    to_right = border_columns(ext_ref, TILE)
    to_left = border_columns(ext_ref, 2)
    put_plane(swap_ref, 2 * TILE, jnp.where(odd == 0, to_right, to_left))
    put_plane(near_ref, TILE, jnp.where(odd == 0, to_left, to_right))


def kept(x):
    return pltpu.with_memory_space_constraint(x, pltpu.VMEM)


def wavelet_parts(place, coeff, tiles, own, nch, length):
    w = jnp.asarray(channel_matrices(nch))
    k = jnp.asarray(scatter_matrices(length))
    smem = pl.BlockSpec(memory_space=pltpu.SMEM)
    vmem = pl.BlockSpec(memory_space=pltpu.VMEM)
    plain = pltpu.VMEM(tiles[-1].shape, jnp.float32)
    taller = pltpu.VMEM(tiles[0].shape, jnp.float32)
    pair = pltpu.VMEM((2 * TILE + 1,) + tiles[0].shape[1:], jnp.float32)
    return pl.pallas_call(
        wavelet_kernel,
        out_shape=[plain, pair, taller, plain, pltpu.VMEM(own.shape, jnp.float32)],
        in_specs=[smem] + [vmem] * 8 + [pl.BlockSpec(memory_space=pl.ANY)],
        out_specs=[vmem] * 5,
        scratch_shapes=[
            pltpu.VMEM((LEVELS, TILE, TILE, nch), jnp.float32),
            pltpu.VMEM((TILE, 10 * TILE, nch), jnp.bfloat16),
            pltpu.VMEM(w.shape, jnp.bfloat16),
            pltpu.SemaphoreType.DMA((LEVELS + 2,)),
        ],
        compiler_params=pltpu.CompilerParams(vmem_limit_bytes=VMEM_LIMIT),
        cost_estimate=pl.CostEstimate(flops=4_000_000_000, bytes_accessed=9_000_000, transcendentals=0),
        name="wavelet_parts",
    )(place, *[kept(x) for x in (coeff, *tiles, k, own)], pltpu.with_memory_space_constraint(w, pltpu.HBM))


def add_kernel(near_ref, swapped_ref, _, out_ref):
    def body(row, carry):
        out_ref[row] = near_ref[row] + swapped_ref[row + TILE]
        return carry

    lax.fori_loop(0, TILE, body, 0, unroll=4)
    out_ref[TILE] = near_ref[TILE]


def outward(near, swapped, far):
    vmem = pl.BlockSpec(memory_space=pltpu.VMEM)
    return pl.pallas_call(
        add_kernel,
        out_shape=pltpu.VMEM(near.shape, jnp.float32),
        in_specs=[vmem] * 2 + [pl.BlockSpec(memory_space=pl.ANY)],
        out_specs=vmem,
        compiler_params=pltpu.CompilerParams(vmem_limit_bytes=VMEM_LIMIT),
        cost_estimate=pl.CostEstimate(flops=100_000, bytes_accessed=1_500_000, transcendentals=0),
        name="outward",
    )(kept(near), kept(swapped), kept(far))


def model_kernel(amp_ref, index_ref, spread_ref, model_ref, flat_ref, own_ref, scale_ref):
    nch, pixels = model_ref.shape
    own_ref[...] = jnp.zeros_like(own_ref)
    for t in range(3):
        for row in range(TILE):
            got = own_row(t, row, amp_ref, index_ref, spread_ref, nch)
            at = (row + 2) * PITCH + 2
            own_ref[t, :, at : at + TILE] = got
            flat_ref[t, :, row * TILE : (row + 1) * TILE] = got
    mu = flat_ref[1] * float(nch)
    inv = 1.0 / flat_ref[2]
    flat_ref[1] = mu
    flat_ref[2] = inv
    scale_ref[...] = (-0.5 * math.log2(math.e)) * inv * inv

    def body(step, carry):
        base = pl.multiple_of(step * 8, 8)
        chan = (lax.broadcasted_iota(jnp.int32, (8, pixels), 0) + base).astype(jnp.float32)
        total = jnp.zeros((8, pixels), jnp.float32)
        for k in range(COMPS):
            diff = chan - flat_ref[1, k : k + 1, :]
            bump = jnp.exp2(diff * diff * scale_ref[k : k + 1, :])
            total += flat_ref[0, k : k + 1, :] * bump
        model_ref[pl.ds(base, 8), :] = total
        return carry

    lax.fori_loop(0, nch // 8, body, 0, unroll=2)


def model_of(amplitude, centre_index, spread, nch):
    vmem = pl.BlockSpec(memory_space=pltpu.VMEM)
    pixels = TILE * TILE
    return pl.pallas_call(
        model_kernel,
        out_shape=[
            pltpu.VMEM((nch, pixels), jnp.float32),
            pltpu.VMEM((3, COMPS, pixels), jnp.float32),
            pltpu.VMEM((3, COMPS, EXT), jnp.float32),
        ],
        in_specs=[vmem] * 3,
        out_specs=[vmem] * 3,
        scratch_shapes=[pltpu.VMEM((COMPS, pixels), jnp.float32)],
        compiler_params=pltpu.CompilerParams(vmem_limit_bytes=VMEM_LIMIT),
        cost_estimate=pl.CostEstimate(flops=10_000_000, bytes_accessed=1_000_000, transcendentals=1_100_000),
        name="gaussian_model",
    )(amplitude, centre_index, spread)


def step_kernel(
    place_ref, o_0, swapped_ref, far_ref, near_ref, model_ref, flat_ref, ext_ref,
    den_hbm, fit_ref, den_ref, r_ref, sem,
):
    nch, pixels = model_ref.shape
    rows = LANES // TILE
    parts = pixels // LANES
    copies = []
    even = place_ref[2] % 2 == 0
    inner, outer = from_plane(swapped_ref, 2 * TILE), from_plane(near_ref, TILE)
    left, right = jnp.where(even, outer, inner), jnp.where(even, inner, outer)
    bases = smoothed(ext_ref, left, right, place_ref)
    for part in range(parts):
        at = slice(part * rows, (part + 1) * rows)
        for row in range(part * rows, (part + 1) * rows):
            den_ref[row] = (o_0[row] + swapped_ref[row]) + (far_ref[row] + near_ref[row])
        copies.append(pltpu.make_async_copy(den_ref.at[at], den_hbm.at[at], sem.at[part]))
        copies[-1].start()

    for part in range(parts):
        block = den_ref[part * rows : (part + 1) * rows].reshape(LANES, nch)
        at = slice(part * LANES, (part + 1) * LANES)
        r_ref[:, at] = model_ref[:, at] - block.T

    for part in range(parts):
        at = slice(part * LANES, (part + 1) * LANES)
        sums = [[] for _ in range(3)]
        for first in range(0, COMPS, 4):
            chosen = range(first, first + 4)
            mus = [jnp.broadcast_to(flat_ref[1, k : k + 1, at], (8, LANES)) for k in chosen]
            inv = [jnp.broadcast_to(flat_ref[2, k : k + 1, at], (8, LANES)) for k in chosen]
            scales = [(-0.5 * math.log2(math.e)) * v * v for v in inv]

            def body(step, carry):
                base = pl.multiple_of(step * 8, 8)
                chan = (lax.broadcasted_iota(jnp.int32, (8, LANES), 0) + base).astype(jnp.float32)
                r = r_ref[pl.ds(base, 8), at]
                out = []
                for mu, scale, (a, b, c) in zip(mus, scales, carry):
                    diff = chan - mu
                    one = r * jnp.exp2(diff * diff * scale)
                    two = one * diff
                    out.append((a + one, b + two, c + two * diff))
                return tuple(out)

            zero = jnp.zeros((8, LANES), jnp.float32)
            done = lax.fori_loop(0, nch // 8, body, ((zero,) * 3,) * 4, unroll=8)
            for four in done:
                for t in range(3):
                    sums[t].append(jnp.sum(four[t], axis=0, keepdims=True))
        amp = flat_ref[0, :, at]
        inv = flat_ref[2, :, at]
        slope = amp * inv * inv
        grads = (
            jnp.concatenate(sums[0], axis=0) * (1.0 / nch),
            jnp.concatenate(sums[1], axis=0) * slope,
            jnp.concatenate(sums[2], axis=0) * (slope * inv * (1.0 / nch)),
        )
        for t in range(3):
            step = STEPS[t] * grads[t]
            for i in range(rows):
                row = part * rows + i
                lane = (row + 2) * PITCH + 2
                base = bases[t][:, lane : lane + TILE]
                fit_ref[t, :, row, :] = base - step[:, i * TILE : (i + 1) * TILE]

    for copy in copies:
        copy.wait()


def gradient_step(place, parts, model, flat, ext):
    vmem = pl.BlockSpec(memory_space=pltpu.VMEM)
    shape = parts[0].shape
    return pl.pallas_call(
        step_kernel,
        out_shape=[
            jax.ShapeDtypeStruct(shape, jnp.float32),
            jax.ShapeDtypeStruct((3, COMPS, TILE, TILE), jnp.float32),
        ],
        in_specs=[pl.BlockSpec(memory_space=pltpu.SMEM)] + [vmem] * 7,
        out_specs=[pl.BlockSpec(memory_space=pl.ANY), vmem],
        scratch_shapes=[
            pltpu.VMEM(shape, jnp.float32),
            pltpu.VMEM(model.shape, jnp.float32),
            pltpu.SemaphoreType.DMA((2,)),
        ],
        compiler_params=pltpu.CompilerParams(vmem_limit_bytes=VMEM_LIMIT),
        cost_estimate=pl.CostEstimate(flops=15_000_000, bytes_accessed=4_000_000, transcendentals=1_100_000),
        name="gradient_step",
    )(place, *[kept(x) for x in (*parts, model, flat, ext)])


def on_device(cube, level_table, level_index, amplitude, centre_index, spread):
    nch = cube.shape[2]
    places = [f(axis) for axis in ("skyy", "skyx") for f in (lax.axis_index, lax.axis_size)]
    place = jnp.stack([jnp.asarray(p, jnp.int32) for p in places])

    for_down, for_up = packed(cube, amplitude, centre_index, spread)
    up1, down1 = sent(for_down, "skyy", 1), sent(for_up, "skyy", -1)
    up2, down2 = sent(cube[BEYOND:], "skyy", 2), sent(cube[:-BEYOND], "skyy", -2)

    entries = jnp.arange(level_table.shape[0], dtype=jnp.int32)
    picks = (level_index[:, :, None] == entries).astype(jnp.float32)
    weight = jnp.sum(picks * level_table, axis=2)
    one = jnp.ones((1, nch), jnp.float32)
    coeff = jnp.concatenate([weight, one]) - jnp.concatenate([0.0 * one, weight])
    scale = jnp.array([16.0 ** (-3 * j) for j in range(LEVELS + 1)], jnp.float32)
    coeff = (coeff * scale[:, None])[:, None, :]
    model, flat, own = model_of(amplitude, centre_index, spread, nch)

    o_0, swap, near, far, ext = wavelet_parts(
        place, coeff, (up1, down1, up2, down2, cube), own, nch, places[3] * TILE
    )

    swapped = lax.ppermute(swap, "skyx", [(i, i ^ 1) for i in range(places[3])])
    far = away(far, "skyx", 2)
    near = away(outward(near, swapped, far), "skyx", 1)
    return gradient_step(place, (o_0, swapped, far, near), model, flat, ext)


def solution(mesh):
    placed = (
        P("skyy", "skyx", None),
        P(),
        P(),
        P(None, "skyy", "skyx"),
        P(None, "skyy", "skyx"),
        P(None, "skyy", "skyx"),
    )
    return jax.shard_map(
        on_device,
        mesh=mesh,
        in_specs=placed,
        out_specs=(P("skyy", "skyx", None), P(None, None, "skyy", "skyx")),
        check_vma=False,
    )
```

```python
import functools
import math

import jax
import jax.numpy as jnp
import numpy as np
from jax import lax
from jax.experimental import pallas as pl
from jax.experimental.pallas import tpu as pltpu
from jax.sharding import PartitionSpec as P

TILE = 16
LEVELS = 4
COMPS = 8
LANES = 128
TAPS = (1, 4, 6, 4, 1)
BEYOND = 2
VMEM_LIMIT = 20 * 1024 * 1024
ROLES = ((2, 3, 4, 1, 0), (2, 1, 0, 3, 4))
PITCH = 32
EXT = 20 * PITCH
STEPS = (0.5, 0.002, 2.0)
LAMS = (0.2, 0.5, 0.05)


def blur_matrix(length, gap):
    out = np.zeros((length, length), np.float64)
    for tap, factor in enumerate(TAPS):
        offset = (tap - 2) * gap
        for i in range(max(0, -offset), min(length, length - offset)):
            out[i, i + offset] = factor
    return out


def composites(length):
    made, now = [], np.eye(length)
    for level in range(LEVELS):
        now = blur_matrix(length, 2**level) @ now
        made.append(now)
    return made


def halves(matrix):
    bf16 = jnp.bfloat16
    high = np.asarray(matrix, np.float32).astype(bf16)
    low = (np.asarray(matrix, np.float32) - high.astype(np.float32)).astype(bf16)
    return high, low


def channel_matrices(nch):
    parts = [halves(m.T) for m in composites(nch)]
    return np.stack([p[0] for p in parts] + [p[1] for p in parts[2:]])


def scatter_matrices(length):
    whole = composites(length)
    kinds = []
    for start in (0, TILE * (length // TILE // 2), length - TILE):
        parts = []
        for m in whole:
            block = np.zeros((5 * TILE, TILE))
            for k in range(5 * TILE):
                at = start - 2 * TILE + k
                if 0 <= at < length:
                    block[k] = m[at, start : start + TILE]
            parts.append(halves(block))
        high = np.concatenate([p[0] for p in parts], axis=1)
        low = np.concatenate([p[1] for p in parts[2:]], axis=1)
        columns = np.concatenate([high, high, low], axis=1).reshape(5, TILE, -1)
        for order in ROLES:
            kinds.append(np.concatenate([columns[i] for i in order]))
    return np.stack(kinds)


def sent(values, axis, by):
    size = lax.axis_size(axis)
    if by > 0:
        pairs = [(i, i + by) for i in range(size - by)]
    else:
        pairs = [(i, i + by) for i in range(-by, size)]
    return lax.ppermute(values, axis, pairs)


def away(values, axis, by):
    size = lax.axis_size(axis)
    pairs = [(i, i + by if i % 2 else i - by) for i in range(size)]
    return lax.ppermute(values, axis, [(i, j) for i, j in pairs if 0 <= j < size])


def own_row(t, row, amp_ref, index_ref, spread_ref, nch):
    if t == 0:
        return amp_ref[:, row, :]
    if t == 1:
        return (index_ref[:, row, :].astype(jnp.float32) + 0.5) * (1.0 / nch)
    return spread_ref[:, row, :]


def pack_kernel(x_ref, amp_ref, index_ref, spread_ref, up_ref, down_ref):
    nch = x_ref.shape[2]
    for out, first in ((up_ref, TILE - 2), (down_ref, 0)):
        for row in range(TILE):
            out[row] = x_ref[row]
        out[TILE] = jnp.zeros((TILE, nch), jnp.float32)
        for t in range(3):
            for r in range(2):
                lane = (2 * t + r) * TILE
                got = own_row(t, first + r, amp_ref, index_ref, spread_ref, nch)
                out[TILE, 0:COMPS, lane : lane + TILE] = got


def packed(cube, amplitude, centre_index, spread):
    vmem = pl.BlockSpec(memory_space=pltpu.VMEM)
    shape = (TILE + 1,) + cube.shape[1:]
    return pl.pallas_call(
        pack_kernel,
        out_shape=[pltpu.VMEM(shape, jnp.float32)] * 2,
        in_specs=[vmem] * 4,
        out_specs=[vmem] * 2,
        compiler_params=pltpu.CompilerParams(vmem_limit_bytes=VMEM_LIMIT),
        cost_estimate=pl.CostEstimate(flops=1000, bytes_accessed=1_000_000, transcendentals=0),
        name="pack",
    )(*[pltpu.with_memory_space_constraint(v, pltpu.HBM) for v in (cube, amplitude, centre_index, spread)])


def border_columns(ext_ref, shift):
    lane = lax.broadcasted_iota(jnp.int32, (COMPS, EXT), 1) % PITCH
    total = jnp.zeros((COMPS, EXT), jnp.float32)
    for t in range(3):
        moved = pltpu.roll(ext_ref[t], (2 * t - shift) % EXT, 1)
        total = jnp.where((lane >= 2 * t) & (lane < 2 * t + 2), moved, total)
    return total


def put_plane(out, index, lanes):
    nch = out.shape[2]
    out[index] = jnp.zeros((TILE, nch), jnp.float32)
    out[index, 0:COMPS, :] = lanes[:, :nch]
    out[index, COMPS:, 0 : EXT - nch] = lanes[:, nch:]


def from_plane(ref, index):
    nch = ref.shape[2]
    return jnp.concatenate([ref[index, 0:COMPS, :], ref[index, COMPS:, 0 : EXT - nch]], axis=1)


def stencil(p):
    near = pltpu.roll(p, 1, 1) + pltpu.roll(p, EXT - 1, 1)
    return 4.0 * p - (near + (pltpu.roll(p, PITCH, 1) + pltpu.roll(p, EXT - PITCH, 1)))


def smoothed(ext_ref, left, right, place_ref):
    lane = lax.broadcasted_iota(jnp.int32, (COMPS, EXT), 1)
    row, column = lane // PITCH, lane % PITCH
    y = row + (place_ref[0] * TILE - 2)
    x = column + (place_ref[2] * TILE - 2)
    on_sky = (y >= 0) & (y < place_ref[1] * TILE) & (x >= 0) & (x < place_ref[3] * TILE)
    out = []
    for t in range(3):
        p = ext_ref[t]
        p = jnp.where(column < 2, pltpu.roll(left, (EXT - 2 * t) % EXT, 1), p)
        p = jnp.where(column >= TILE + 2, pltpu.roll(right, (TILE + 2 - 2 * t) % EXT, 1), p)
        first = jnp.where(on_sky, stencil(p), 0.0)
        out.append(p - (STEPS[t] * LAMS[t]) * stencil(first))
    return out


def five(v, flag=None):
    total = (v[0] + v[4]) + 4.0 * (v[1] + v[3]) + 6.0 * v[2]
    return total if flag is None else total * flag


def split(v):
    high = v.astype(jnp.bfloat16)
    return high, (v - high.astype(jnp.float32)).astype(jnp.bfloat16)


def wavelet_kernel(
    place_ref, a_ref, m1, p1, m2, p2, x_ref, k_ref, own_ref, w_ref,
    o_0, swap_ref, near_ref, far_ref, ext_ref, rows_ref, y_ref,
):
    nch = x_ref.shape[2]
    tiles = (m2, m1, x_ref, p1, p2)
    near = [place_ref[0] + i for i in (-2, -1, 0, 1, 2)]
    flags = [jnp.where((i >= 0) & (i < place_ref[1]), 1.0, 0.0) for i in near]

    lane_tiles = nch // LANES

    def row_pass(step, carry):
        sub = pl.ds(pl.multiple_of((step // lane_tiles) * 8, 8), 8)
        lane = pl.ds(pl.multiple_of((step % lane_tiles) * LANES, LANES), LANES)

        @functools.cache
        def value(level, at):
            tile = (at + 2 * TILE) // TILE
            if level == 0:
                return tiles[tile][at % TILE - (BEYOND if tile == 0 else 0), sub, lane]
            gap = 2 ** (level - 1)
            taps = [value(level - 1, at + (t - 2) * gap) for t in range(5)]
            return five(taps, None if tile == 2 else flags[tile])

        reach = {1: 28, 2: 24, 3: 16, 4: 0}
        lag = {1: 2, 2: 6, 3: 14, 4: 30}
        for at in range(-30, TILE + 30):
            value(0, at)
            for level in range(1, LEVELS + 1):
                row = at - lag[level]
                if -reach[level] <= row < TILE + reach[level]:
                    got = value(level, row)
                    if 0 <= row < TILE:
                        rows_ref[level - 1, row, sub, lane] = got
        return carry

    lax.fori_loop(0, 2 * lane_tiles, row_pass, 0)

    pixels = TILE * TILE
    dot = functools.partial(jnp.dot, preferred_element_type=jnp.float32)
    for level in range(LEVELS):
        high, low = split(rows_ref[level].reshape(pixels, nch))
        got = dot(high, w_ref[level]) + dot(low, w_ref[level])
        if level >= 2:
            got = got + dot(high, w_ref[level + 2])
        high, low = split(got * a_ref[level + 1])
        high = high.reshape(TILE, TILE, nch)
        y_ref[:, level * TILE : (level + 1) * TILE] = high
        at = (level + LEVELS) * TILE
        y_ref[:, at : at + TILE] = low.reshape(TILE, TILE, nch)
        if level >= 2:
            at = (level + 6) * TILE
            y_ref[:, at : at + TILE] = high

    kind = jnp.where(place_ref[2] == 0, 0, jnp.where(place_ref[2] == place_ref[3] - 1, 2, 1))
    odd = place_ref[2] % 2
    columns = k_ref[2 * kind + odd]

    def column_pass(row, carry):
        got = dot(columns, y_ref[row])
        o_0[row] = got[:TILE] + a_ref[0] * x_ref[row]
        swap_ref[row] = got[TILE : 2 * TILE]
        swap_ref[row + TILE] = got[2 * TILE : 3 * TILE]
        near_ref[row] = got[3 * TILE : 4 * TILE]
        far_ref[row] = got[4 * TILE :]
        return carry

    lax.fori_loop(0, TILE, column_pass, 0, unroll=4)

    ext_ref[...] = own_ref[...]
    for t in range(3):
        for r in range(2):
            lane = (2 * t + r) * TILE
            at = r * PITCH + 2
            ext_ref[t, :, at : at + TILE] = m1[TILE, 0:COMPS, lane : lane + TILE]
            at = (TILE + 2 + r) * PITCH + 2
            ext_ref[t, :, at : at + TILE] = p1[TILE, 0:COMPS, lane : lane + TILE]
    to_right = border_columns(ext_ref, TILE)
    to_left = border_columns(ext_ref, 2)
    put_plane(swap_ref, 2 * TILE, jnp.where(odd == 0, to_right, to_left))
    put_plane(near_ref, TILE, jnp.where(odd == 0, to_left, to_right))


def kept(x):
    return pltpu.with_memory_space_constraint(x, pltpu.VMEM)


def wavelet_parts(place, coeff, tiles, own, w, nch, length):
    k = jnp.asarray(scatter_matrices(length))
    smem = pl.BlockSpec(memory_space=pltpu.SMEM)
    vmem = pl.BlockSpec(memory_space=pltpu.VMEM)
    plain = pltpu.VMEM(tiles[-1].shape, jnp.float32)
    taller = pltpu.VMEM(tiles[0].shape, jnp.float32)
    padded = pltpu.VMEM((TILE + 1,) + tiles[0].shape[1:], jnp.float32)
    pair = pltpu.VMEM((2 * TILE + 1,) + tiles[0].shape[1:], jnp.float32)
    return pl.pallas_call(
        wavelet_kernel,
        out_shape=[plain, pair, taller, padded, pltpu.VMEM(own.shape, jnp.float32)],
        in_specs=[smem] + [vmem] * 9,
        out_specs=[vmem] * 5,
        scratch_shapes=[
            pltpu.VMEM((LEVELS, TILE, TILE, nch), jnp.float32),
            pltpu.VMEM((TILE, 10 * TILE, nch), jnp.bfloat16),
        ],
        compiler_params=pltpu.CompilerParams(vmem_limit_bytes=VMEM_LIMIT),
        cost_estimate=pl.CostEstimate(flops=4_000_000_000, bytes_accessed=9_000_000, transcendentals=0),
        name="wavelet_parts",
    )(place, *[kept(x) for x in (coeff, *tiles, k, own, w)])


def add_kernel(near_ref, swapped_ref, out_ref):
    def body(row, carry):
        out_ref[row] = near_ref[row] + swapped_ref[row + TILE]
        return carry

    lax.fori_loop(0, TILE, body, 0, unroll=4)
    out_ref[TILE] = near_ref[TILE]


def outward(near, swapped):
    vmem = pl.BlockSpec(memory_space=pltpu.VMEM)
    return pl.pallas_call(
        add_kernel,
        out_shape=pltpu.VMEM(near.shape, jnp.float32),
        in_specs=[vmem] * 2,
        out_specs=vmem,
        compiler_params=pltpu.CompilerParams(vmem_limit_bytes=VMEM_LIMIT),
        cost_estimate=pl.CostEstimate(flops=100_000, bytes_accessed=1_500_000, transcendentals=0),
        name="outward",
    )(kept(near), kept(swapped))


def model_kernel(amp_ref, index_ref, spread_ref, w_hbm, model_ref, flat_ref, own_ref, w_ref, scale_ref, sem):
    load = pltpu.make_async_copy(w_hbm, w_ref, sem)
    load.start()
    nch, pixels = model_ref.shape
    own_ref[...] = jnp.zeros_like(own_ref)
    for t in range(3):
        for row in range(TILE):
            got = own_row(t, row, amp_ref, index_ref, spread_ref, nch)
            at = (row + 2) * PITCH + 2
            own_ref[t, :, at : at + TILE] = got
            flat_ref[t, :, row * TILE : (row + 1) * TILE] = got
    mu = flat_ref[1] * float(nch)
    inv = 1.0 / flat_ref[2]
    flat_ref[1] = mu
    flat_ref[2] = inv
    scale_ref[...] = (-0.5 * math.log2(math.e)) * inv * inv

    def body(step, carry):
        base = pl.multiple_of(step * 8, 8)
        chan = (lax.broadcasted_iota(jnp.int32, (8, pixels), 0) + base).astype(jnp.float32)
        total = jnp.zeros((8, pixels), jnp.float32)
        for k in range(COMPS):
            diff = chan - flat_ref[1, k : k + 1, :]
            bump = jnp.exp2(diff * diff * scale_ref[k : k + 1, :])
            total += flat_ref[0, k : k + 1, :] * bump
        model_ref[pl.ds(base, 8), :] = total
        return carry

    lax.fori_loop(0, nch // 8, body, 0, unroll=2)
    load.wait()


def model_of(amplitude, centre_index, spread, nch):
    w = jnp.asarray(channel_matrices(nch))
    vmem = pl.BlockSpec(memory_space=pltpu.VMEM)
    pixels = TILE * TILE
    return pl.pallas_call(
        model_kernel,
        out_shape=[
            pltpu.VMEM((nch, pixels), jnp.float32),
            pltpu.VMEM((3, COMPS, pixels), jnp.float32),
            pltpu.VMEM((3, COMPS, EXT), jnp.float32),
            pltpu.VMEM(w.shape, w.dtype),
        ],
        in_specs=[vmem] * 3 + [pl.BlockSpec(memory_space=pl.ANY)],
        out_specs=[vmem] * 4,
        scratch_shapes=[pltpu.VMEM((COMPS, pixels), jnp.float32), pltpu.SemaphoreType.DMA],
        compiler_params=pltpu.CompilerParams(vmem_limit_bytes=VMEM_LIMIT),
        cost_estimate=pl.CostEstimate(flops=10_000_000, bytes_accessed=1_000_000, transcendentals=1_100_000),
        name="gaussian_model",
    )(amplitude, centre_index, spread, pltpu.with_memory_space_constraint(w, pltpu.HBM))


def step_kernel(
    place_ref, o_0, swapped_ref, far_ref, near_ref, model_ref, flat_ref, ext_ref,
    den_hbm, fit_ref, den_ref, r_ref, sem,
):
    nch, pixels = model_ref.shape
    rows = LANES // TILE
    parts = pixels // LANES
    copies = []
    even = place_ref[2] % 2 == 0
    inner, outer = from_plane(swapped_ref, 2 * TILE), from_plane(near_ref, TILE)
    left, right = jnp.where(even, outer, inner), jnp.where(even, inner, outer)
    bases = smoothed(ext_ref, left, right, place_ref)
    for part in range(parts):
        at = slice(part * rows, (part + 1) * rows)
        for row in range(part * rows, (part + 1) * rows):
            den_ref[row] = (o_0[row] + swapped_ref[row]) + (far_ref[row] + near_ref[row])
        copies.append(pltpu.make_async_copy(den_ref.at[at], den_hbm.at[at], sem.at[part]))
        copies[-1].start()

    shape = (COMPS, rows, LANES)
    own_lanes = lax.broadcasted_iota(jnp.int32, shape, 2) // TILE == lax.broadcasted_iota(jnp.int32, shape, 1)
    for part in range(parts):
        block = den_ref[part * rows : (part + 1) * rows].reshape(LANES, nch)
        at = slice(part * LANES, (part + 1) * LANES)
        r_ref[:, at] = model_ref[:, at] - block.T

    for part in range(parts):
        at = slice(part * LANES, (part + 1) * LANES)
        sums = [[] for _ in range(3)]
        for first in range(0, COMPS, 4):
            chosen = range(first, first + 4)
            mus = [jnp.broadcast_to(flat_ref[1, k : k + 1, at], (8, LANES)) for k in chosen]
            inv = [jnp.broadcast_to(flat_ref[2, k : k + 1, at], (8, LANES)) for k in chosen]
            scales = [(-0.5 * math.log2(math.e)) * v * v for v in inv]

            def body(step, carry):
                base = pl.multiple_of(step * 8, 8)
                chan = (lax.broadcasted_iota(jnp.int32, (8, LANES), 0) + base).astype(jnp.float32)
                r = r_ref[pl.ds(base, 8), at]
                out = []
                for mu, scale, (a, b, c) in zip(mus, scales, carry):
                    diff = chan - mu
                    one = r * jnp.exp2(diff * diff * scale)
                    two = one * diff
                    out.append((a + one, b + two, c + two * diff))
                return tuple(out)

            zero = jnp.zeros((8, LANES), jnp.float32)
            done = lax.fori_loop(0, nch // 8, body, ((zero,) * 3,) * 4, unroll=8)
            for four in done:
                for t in range(3):
                    sums[t].append(jnp.sum(four[t], axis=0, keepdims=True))
        amp = flat_ref[0, :, at]
        inv = flat_ref[2, :, at]
        slope = amp * inv * inv
        grads = (
            jnp.concatenate(sums[0], axis=0) * (1.0 / nch),
            jnp.concatenate(sums[1], axis=0) * slope,
            jnp.concatenate(sums[2], axis=0) * (slope * inv * (1.0 / nch)),
        )
        for t in range(3):
            lanes = [(part * rows + i + 2) * PITCH + 2 for i in range(rows)]
            base = jnp.concatenate([bases[t][:, lane : lane + TILE] for lane in lanes], axis=1)
            new = base - STEPS[t] * grads[t]
            spread_out = jnp.where(own_lanes, jnp.broadcast_to(new[:, None, :], own_lanes.shape), 0.0)
            for shift in (LANES // 2, LANES // 4, LANES // 8):
                spread_out = spread_out + pltpu.roll(spread_out, shift, 2)
            fit_ref[t, :, part * rows : (part + 1) * rows, :] = spread_out[:, :, :TILE]

    for copy in copies:
        copy.wait()


def gradient_step(place, parts, model, flat, ext):
    vmem = pl.BlockSpec(memory_space=pltpu.VMEM)
    shape = parts[0].shape
    return pl.pallas_call(
        step_kernel,
        out_shape=[
            jax.ShapeDtypeStruct(shape, jnp.float32),
            jax.ShapeDtypeStruct((3, COMPS, TILE, TILE), jnp.float32),
        ],
        in_specs=[pl.BlockSpec(memory_space=pltpu.SMEM)] + [vmem] * 7,
        out_specs=[pl.BlockSpec(memory_space=pl.ANY), vmem],
        scratch_shapes=[
            pltpu.VMEM(shape, jnp.float32),
            pltpu.VMEM(model.shape, jnp.float32),
            pltpu.SemaphoreType.DMA((2,)),
        ],
        compiler_params=pltpu.CompilerParams(vmem_limit_bytes=VMEM_LIMIT),
        cost_estimate=pl.CostEstimate(flops=15_000_000, bytes_accessed=4_000_000, transcendentals=1_100_000),
        name="gradient_step",
    )(place, *[kept(x) for x in (*parts, model, flat, ext)])


def on_device(cube, level_table, level_index, amplitude, centre_index, spread):
    nch = cube.shape[2]
    places = [f(axis) for axis in ("skyy", "skyx") for f in (lax.axis_index, lax.axis_size)]
    place = jnp.stack([jnp.asarray(p, jnp.int32) for p in places])

    for_down, for_up = packed(cube, amplitude, centre_index, spread)
    up1, down1 = sent(for_down, "skyy", 1), sent(for_up, "skyy", -1)
    up2, down2 = sent(cube[BEYOND:], "skyy", 2), sent(cube[:-BEYOND], "skyy", -2)

    entries = jnp.arange(level_table.shape[0], dtype=jnp.int32)
    picks = (level_index[:, :, None] == entries).astype(jnp.float32)
    weight = jnp.sum(picks * level_table, axis=2)
    one = jnp.ones((1, nch), jnp.float32)
    coeff = jnp.concatenate([weight, one]) - jnp.concatenate([0.0 * one, weight])
    scale = jnp.array([16.0 ** (-3 * j) for j in range(LEVELS + 1)], jnp.float32)
    coeff = (coeff * scale[:, None])[:, None, :]
    model, flat, own, w = model_of(amplitude, centre_index, spread, nch)

    o_0, swap, near, far, ext = wavelet_parts(
        place, coeff, (up1, down1, up2, down2, cube), own, w, nch, places[3] * TILE
    )

    swapped = lax.ppermute(swap, "skyx", [(i, i ^ 1) for i in range(places[3])])
    far = away(far, "skyx", 2)
    near = away(outward(near, swapped), "skyx", 1)
    return gradient_step(place, (o_0, swapped, far, near), model, flat, ext)


def solution(mesh):
    placed = (
        P("skyy", "skyx", None),
        P(),
        P(),
        P(None, "skyy", "skyx"),
        P(None, "skyy", "skyx"),
        P(None, "skyy", "skyx"),
    )
    return jax.shard_map(
        on_device,
        mesh=mesh,
        in_specs=placed,
        out_specs=(P("skyy", "skyx", None), P(None, None, "skyy", "skyx")),
        check_vma=False,
    )
```

```python
import functools
import math

import jax
import jax.numpy as jnp
import numpy as np
from jax import lax
from jax.experimental import pallas as pl
from jax.experimental.pallas import tpu as pltpu
from jax.sharding import PartitionSpec as P

TILE = 16
LEVELS = 4
COMPS = 8
LANES = 128
TAPS = (1, 4, 6, 4, 1)
BEYOND = 2
VMEM_LIMIT = 20 * 1024 * 1024
ROLES = ((2, 3, 4, 1, 0), (2, 1, 0, 3, 4))
PITCH = 24
EXT = 512
STEPS = (0.5, 0.002, 2.0)
LAMS = (0.2, 0.5, 0.05)


def blur_matrix(length, gap):
    out = np.zeros((length, length), np.float64)
    for tap, factor in enumerate(TAPS):
        offset = (tap - 2) * gap
        for i in range(max(0, -offset), min(length, length - offset)):
            out[i, i + offset] = factor
    return out


def composites(length):
    made, now = [], np.eye(length)
    for level in range(LEVELS):
        now = blur_matrix(length, 2**level) @ now
        made.append(now)
    return made


def halves(matrix):
    bf16 = jnp.bfloat16
    high = np.asarray(matrix, np.float32).astype(bf16)
    low = (np.asarray(matrix, np.float32) - high.astype(np.float32)).astype(bf16)
    return high, low


def channel_matrices(nch):
    parts = [halves(m.T) for m in composites(nch)]
    return np.stack([p[0] for p in parts] + [p[1] for p in parts[2:]])


def scatter_matrices(length):
    whole = composites(length)
    kinds = []
    for start in (0, TILE * (length // TILE // 2), length - TILE):
        parts = []
        for m in whole:
            block = np.zeros((5 * TILE, TILE))
            for k in range(5 * TILE):
                at = start - 2 * TILE + k
                if 0 <= at < length:
                    block[k] = m[at, start : start + TILE]
            parts.append(halves(block))
        high = np.concatenate([p[0] for p in parts], axis=1)
        low = np.concatenate([p[1] for p in parts[2:]], axis=1)
        columns = np.concatenate([high, high, low], axis=1).reshape(5, TILE, -1)
        for order in ROLES:
            kinds.append(np.concatenate([columns[i] for i in order]))
    return np.stack(kinds)


def sent(values, axis, by):
    size = lax.axis_size(axis)
    if by > 0:
        pairs = [(i, i + by) for i in range(size - by)]
    else:
        pairs = [(i, i + by) for i in range(-by, size)]
    return lax.ppermute(values, axis, pairs)


def away(values, axis, by):
    size = lax.axis_size(axis)
    pairs = [(i, i + by if i % 2 else i - by) for i in range(size)]
    return lax.ppermute(values, axis, [(i, j) for i, j in pairs if 0 <= j < size])


def own_row(t, row, amp_ref, index_ref, spread_ref, nch):
    if t == 0:
        return amp_ref[:, row, :]
    if t == 1:
        return (index_ref[:, row, :].astype(jnp.float32) + 0.5) * (1.0 / nch)
    return spread_ref[:, row, :]


def border_columns(ext_ref, shift):
    lane = lax.broadcasted_iota(jnp.int32, (COMPS, EXT), 1) % PITCH
    total = jnp.zeros((COMPS, EXT), jnp.float32)
    for t in range(3):
        moved = pltpu.roll(ext_ref[t], (2 * t - shift) % EXT, 1)
        total = jnp.where((lane >= 2 * t) & (lane < 2 * t + 2), moved, total)
    return total


def border_rows(rows, first):
    lane = lax.broadcasted_iota(jnp.int32, (COMPS, EXT), 1)
    total = jnp.zeros((COMPS, EXT), jnp.float32)
    for t in range(3):
        moved = pltpu.roll(rows[t], ((2 * t - first) * PITCH) % EXT, 1)
        total = jnp.where((lane >= 2 * t * PITCH) & (lane < (2 * t + 2) * PITCH), moved, total)
    return total


def with_columns(own, left, right):
    column = lax.broadcasted_iota(jnp.int32, (COMPS, EXT), 1) % PITCH
    out = []
    for t in range(3):
        p = jnp.where(column < 2, pltpu.roll(left, (EXT - 2 * t) % EXT, 1), own[t])
        out.append(jnp.where(column >= TILE + 2, pltpu.roll(right, (TILE + 2 - 2 * t) % EXT, 1), p))
    return out


def with_rows(own, above, below):
    row = lax.broadcasted_iota(jnp.int32, (COMPS, EXT), 1) // PITCH
    out = []
    for t in range(3):
        p = jnp.where(row < 2, pltpu.roll(above, (EXT - 2 * t * PITCH) % EXT, 1), own[t])
        out.append(jnp.where(row >= TILE + 2, pltpu.roll(below, ((TILE + 2 - 2 * t) * PITCH) % EXT, 1), p))
    return out


def stencil(p):
    near = pltpu.roll(p, 1, 1) + pltpu.roll(p, EXT - 1, 1)
    return 4.0 * p - (near + (pltpu.roll(p, PITCH, 1) + pltpu.roll(p, EXT - PITCH, 1)))


def smoothed(params):
    lane = lax.broadcasted_iota(jnp.int32, (COMPS, EXT), 1)
    y = lane // PITCH + (lax.axis_index("skyy") * TILE - 2)
    x = lane % PITCH + (lax.axis_index("skyx") * TILE - 2)
    ny, nx = lax.axis_size("skyy") * TILE, lax.axis_size("skyx") * TILE
    on_sky = (y >= 0) & (y < ny) & (x >= 0) & (x < nx)
    out = []
    for t, p in enumerate(params):
        first = jnp.where(on_sky, stencil(p), 0.0)
        out.append(p - (STEPS[t] * LAMS[t]) * stencil(first))
    return out


def base_kernel(ext_ref, above_ref, below_ref, base_ref):
    params = smoothed(with_rows(ext_ref, above_ref[...], below_ref[...]))
    for t in range(3):
        for row in range(TILE):
            lane = (row + 2) * PITCH + 2
            base_ref[t, :, row * TILE : (row + 1) * TILE] = params[t][:, lane : lane + TILE]


def base_of(ext, above, below):
    vmem = pl.BlockSpec(memory_space=pltpu.VMEM)
    return pl.pallas_call(
        base_kernel,
        out_shape=pltpu.VMEM((3, COMPS, TILE * TILE), jnp.float32),
        in_specs=[vmem] * 3,
        out_specs=vmem,
        compiler_params=pltpu.CompilerParams(vmem_limit_bytes=VMEM_LIMIT),
        cost_estimate=pl.CostEstimate(flops=200_000, bytes_accessed=100_000, transcendentals=0),
        name="smoothed_base",
    )(*[kept(x) for x in (ext, above, below)])


def five(v, flag=None):
    total = (v[0] + v[4]) + 4.0 * (v[1] + v[3]) + 6.0 * v[2]
    return total if flag is None else total * flag


def split(v):
    high = v.astype(jnp.bfloat16)
    return high, (v - high.astype(jnp.float32)).astype(jnp.bfloat16)


def wavelet_kernel(
    a_ref, m1, p1, m2, p2, x_ref, k_ref, own_ref, inner_ref, outer_ref, w_ref,
    o_0, swap_ref, near_ref, far_ref, ext_ref, up_ref, down_ref, rows_ref, y_ref,
):
    nch = x_ref.shape[2]
    tiles = (m2, m1, x_ref, p1, p2)
    iy, ix = lax.axis_index("skyy"), lax.axis_index("skyx")
    near = [iy + i for i in (-2, -1, 0, 1, 2)]
    flags = [jnp.where((i >= 0) & (i < lax.axis_size("skyy")), 1.0, 0.0) for i in near]

    lane_tiles = nch // LANES

    def row_pass(step, carry):
        sub = pl.ds(pl.multiple_of((step // lane_tiles) * 8, 8), 8)
        lane = pl.ds(pl.multiple_of((step % lane_tiles) * LANES, LANES), LANES)

        @functools.cache
        def value(level, at):
            tile = (at + 2 * TILE) // TILE
            if level == 0:
                return tiles[tile][at % TILE - (BEYOND if tile == 0 else 0), sub, lane]
            gap = 2 ** (level - 1)
            taps = [value(level - 1, at + (t - 2) * gap) for t in range(5)]
            return five(taps, None if tile == 2 else flags[tile])

        reach = {1: 28, 2: 24, 3: 16, 4: 0}
        lag = {1: 2, 2: 6, 3: 14, 4: 30}
        for at in range(-30, TILE + 30):
            value(0, at)
            for level in range(1, LEVELS + 1):
                row = at - lag[level]
                if -reach[level] <= row < TILE + reach[level]:
                    got = value(level, row)
                    if 0 <= row < TILE:
                        rows_ref[level - 1, row, sub, lane] = got
        return carry

    lax.fori_loop(0, 2 * lane_tiles, row_pass, 0)

    pixels = TILE * TILE
    dot = functools.partial(jnp.dot, preferred_element_type=jnp.float32)
    for level in range(LEVELS):
        high, low = split(rows_ref[level].reshape(pixels, nch))
        got = dot(high, w_ref[level]) + dot(low, w_ref[level])
        if level >= 2:
            got = got + dot(high, w_ref[level + 2])
        high, low = split(got * a_ref[level + 1])
        high = high.reshape(TILE, TILE, nch)
        y_ref[:, level * TILE : (level + 1) * TILE] = high
        at = (level + LEVELS) * TILE
        y_ref[:, at : at + TILE] = low.reshape(TILE, TILE, nch)
        if level >= 2:
            at = (level + 6) * TILE
            y_ref[:, at : at + TILE] = high

    kind = jnp.where(ix == 0, 0, jnp.where(ix == lax.axis_size("skyx") - 1, 2, 1))
    odd = lax.rem(ix, 2)
    columns = k_ref[2 * kind + odd]

    def column_pass(row, carry):
        got = dot(columns, y_ref[row])
        o_0[row] = got[:TILE] + a_ref[0] * x_ref[row]
        swap_ref[row] = got[TILE : 2 * TILE]
        swap_ref[row + TILE] = got[2 * TILE : 3 * TILE]
        near_ref[row] = got[3 * TILE : 4 * TILE]
        far_ref[row] = got[4 * TILE :]
        return carry

    lax.fori_loop(0, TILE, column_pass, 0, unroll=4)

    inner, outer = inner_ref[...], outer_ref[...]
    left, right = jnp.where(odd == 0, outer, inner), jnp.where(odd == 0, inner, outer)
    params = with_columns(own_ref, left, right)
    for t in range(3):
        ext_ref[t] = params[t]
    up_ref[...] = border_rows(params, 2)
    down_ref[...] = border_rows(params, TILE)


def kept(x):
    return pltpu.with_memory_space_constraint(x, pltpu.VMEM)


def wavelet_parts(coeff, tiles, own, sides, w, nch, length):
    k = jnp.asarray(scatter_matrices(length))
    vmem = pl.BlockSpec(memory_space=pltpu.VMEM)
    plain = pltpu.VMEM(tiles[-1].shape, jnp.float32)
    pair = pltpu.VMEM((2 * TILE,) + tiles[0].shape[1:], jnp.float32)
    rows = pltpu.VMEM((COMPS, EXT), jnp.float32)
    return pl.pallas_call(
        wavelet_kernel,
        out_shape=[plain, pair, plain, plain, pltpu.VMEM(own.shape, jnp.float32), rows, rows],
        in_specs=[vmem] * 11,
        out_specs=[vmem] * 7,
        scratch_shapes=[
            pltpu.VMEM((LEVELS, TILE, TILE, nch), jnp.float32),
            pltpu.VMEM((TILE, 10 * TILE, nch), jnp.bfloat16),
        ],
        compiler_params=pltpu.CompilerParams(vmem_limit_bytes=VMEM_LIMIT),
        cost_estimate=pl.CostEstimate(flops=4_000_000_000, bytes_accessed=9_000_000, transcendentals=0),
        name="wavelet_parts",
    )(*[kept(x) for x in (coeff, *tiles, k, own, *sides, w)])


def add_kernel(near_ref, swapped_ref, out_ref):
    def body(row, carry):
        out_ref[row] = near_ref[row] + swapped_ref[row + TILE]
        return carry

    lax.fori_loop(0, TILE, body, 0, unroll=4)


def outward(near, swapped):
    vmem = pl.BlockSpec(memory_space=pltpu.VMEM)
    return pl.pallas_call(
        add_kernel,
        out_shape=pltpu.VMEM(near.shape, jnp.float32),
        in_specs=[vmem] * 2,
        out_specs=vmem,
        compiler_params=pltpu.CompilerParams(vmem_limit_bytes=VMEM_LIMIT),
        cost_estimate=pl.CostEstimate(flops=100_000, bytes_accessed=1_500_000, transcendentals=0),
        name="outward",
    )(kept(near), kept(swapped))


def model_kernel(amp_ref, index_ref, spread_ref, w_hbm, model_ref, flat_ref, own_ref, inner_ref, outer_ref, w_ref, scale_ref, sem):
    load = pltpu.make_async_copy(w_hbm, w_ref, sem)
    load.start()
    nch, pixels = model_ref.shape
    own_ref[...] = jnp.zeros_like(own_ref)
    for t in range(3):
        for row in range(TILE):
            got = own_row(t, row, amp_ref, index_ref, spread_ref, nch)
            at = (row + 2) * PITCH + 2
            own_ref[t, :, at : at + TILE] = got
            flat_ref[t, :, row * TILE : (row + 1) * TILE] = got
    even = lax.rem(lax.axis_index("skyx"), 2) == 0
    to_right, to_left = border_columns(own_ref, TILE), border_columns(own_ref, 2)
    inner_ref[...] = jnp.where(even, to_right, to_left)
    outer_ref[...] = jnp.where(even, to_left, to_right)
    mu = flat_ref[1] * float(nch)
    inv = 1.0 / flat_ref[2]
    flat_ref[1] = mu
    flat_ref[2] = inv
    scale_ref[...] = (-0.5 * math.log2(math.e)) * inv * inv

    def body(step, carry):
        base = pl.multiple_of(step * 8, 8)
        chan = (lax.broadcasted_iota(jnp.int32, (8, pixels), 0) + base).astype(jnp.float32)
        total = jnp.zeros((8, pixels), jnp.float32)
        for k in range(COMPS):
            diff = chan - flat_ref[1, k : k + 1, :]
            bump = jnp.exp2(diff * diff * scale_ref[k : k + 1, :])
            total += flat_ref[0, k : k + 1, :] * bump
        model_ref[pl.ds(base, 8), :] = total
        return carry

    lax.fori_loop(0, nch // 8, body, 0, unroll=2)
    load.wait()


def model_of(amplitude, centre_index, spread, nch):
    w = jnp.asarray(channel_matrices(nch))
    vmem = pl.BlockSpec(memory_space=pltpu.VMEM)
    pixels = TILE * TILE
    return pl.pallas_call(
        model_kernel,
        out_shape=[
            pltpu.VMEM((nch, pixels), jnp.float32),
            pltpu.VMEM((3, COMPS, pixels), jnp.float32),
            pltpu.VMEM((3, COMPS, EXT), jnp.float32),
            pltpu.VMEM((COMPS, EXT), jnp.float32),
            pltpu.VMEM((COMPS, EXT), jnp.float32),
            pltpu.VMEM(w.shape, w.dtype),
        ],
        in_specs=[vmem] * 3 + [pl.BlockSpec(memory_space=pl.ANY)],
        out_specs=[vmem] * 6,
        scratch_shapes=[pltpu.VMEM((COMPS, pixels), jnp.float32), pltpu.SemaphoreType.DMA],
        compiler_params=pltpu.CompilerParams(vmem_limit_bytes=VMEM_LIMIT),
        cost_estimate=pl.CostEstimate(flops=10_000_000, bytes_accessed=1_000_000, transcendentals=1_100_000),
        name="gaussian_model",
    )(amplitude, centre_index, spread, pltpu.with_memory_space_constraint(w, pltpu.HBM))


def step_kernel(
    o_0, swapped_ref, far_ref, near_ref, model_ref, flat_ref, base_ref,
    den_hbm, fit_ref, den_ref, r_ref, sem,
):
    nch, pixels = model_ref.shape
    rows = LANES // TILE
    parts = pixels // LANES
    copies = []
    for part in range(parts):
        at = slice(part * rows, (part + 1) * rows)
        for row in range(part * rows, (part + 1) * rows):
            den_ref[row] = (o_0[row] + swapped_ref[row]) + (far_ref[row] + near_ref[row])
        copies.append(pltpu.make_async_copy(den_ref.at[at], den_hbm.at[at], sem.at[part]))
        copies[-1].start()

    shape = (COMPS, rows, LANES)
    own_lanes = lax.broadcasted_iota(jnp.int32, shape, 2) // TILE == lax.broadcasted_iota(jnp.int32, shape, 1)
    for part in range(parts):
        block = den_ref[part * rows : (part + 1) * rows].reshape(LANES, nch)
        at = slice(part * LANES, (part + 1) * LANES)
        r_ref[:, at] = model_ref[:, at] - block.T

    for part in range(parts):
        at = slice(part * LANES, (part + 1) * LANES)
        sums = [[] for _ in range(3)]
        for first in range(0, COMPS, 4):
            chosen = range(first, first + 4)
            mus = [jnp.broadcast_to(flat_ref[1, k : k + 1, at], (8, LANES)) for k in chosen]
            inv = [jnp.broadcast_to(flat_ref[2, k : k + 1, at], (8, LANES)) for k in chosen]
            scales = [(-0.5 * math.log2(math.e)) * v * v for v in inv]

            def body(step, carry):
                base = pl.multiple_of(step * 8, 8)
                chan = (lax.broadcasted_iota(jnp.int32, (8, LANES), 0) + base).astype(jnp.float32)
                r = r_ref[pl.ds(base, 8), at]
                out = []
                for mu, scale, (a, b, c) in zip(mus, scales, carry):
                    diff = chan - mu
                    one = r * jnp.exp2(diff * diff * scale)
                    two = one * diff
                    out.append((a + one, b + two, c + two * diff))
                return tuple(out)

            zero = jnp.zeros((8, LANES), jnp.float32)
            done = lax.fori_loop(0, nch // 8, body, ((zero,) * 3,) * 4, unroll=8)
            for four in done:
                for t in range(3):
                    sums[t].append(jnp.sum(four[t], axis=0, keepdims=True))
        amp = flat_ref[0, :, at]
        inv = flat_ref[2, :, at]
        slope = amp * inv * inv
        grads = (
            jnp.concatenate(sums[0], axis=0) * (1.0 / nch),
            jnp.concatenate(sums[1], axis=0) * slope,
            jnp.concatenate(sums[2], axis=0) * (slope * inv * (1.0 / nch)),
        )
        for t in range(3):
            new = base_ref[t, :, at] - STEPS[t] * grads[t]
            spread_out = jnp.where(own_lanes, jnp.broadcast_to(new[:, None, :], own_lanes.shape), 0.0)
            for shift in (LANES // 2, LANES // 4, LANES // 8):
                spread_out = spread_out + pltpu.roll(spread_out, shift, 2)
            fit_ref[t, :, part * rows : (part + 1) * rows, :] = spread_out[:, :, :TILE]

    for copy in copies:
        copy.wait()


def gradient_step(parts, model, flat, base):
    vmem = pl.BlockSpec(memory_space=pltpu.VMEM)
    shape = parts[0].shape
    return pl.pallas_call(
        step_kernel,
        out_shape=[
            jax.ShapeDtypeStruct(shape, jnp.float32),
            jax.ShapeDtypeStruct((3, COMPS, TILE, TILE), jnp.float32),
        ],
        in_specs=[vmem] * 7,
        out_specs=[pl.BlockSpec(memory_space=pl.ANY), vmem],
        scratch_shapes=[
            pltpu.VMEM(shape, jnp.float32),
            pltpu.VMEM(model.shape, jnp.float32),
            pltpu.SemaphoreType.DMA((2,)),
        ],
        compiler_params=pltpu.CompilerParams(vmem_limit_bytes=VMEM_LIMIT),
        cost_estimate=pl.CostEstimate(flops=15_000_000, bytes_accessed=4_000_000, transcendentals=1_100_000),
        name="gradient_step",
    )(*[kept(x) for x in (*parts, model, flat, base)])


def on_device(cube, level_table, level_index, amplitude, centre_index, spread):
    nch = cube.shape[2]
    size = lax.axis_size("skyx")
    partner = [(i, i ^ 1) for i in range(size)]

    up1, down1 = sent(cube, "skyy", 1), sent(cube, "skyy", -1)
    up2, down2 = sent(cube[BEYOND:], "skyy", 2), sent(cube[:-BEYOND], "skyy", -2)

    entries = jnp.arange(level_table.shape[0], dtype=jnp.int32)
    picks = (level_index[:, :, None] == entries).astype(jnp.float32)
    weight = jnp.sum(picks * level_table, axis=2)
    one = jnp.ones((1, nch), jnp.float32)
    coeff = jnp.concatenate([weight, one]) - jnp.concatenate([0.0 * one, weight])
    scale = jnp.array([16.0 ** (-3 * j) for j in range(LEVELS + 1)], jnp.float32)
    coeff = (coeff * scale[:, None])[:, None, :]
    model, flat, own, inner, outer, w = model_of(amplitude, centre_index, spread, nch)
    sides = lax.ppermute(inner, "skyx", partner), away(outer, "skyx", 1)
    o_0, swap, near, far, ext, for_up, for_down = wavelet_parts(
        coeff, (up1, down1, up2, down2, cube), own, sides, w, nch, size * TILE
    )

    swapped = lax.ppermute(swap, "skyx", partner)
    far = away(far, "skyx", 2)
    near = away(outward(near, swapped), "skyx", 1)
    above, below = sent(for_down, "skyy", 1), sent(for_up, "skyy", -1)
    return gradient_step((o_0, swapped, far, near), model, flat, base_of(ext, above, below))


def solution(mesh):
    placed = (
        P("skyy", "skyx", None),
        P(),
        P(),
        P(None, "skyy", "skyx"),
        P(None, "skyy", "skyx"),
        P(None, "skyy", "skyx"),
    )
    return jax.shard_map(
        on_device,
        mesh=mesh,
        in_specs=placed,
        out_specs=(P("skyy", "skyx", None), P(None, None, "skyy", "skyx")),
        check_vma=False,
    )
```

```python
import functools
import math

import jax
import jax.numpy as jnp
import numpy as np
from jax import lax
from jax.experimental import pallas as pl
from jax.experimental.pallas import tpu as pltpu
from jax.sharding import PartitionSpec as P

TILE = 16
LEVELS = 4
COMPS = 8
LANES = 128
TAPS = (1, 4, 6, 4, 1)
BEYOND = 2
VMEM_LIMIT = 20 * 1024 * 1024
ROLES = ((2, 3, 4, 1, 0), (2, 1, 0, 3, 4))
PIXELS = TILE * TILE
PITCH = 24
EXT = 512
STEPS = (0.5, 0.002, 2.0)
LAMS = (0.2, 0.5, 0.05)


def blur_matrix(length, gap):
    out = np.zeros((length, length), np.float64)
    for tap, factor in enumerate(TAPS):
        offset = (tap - 2) * gap
        for i in range(max(0, -offset), min(length, length - offset)):
            out[i, i + offset] = factor
    return out


def composites(length):
    made, now = [], np.eye(length)
    for level in range(LEVELS):
        now = blur_matrix(length, 2**level) @ now
        made.append(now)
    return made


def halves(matrix):
    bf16 = jnp.bfloat16
    high = np.asarray(matrix, np.float32).astype(bf16)
    low = (np.asarray(matrix, np.float32) - high.astype(np.float32)).astype(bf16)
    return high, low


def channel_matrices(nch):
    parts = [halves(m.T) for m in composites(nch)]
    half, quarter = nch // 2, nch // 4
    out = []
    for whole in [p[0] for p in parts] + [p[1] for p in parts[2:]]:
        across = whole[quarter : quarter + half, quarter : quarter + half].copy()
        across[:quarter, :quarter] = 0
        across[quarter:, quarter:] = 0
        out.append(np.stack([whole[:half, :half], across, whole[half:, half:]]))
    return np.stack(out)


def scatter_matrices(length):
    whole = composites(length)
    kinds = []
    for start in (0, TILE * (length // TILE // 2), length - TILE):
        parts = []
        for m in whole:
            block = np.zeros((5 * TILE, TILE))
            for k in range(5 * TILE):
                at = start - 2 * TILE + k
                if 0 <= at < length:
                    block[k] = m[at, start : start + TILE]
            parts.append(halves(block))
        high = np.concatenate([p[0] for p in parts], axis=1)
        low = np.concatenate([p[1] for p in parts[2:]], axis=1)
        columns = np.concatenate([high, high, low], axis=1).reshape(5, TILE, -1)
        for order in ROLES:
            kinds.append(np.concatenate([columns[i] for i in order]))
    return np.stack(kinds)


def sent(values, axis, by):
    size = lax.axis_size(axis)
    if by > 0:
        pairs = [(i, i + by) for i in range(size - by)]
    else:
        pairs = [(i, i + by) for i in range(-by, size)]
    return lax.ppermute(values, axis, pairs)


def away(values, axis, by):
    size = lax.axis_size(axis)
    pairs = [(i, i + by if i % 2 else i - by) for i in range(size)]
    return lax.ppermute(values, axis, [(i, j) for i, j in pairs if 0 <= j < size])


def own_row(t, row, amp_ref, index_ref, spread_ref, nch):
    if t == 0:
        return amp_ref[:, row, :]
    if t == 1:
        return (index_ref[:, row, :].astype(jnp.float32) + 0.5) * (1.0 / nch)
    return spread_ref[:, row, :]


def pack_kernel(cube_hbm, amp_ref, index_ref, spread_ref, up_ref, down_ref, sem):
    nch = cube_hbm.shape[1]
    copies = []
    for i, out in enumerate((up_ref, down_ref)):
        copies.append(pltpu.make_async_copy(cube_hbm, out.at[0:PIXELS], sem.at[i]))
        copies[-1].start()
    for out, first in ((up_ref, TILE - 2), (down_ref, 0)):
        out[PIXELS:, :] = jnp.zeros((COMPS, nch), jnp.float32)
        for t in range(3):
            for r in range(2):
                lane = (2 * t + r) * PITCH + 2
                got = own_row(t, first + r, amp_ref, index_ref, spread_ref, nch)
                out[PIXELS:, lane : lane + TILE] = got
    for copy in copies:
        copy.wait()


def packed(cube, amplitude, centre_index, spread):
    vmem = pl.BlockSpec(memory_space=pltpu.VMEM)
    hbm = [pltpu.with_memory_space_constraint(v, pltpu.HBM) for v in (cube, amplitude, centre_index, spread)]
    return pl.pallas_call(
        pack_kernel,
        out_shape=[pltpu.VMEM((PIXELS + COMPS, cube.shape[1]), jnp.float32)] * 2,
        in_specs=[pl.BlockSpec(memory_space=pl.ANY)] + [vmem] * 3,
        out_specs=[vmem] * 2,
        scratch_shapes=[pltpu.SemaphoreType.DMA((2,))],
        compiler_params=pltpu.CompilerParams(vmem_limit_bytes=VMEM_LIMIT),
        cost_estimate=pl.CostEstimate(flops=1000, bytes_accessed=1_000_000, transcendentals=0),
        name="pack",
    )(*hbm)


def border_columns(ext_ref, shift):
    lane = lax.broadcasted_iota(jnp.int32, (COMPS, EXT), 1) % PITCH
    total = jnp.zeros((COMPS, EXT), jnp.float32)
    for t in range(3):
        moved = pltpu.roll(ext_ref[t], (2 * t - shift) % EXT, 1)
        total = jnp.where((lane >= 2 * t) & (lane < 2 * t + 2), moved, total)
    return total


def with_columns(own, left, right):
    column = lax.broadcasted_iota(jnp.int32, (COMPS, EXT), 1) % PITCH
    out = []
    for t in range(3):
        p = jnp.where(column < 2, pltpu.roll(left, (EXT - 2 * t) % EXT, 1), own[t])
        out.append(jnp.where(column >= TILE + 2, pltpu.roll(right, (TILE + 2 - 2 * t) % EXT, 1), p))
    return out


def with_rows(own, above, below):
    row = lax.broadcasted_iota(jnp.int32, (COMPS, EXT), 1) // PITCH
    out = []
    for t in range(3):
        p = jnp.where(row < 2, pltpu.roll(above, (EXT - 2 * t * PITCH) % EXT, 1), own[t])
        out.append(jnp.where(row >= TILE + 2, pltpu.roll(below, ((TILE + 2 - 2 * t) * PITCH) % EXT, 1), p))
    return out


def stencil(p):
    near = pltpu.roll(p, 1, 1) + pltpu.roll(p, EXT - 1, 1)
    return 4.0 * p - (near + (pltpu.roll(p, PITCH, 1) + pltpu.roll(p, EXT - PITCH, 1)))


def smoothed(params):
    lane = lax.broadcasted_iota(jnp.int32, (COMPS, EXT), 1)
    y = lane // PITCH + (lax.axis_index("skyy") * TILE - 2)
    x = lane % PITCH + (lax.axis_index("skyx") * TILE - 2)
    ny, nx = lax.axis_size("skyy") * TILE, lax.axis_size("skyx") * TILE
    on_sky = (y >= 0) & (y < ny) & (x >= 0) & (x < nx)
    out = []
    for t, p in enumerate(params):
        first = jnp.where(on_sky, stencil(p), 0.0)
        out.append(p - (STEPS[t] * LAMS[t]) * stencil(first))
    return out


def five(v, flag=None):
    total = (v[0] + v[4]) + 4.0 * (v[1] + v[3]) + 6.0 * v[2]
    return total if flag is None else total * flag


def split(v):
    high = v.astype(jnp.bfloat16)
    return high, (v - high.astype(jnp.float32)).astype(jnp.bfloat16)


def wavelet_kernel(
    a_ref, m1, p1, m2, p2, x_ref, k_ref, own_ref, w_ref,
    o_0, swap_ref, near_ref, far_ref, ext_ref, rows_ref, y_ref,
):
    nch = x_ref.shape[2]
    tiles = (m2, m1, x_ref, p1, p2)
    iy, ix = lax.axis_index("skyy"), lax.axis_index("skyx")
    near = [iy + i for i in (-2, -1, 0, 1, 2)]
    flags = [jnp.where((i >= 0) & (i < lax.axis_size("skyy")), 1.0, 0.0) for i in near]

    lane_tiles = nch // LANES

    def row_pass(step, carry):
        sub = pl.ds(pl.multiple_of((step // lane_tiles) * 8, 8), 8)
        lane = pl.ds(pl.multiple_of((step % lane_tiles) * LANES, LANES), LANES)

        @functools.cache
        def value(level, at):
            tile = (at + 2 * TILE) // TILE
            if level == 0:
                if tile in (1, 3):
                    start = pl.multiple_of(at % TILE * TILE + step // lane_tiles * 8, 8)
                    return tiles[tile][pl.ds(start, 8), lane]
                return tiles[tile][at % TILE - (BEYOND if tile == 0 else 0), sub, lane]
            gap = 2 ** (level - 1)
            taps = [value(level - 1, at + (t - 2) * gap) for t in range(5)]
            return five(taps, None if tile == 2 else flags[tile])

        reach = {1: 28, 2: 24, 3: 16, 4: 0}
        lag = {1: 2, 2: 6, 3: 14, 4: 30}
        for at in range(-30, TILE + 30):
            value(0, at)
            for level in range(1, LEVELS + 1):
                row = at - lag[level]
                if -reach[level] <= row < TILE + reach[level]:
                    got = value(level, row)
                    if 0 <= row < TILE:
                        rows_ref[level - 1, row, sub, lane] = got
        return carry

    lax.fori_loop(0, 2 * lane_tiles, row_pass, 0)

    half, quarter = nch // 2, nch // 4

    def product(v, index):
        blocks = [
            jnp.dot(v[:, at : at + half], w_ref[index, i], preferred_element_type=jnp.float32)
            for i, at in enumerate((0, quarter, half))
        ]
        return blocks

    for level in range(LEVELS):
        high, low = split(rows_ref[level].reshape(PIXELS, nch))
        terms = [product(high, level), product(low, level)]
        if level >= 2:
            terms.append(product(high, level + 2))
        first, middle, last = [functools.reduce(lambda a, b: a + b, v) for v in zip(*terms)]
        pieces = (
            first[:, :quarter],
            first[:, quarter:] + middle[:, :quarter],
            middle[:, quarter:] + last[:, :quarter],
            last[:, quarter:],
        )
        for i, piece in enumerate(pieces):
            lane = slice(i * quarter, (i + 1) * quarter)
            high, low = split(piece * a_ref[level + 1, :, lane])
            high = high.reshape(TILE, TILE, quarter)
            y_ref[:, level * TILE : (level + 1) * TILE, lane] = high
            at = (level + LEVELS) * TILE
            y_ref[:, at : at + TILE, lane] = low.reshape(TILE, TILE, quarter)
            if level >= 2:
                at = (level + 6) * TILE
                y_ref[:, at : at + TILE, lane] = high

    kind = jnp.where(ix == 0, 0, jnp.where(ix == lax.axis_size("skyx") - 1, 2, 1))
    odd = lax.rem(ix, 2)
    columns = k_ref[2 * kind + odd]

    def column_pass(row, carry):
        got = jnp.dot(columns, y_ref[row], preferred_element_type=jnp.float32)
        at = pl.ds(pl.multiple_of(row * TILE, TILE), TILE)
        at_more = pl.ds(pl.multiple_of(row * TILE + PIXELS, TILE), TILE)
        o_0[row] = got[:TILE] + a_ref[0] * x_ref[row]
        swap_ref[at] = got[TILE : 2 * TILE]
        swap_ref[at_more] = got[2 * TILE : 3 * TILE]
        near_ref[at] = got[3 * TILE : 4 * TILE]
        far_ref[at] = got[4 * TILE :]
        return carry

    lax.fori_loop(0, TILE, column_pass, 0, unroll=4)

    params = with_rows(own_ref, m1[PIXELS:, :], p1[PIXELS:, :])
    for t in range(3):
        ext_ref[t] = params[t]
    to_right, to_left = border_columns(ext_ref, TILE), border_columns(ext_ref, 2)
    swap_ref[2 * PIXELS :, :] = jnp.where(odd == 0, to_right, to_left)
    near_ref[PIXELS:, :] = jnp.where(odd == 0, to_left, to_right)


def kept(x):
    return pltpu.with_memory_space_constraint(x, pltpu.VMEM)


def wavelet_parts(coeff, tiles, own, w, nch, length):
    k = jnp.asarray(scatter_matrices(length))
    vmem = pl.BlockSpec(memory_space=pltpu.VMEM)
    shapes = [tiles[-1].shape] + [(n, nch) for n in (2 * PIXELS + COMPS, PIXELS + COMPS, PIXELS + COMPS)] + [own.shape]
    return pl.pallas_call(
        wavelet_kernel,
        out_shape=[pltpu.VMEM(shape, jnp.float32) for shape in shapes],
        in_specs=[vmem] * 9,
        out_specs=[vmem] * 5,
        scratch_shapes=[
            pltpu.VMEM((LEVELS, TILE, TILE, nch), jnp.float32),
            pltpu.VMEM((TILE, 10 * TILE, nch), jnp.bfloat16),
        ],
        compiler_params=pltpu.CompilerParams(vmem_limit_bytes=VMEM_LIMIT),
        cost_estimate=pl.CostEstimate(flops=4_000_000_000, bytes_accessed=9_000_000, transcendentals=0),
        name="wavelet_parts",
    )(*[kept(x) for x in (coeff, *tiles, k, own, w)])


def add_kernel(near_ref, swapped_ref, out_ref):
    def body(row, carry):
        at = pl.ds(pl.multiple_of(row * TILE, TILE), TILE)
        more = pl.ds(pl.multiple_of(row * TILE + PIXELS, TILE), TILE)
        out_ref[at] = near_ref[at] + swapped_ref[more]
        return carry

    lax.fori_loop(0, TILE, body, 0, unroll=4)
    out_ref[PIXELS:, :] = near_ref[PIXELS:, :]


def outward(near, swapped):
    vmem = pl.BlockSpec(memory_space=pltpu.VMEM)
    return pl.pallas_call(
        add_kernel,
        out_shape=pltpu.VMEM(near.shape, jnp.float32),
        in_specs=[vmem] * 2,
        out_specs=vmem,
        compiler_params=pltpu.CompilerParams(vmem_limit_bytes=VMEM_LIMIT),
        cost_estimate=pl.CostEstimate(flops=100_000, bytes_accessed=1_500_000, transcendentals=0),
        name="outward",
    )(kept(near), kept(swapped))


def model_kernel(amp_ref, index_ref, spread_ref, w_hbm, model_ref, flat_ref, own_ref, w_ref, scale_ref, sem):
    load = pltpu.make_async_copy(w_hbm, w_ref, sem)
    load.start()
    nch, pixels = model_ref.shape
    own_ref[...] = jnp.zeros_like(own_ref)
    for t in range(3):
        for row in range(TILE):
            got = own_row(t, row, amp_ref, index_ref, spread_ref, nch)
            at = (row + 2) * PITCH + 2
            own_ref[t, :, at : at + TILE] = got
            flat_ref[t, :, row * TILE : (row + 1) * TILE] = got
    mu = flat_ref[1] * float(nch)
    inv = 1.0 / flat_ref[2]
    flat_ref[1] = mu
    flat_ref[2] = inv
    scale_ref[...] = (-0.5 * math.log2(math.e)) * inv * inv

    def body(step, carry):
        base = pl.multiple_of(step * 8, 8)
        chan = (lax.broadcasted_iota(jnp.int32, (8, pixels), 0) + base).astype(jnp.float32)
        total = jnp.zeros((8, pixels), jnp.float32)
        for k in range(COMPS):
            diff = chan - flat_ref[1, k : k + 1, :]
            bump = jnp.exp2(diff * diff * scale_ref[k : k + 1, :])
            total += flat_ref[0, k : k + 1, :] * bump
        model_ref[pl.ds(base, 8), :] = total
        return carry

    lax.fori_loop(0, nch // 8, body, 0, unroll=2)
    load.wait()


def model_of(amplitude, centre_index, spread, nch):
    w = jnp.asarray(channel_matrices(nch))
    vmem = pl.BlockSpec(memory_space=pltpu.VMEM)
    pixels = TILE * TILE
    return pl.pallas_call(
        model_kernel,
        out_shape=[
            pltpu.VMEM((nch, pixels), jnp.float32),
            pltpu.VMEM((3, COMPS, pixels), jnp.float32),
            pltpu.VMEM((3, COMPS, EXT), jnp.float32),
            pltpu.VMEM(w.shape, w.dtype),
        ],
        in_specs=[vmem] * 3 + [pl.BlockSpec(memory_space=pl.ANY)],
        out_specs=[vmem] * 4,
        scratch_shapes=[pltpu.VMEM((COMPS, pixels), jnp.float32), pltpu.SemaphoreType.DMA],
        compiler_params=pltpu.CompilerParams(vmem_limit_bytes=VMEM_LIMIT),
        cost_estimate=pl.CostEstimate(flops=10_000_000, bytes_accessed=1_000_000, transcendentals=1_100_000),
        name="gaussian_model",
    )(amplitude, centre_index, spread, pltpu.with_memory_space_constraint(w, pltpu.HBM))


def step_kernel(
    o_0, swapped_ref, far_ref, near_ref, model_ref, flat_ref, ext_ref,
    den_hbm, fit_ref, den_ref, r_ref, sem,
):
    nch, pixels = model_ref.shape
    rows = LANES // TILE
    parts = pixels // LANES
    copies = []
    inner, outer = swapped_ref[2 * PIXELS :, :], near_ref[PIXELS:, :]
    even = lax.rem(lax.axis_index("skyx"), 2) == 0
    left, right = jnp.where(even, outer, inner), jnp.where(even, inner, outer)
    bases = smoothed(with_columns(ext_ref, left, right))
    for part in range(parts):
        at = slice(part * rows, (part + 1) * rows)
        for row in range(part * rows, (part + 1) * rows):
            flat = slice(row * TILE, (row + 1) * TILE)
            den_ref[row] = (o_0[row] + swapped_ref[flat]) + (far_ref[flat] + near_ref[flat])
        copies.append(pltpu.make_async_copy(den_ref.at[at], den_hbm.at[at], sem.at[part]))
        copies[-1].start()

    shape = (COMPS, rows, LANES)
    own_lanes = lax.broadcasted_iota(jnp.int32, shape, 2) // TILE == lax.broadcasted_iota(jnp.int32, shape, 1)
    for part in range(parts):
        block = den_ref[part * rows : (part + 1) * rows].reshape(LANES, nch)
        at = slice(part * LANES, (part + 1) * LANES)
        r_ref[:, at] = model_ref[:, at] - block.T

    for part in range(parts):
        at = slice(part * LANES, (part + 1) * LANES)
        sums = [[] for _ in range(3)]
        for first in range(0, COMPS, 4):
            chosen = range(first, first + 4)
            mus = [jnp.broadcast_to(flat_ref[1, k : k + 1, at], (8, LANES)) for k in chosen]
            inv = [jnp.broadcast_to(flat_ref[2, k : k + 1, at], (8, LANES)) for k in chosen]
            scales = [(-0.5 * math.log2(math.e)) * v * v for v in inv]

            def body(step, carry):
                base = pl.multiple_of(step * 8, 8)
                chan = (lax.broadcasted_iota(jnp.int32, (8, LANES), 0) + base).astype(jnp.float32)
                r = r_ref[pl.ds(base, 8), at]
                out = []
                for mu, scale, (a, b, c) in zip(mus, scales, carry):
                    diff = chan - mu
                    one = r * jnp.exp2(diff * diff * scale)
                    two = one * diff
                    out.append((a + one, b + two, c + two * diff))
                return tuple(out)

            zero = jnp.zeros((8, LANES), jnp.float32)
            done = lax.fori_loop(0, nch // 8, body, ((zero,) * 3,) * 4, unroll=8)
            for four in done:
                for t in range(3):
                    sums[t].append(jnp.sum(four[t], axis=0, keepdims=True))
        amp = flat_ref[0, :, at]
        inv = flat_ref[2, :, at]
        slope = amp * inv * inv
        grads = (
            jnp.concatenate(sums[0], axis=0) * (1.0 / nch),
            jnp.concatenate(sums[1], axis=0) * slope,
            jnp.concatenate(sums[2], axis=0) * (slope * inv * (1.0 / nch)),
        )
        for t in range(3):
            lanes = [(part * rows + i + 2) * PITCH + 2 for i in range(rows)]
            base = jnp.concatenate([bases[t][:, lane : lane + TILE] for lane in lanes], axis=1)
            new = base - STEPS[t] * grads[t]
            spread_out = jnp.where(own_lanes, jnp.broadcast_to(new[:, None, :], own_lanes.shape), 0.0)
            for shift in (LANES // 2, LANES // 4, LANES // 8):
                spread_out = spread_out + pltpu.roll(spread_out, shift, 2)
            fit_ref[t, :, part * rows : (part + 1) * rows, :] = spread_out[:, :, :TILE]

    for copy in copies:
        copy.wait()


def gradient_step(parts, model, flat, ext):
    vmem = pl.BlockSpec(memory_space=pltpu.VMEM)
    shape = parts[0].shape
    return pl.pallas_call(
        step_kernel,
        out_shape=[
            jax.ShapeDtypeStruct(shape, jnp.float32),
            jax.ShapeDtypeStruct((3, COMPS, TILE, TILE), jnp.float32),
        ],
        in_specs=[vmem] * 7,
        out_specs=[pl.BlockSpec(memory_space=pl.ANY), vmem],
        scratch_shapes=[
            pltpu.VMEM(shape, jnp.float32),
            pltpu.VMEM(model.shape, jnp.float32),
            pltpu.SemaphoreType.DMA((2,)),
        ],
        compiler_params=pltpu.CompilerParams(vmem_limit_bytes=VMEM_LIMIT),
        cost_estimate=pl.CostEstimate(flops=15_000_000, bytes_accessed=4_000_000, transcendentals=1_100_000),
        name="gradient_step",
    )(*[kept(x) for x in (*parts, model, flat, ext)])


def on_device(cube, level_table, level_index, amplitude, centre_index, spread):
    nch = cube.shape[2]
    size = lax.axis_size("skyx")
    partner = [(i, i ^ 1) for i in range(size)]

    for_down, for_up = packed(cube.reshape(PIXELS, nch), amplitude, centre_index, spread)
    up1, down1 = sent(for_down, "skyy", 1), sent(for_up, "skyy", -1)
    up2, down2 = sent(cube[BEYOND:], "skyy", 2), sent(cube[:-BEYOND], "skyy", -2)

    entries = jnp.arange(level_table.shape[0], dtype=jnp.int32)
    picks = (level_index[:, :, None] == entries).astype(jnp.float32)
    weight = jnp.sum(picks * level_table, axis=2)
    one = jnp.ones((1, nch), jnp.float32)
    coeff = jnp.concatenate([weight, one]) - jnp.concatenate([0.0 * one, weight])
    scale = jnp.array([16.0 ** (-3 * j) for j in range(LEVELS + 1)], jnp.float32)
    coeff = (coeff * scale[:, None])[:, None, :]
    model, flat, own, w = model_of(amplitude, centre_index, spread, nch)
    o_0, swap, near, far, ext = wavelet_parts(coeff, (up1, down1, up2, down2, cube), own, w, nch, size * TILE)

    swapped = lax.ppermute(swap, "skyx", partner)
    far = away(far, "skyx", 2)
    near = away(outward(near, swapped), "skyx", 1)
    return gradient_step((o_0, swapped, far, near), model, flat, ext)


def solution(mesh):
    placed = (
        P("skyy", "skyx", None),
        P(),
        P(),
        P(None, "skyy", "skyx"),
        P(None, "skyy", "skyx"),
        P(None, "skyy", "skyx"),
    )
    return jax.shard_map(
        on_device,
        mesh=mesh,
        in_specs=placed,
        out_specs=(P("skyy", "skyx", None), P(None, None, "skyy", "skyx")),
        check_vma=False,
    )
```

```python
import functools
import math

import jax
import jax.numpy as jnp
import numpy as np
from jax import lax
from jax.experimental import pallas as pl
from jax.experimental.pallas import tpu as pltpu
from jax.sharding import PartitionSpec as P

TILE = 16
LEVELS = 4
COMPS = 8
LANES = 128
TAPS = (1, 4, 6, 4, 1)
BEYOND = 2
VMEM_LIMIT = 20 * 1024 * 1024
ROLES = ((2, 3, 1, 4, 0), (2, 1, 3, 0, 4))
PIXELS = TILE * TILE
PITCH = 24
FIRST_ROWS = 256
EXT = 512
STEPS = (0.5, 0.002, 2.0)
LAMS = (0.2, 0.5, 0.05)


def blur_matrix(length, gap):
    out = np.zeros((length, length), np.float64)
    for tap, factor in enumerate(TAPS):
        offset = (tap - 2) * gap
        for i in range(max(0, -offset), min(length, length - offset)):
            out[i, i + offset] = factor
    return out


def composites(length):
    made, now = [], np.eye(length)
    for level in range(LEVELS):
        now = blur_matrix(length, 2**level) @ now
        made.append(now)
    return made


def halves(matrix):
    bf16 = jnp.bfloat16
    high = np.asarray(matrix, np.float32).astype(bf16)
    low = (np.asarray(matrix, np.float32) - high.astype(np.float32)).astype(bf16)
    return high, low


def channel_matrices(nch):
    parts = [halves(m.T) for m in composites(nch)]
    half, quarter = nch // 2, nch // 4
    out = []
    for whole in [p[0] for p in parts] + [p[1] for p in parts[2:]]:
        across = whole[quarter : quarter + half, quarter : quarter + half].copy()
        across[:quarter, :quarter] = 0
        across[quarter:, quarter:] = 0
        out.append(np.stack([whole[:half, :half], across, whole[half:, half:]]))
    return np.stack(out)


def scatter_matrices(length):
    whole = composites(length)
    kinds = []
    for start in (0, TILE * (length // TILE // 2), length - TILE):
        parts = []
        for m in whole:
            block = np.zeros((5 * TILE, TILE))
            for k in range(5 * TILE):
                at = start - 2 * TILE + k
                if 0 <= at < length:
                    block[k] = m[at, start : start + TILE]
            parts.append(halves(block))
        high = np.concatenate([p[0] for p in parts], axis=1)
        low = np.concatenate([p[1] for p in parts[2:]], axis=1)
        columns = np.concatenate([high, high, low], axis=1).reshape(5, TILE, -1)
        for order in ROLES:
            kinds.append(np.concatenate([columns[i] for i in order]))
    return np.stack(kinds)


def sent(values, axis, by):
    size = lax.axis_size(axis)
    if by > 0:
        pairs = [(i, i + by) for i in range(size - by)]
    else:
        pairs = [(i, i + by) for i in range(-by, size)]
    return lax.ppermute(values, axis, pairs)


def away(values, axis, by):
    size = lax.axis_size(axis)
    pairs = [(i, i + by if i % 2 else i - by) for i in range(size)]
    return lax.ppermute(values, axis, [(i, j) for i, j in pairs if 0 <= j < size])


def own_row(t, row, amp_ref, index_ref, spread_ref, nch):
    if t == 0:
        return amp_ref[:, row, :]
    if t == 1:
        return (index_ref[:, row, :].astype(jnp.float32) + 0.5) * (1.0 / nch)
    return spread_ref[:, row, :]


def pack_kernel(cube_hbm, amp_hbm, index_hbm, spread_hbm, out_ref, amp_ref, index_ref, spread_ref, sem):
    pairs = ((amp_hbm, amp_ref), (index_hbm, index_ref), (spread_hbm, spread_ref), (cube_hbm, out_ref.at[0:PIXELS]))
    copies = [pltpu.make_async_copy(a, b, sem.at[i]) for i, (a, b) in enumerate(pairs)]
    for copy in copies:
        copy.start()
    nch = cube_hbm.shape[1]
    out_ref[PIXELS:, :] = jnp.zeros((COMPS, nch), jnp.float32)
    for copy in copies[:3]:
        copy.wait()
    for start, first in ((0, TILE - 2), (FIRST_ROWS, 0)):
        for t in range(3):
            for r in range(2):
                lane = start + (2 * t + r) * PITCH + 2
                got = own_row(t, first + r, amp_ref, index_ref, spread_ref, nch)
                out_ref[PIXELS:, lane : lane + TILE] = got
    copies[3].wait()


def packed(cube, amplitude, centre_index, spread):
    hbm = [pltpu.with_memory_space_constraint(v, pltpu.HBM) for v in (cube, amplitude, centre_index, spread)]
    return pl.pallas_call(
        pack_kernel,
        out_shape=pltpu.VMEM((PIXELS + COMPS, cube.shape[1]), jnp.float32),
        in_specs=[pl.BlockSpec(memory_space=pl.ANY)] * 4,
        out_specs=pl.BlockSpec(memory_space=pltpu.VMEM),
        scratch_shapes=[pltpu.VMEM(v.shape, v.dtype) for v in hbm[1:]] + [pltpu.SemaphoreType.DMA((4,))],
        compiler_params=pltpu.CompilerParams(vmem_limit_bytes=VMEM_LIMIT),
        cost_estimate=pl.CostEstimate(flops=1000, bytes_accessed=1_000_000, transcendentals=0),
        name="pack",
    )(*hbm)


def border_columns(ext_ref, shift):
    lane = lax.broadcasted_iota(jnp.int32, (COMPS, EXT), 1) % PITCH
    total = jnp.zeros((COMPS, EXT), jnp.float32)
    for t in range(3):
        moved = pltpu.roll(ext_ref[t], (2 * t - shift) % EXT, 1)
        total = jnp.where((lane >= 2 * t) & (lane < 2 * t + 2), moved, total)
    return total


def with_columns(own, left, right):
    column = lax.broadcasted_iota(jnp.int32, (COMPS, EXT), 1) % PITCH
    out = []
    for t in range(3):
        p = jnp.where(column < 2, pltpu.roll(left, (EXT - 2 * t) % EXT, 1), own[t])
        out.append(jnp.where(column >= TILE + 2, pltpu.roll(right, (TILE + 2 - 2 * t) % EXT, 1), p))
    return out


def with_rows(own, above, below):
    row = lax.broadcasted_iota(jnp.int32, (COMPS, EXT), 1) // PITCH
    out = []
    for t in range(3):
        p = jnp.where(row < 2, pltpu.roll(above, (EXT - 2 * t * PITCH) % EXT, 1), own[t])
        out.append(jnp.where(row >= TILE + 2, pltpu.roll(below, ((TILE + 2 - 2 * t) * PITCH - FIRST_ROWS) % EXT, 1), p))
    return out


def stencil(p):
    near = pltpu.roll(p, 1, 1) + pltpu.roll(p, EXT - 1, 1)
    return 4.0 * p - (near + (pltpu.roll(p, PITCH, 1) + pltpu.roll(p, EXT - PITCH, 1)))


def smoothed(params):
    lane = lax.broadcasted_iota(jnp.int32, (COMPS, EXT), 1)
    y = lane // PITCH + (lax.axis_index("skyy") * TILE - 2)
    x = lane % PITCH + (lax.axis_index("skyx") * TILE - 2)
    ny, nx = lax.axis_size("skyy") * TILE, lax.axis_size("skyx") * TILE
    on_sky = (y >= 0) & (y < ny) & (x >= 0) & (x < nx)
    out = []
    for t, p in enumerate(params):
        first = jnp.where(on_sky, stencil(p), 0.0)
        out.append(p - (STEPS[t] * LAMS[t]) * stencil(first))
    return out


def five(v, flag=None):
    total = (v[0] + v[4]) + 4.0 * (v[1] + v[3]) + 6.0 * v[2]
    return total if flag is None else total * flag


def split(v):
    high = v.astype(jnp.bfloat16)
    return high, (v - high.astype(jnp.float32)).astype(jnp.bfloat16)


def wavelet_kernel(
    a_ref, m1, p1, m2, p2, x_ref, k_ref, own_ref, w_ref,
    o_0, swap_ref, near_ref, far_ref, ext_ref, rows_ref, y_ref,
):
    nch = x_ref.shape[1]
    tiles = (m2, m1, x_ref, p1, p2)
    iy, ix = lax.axis_index("skyy"), lax.axis_index("skyx")
    near = [iy + i for i in (-2, -1, 0, 1, 2)]
    flags = [jnp.where((i >= 0) & (i < lax.axis_size("skyy")), 1.0, 0.0) for i in near]

    lane_tiles = nch // LANES

    def row_pass(step, carry):
        sub = pl.ds(pl.multiple_of((step // lane_tiles) * 8, 8), 8)
        lane = pl.ds(pl.multiple_of((step % lane_tiles) * LANES, LANES), LANES)

        @functools.cache
        def value(level, at):
            tile = (at + 2 * TILE) // TILE
            if level == 0:
                if tile in (1, 2, 3):
                    start = pl.multiple_of(at % TILE * TILE + step // lane_tiles * 8, 8)
                    return tiles[tile][pl.ds(start, 8), lane]
                return tiles[tile][at % TILE - (BEYOND if tile == 0 else 0), sub, lane]
            gap = 2 ** (level - 1)
            taps = [value(level - 1, at + (t - 2) * gap) for t in range(5)]
            return five(taps, None if tile == 2 else flags[tile])

        reach = {1: 28, 2: 24, 3: 16, 4: 0}
        lag = {1: 2, 2: 6, 3: 14, 4: 30}
        for at in range(-30, TILE + 30):
            value(0, at)
            for level in range(1, LEVELS + 1):
                row = at - lag[level]
                if -reach[level] <= row < TILE + reach[level]:
                    got = value(level, row)
                    if 0 <= row < TILE:
                        rows_ref[level - 1, row, sub, lane] = got
        return carry

    lax.fori_loop(0, 2 * lane_tiles, row_pass, 0)

    half, quarter = nch // 2, nch // 4

    def product(v, index):
        blocks = [
            jnp.dot(v[:, at : at + half], w_ref[index, i], preferred_element_type=jnp.float32)
            for i, at in enumerate((0, quarter, half))
        ]
        return blocks

    for level in range(LEVELS):
        high, low = split(rows_ref[level].reshape(PIXELS, nch))
        terms = [product(high, level), product(low, level)]
        if level >= 2:
            terms.append(product(high, level + 2))
        first, middle, last = [functools.reduce(lambda a, b: a + b, v) for v in zip(*terms)]
        pieces = (
            first[:, :quarter],
            first[:, quarter:] + middle[:, :quarter],
            middle[:, quarter:] + last[:, :quarter],
            last[:, quarter:],
        )
        for i, piece in enumerate(pieces):
            lane = slice(i * quarter, (i + 1) * quarter)
            high, low = split(piece * a_ref[level + 1, :, lane])
            high = high.reshape(TILE, TILE, quarter)
            y_ref[:, level * TILE : (level + 1) * TILE, lane] = high
            at = (level + LEVELS) * TILE
            y_ref[:, at : at + TILE, lane] = low.reshape(TILE, TILE, quarter)
            if level >= 2:
                at = (level + 6) * TILE
                y_ref[:, at : at + TILE, lane] = high

    kind = jnp.where(ix == 0, 0, jnp.where(ix == lax.axis_size("skyx") - 1, 2, 1))
    odd = lax.rem(ix, 2)
    columns = k_ref[2 * kind + odd]

    def column_pass(row, carry):
        got = jnp.dot(columns, y_ref[row], preferred_element_type=jnp.float32)
        at = pl.ds(pl.multiple_of(row * TILE, TILE), TILE)
        at_more = pl.ds(pl.multiple_of(row * TILE + PIXELS, TILE), TILE)
        o_0[row] = got[:TILE] + a_ref[0] * x_ref[at]
        swap_ref[at] = got[TILE : 2 * TILE]
        swap_ref[at_more] = got[2 * TILE : 3 * TILE]
        near_ref[at] = got[3 * TILE : 4 * TILE]
        far_ref[at] = got[4 * TILE :]
        return carry

    lax.fori_loop(0, TILE, column_pass, 0, unroll=4)

    params = with_rows(own_ref, m1[PIXELS:, :], p1[PIXELS:, :])
    for t in range(3):
        ext_ref[t] = params[t]
    to_right, to_left = border_columns(ext_ref, TILE), border_columns(ext_ref, 2)
    swap_ref[2 * PIXELS : 2 * PIXELS + COMPS] = jnp.where(odd == 0, to_right, to_left)
    swap_ref[2 * PIXELS + COMPS :] = jnp.where(odd == 0, to_left, to_right)


def kept(x):
    return pltpu.with_memory_space_constraint(x, pltpu.VMEM)


def wavelet_parts(coeff, tiles, own, w, nch, length):
    k = jnp.asarray(scatter_matrices(length))
    vmem = pl.BlockSpec(memory_space=pltpu.VMEM)
    heights = (2 * (PIXELS + COMPS), PIXELS, PIXELS + COMPS)
    shapes = [(TILE, TILE, nch)] + [(n, nch) for n in heights] + [own.shape]
    return pl.pallas_call(
        wavelet_kernel,
        out_shape=[pltpu.VMEM(shape, jnp.float32) for shape in shapes],
        in_specs=[vmem] * 9,
        out_specs=[vmem] * 5,
        scratch_shapes=[
            pltpu.VMEM((LEVELS, TILE, TILE, nch), jnp.float32),
            pltpu.VMEM((TILE, 10 * TILE, nch), jnp.bfloat16),
        ],
        compiler_params=pltpu.CompilerParams(vmem_limit_bytes=VMEM_LIMIT),
        cost_estimate=pl.CostEstimate(flops=4_000_000_000, bytes_accessed=9_000_000, transcendentals=0),
        name="wavelet_parts",
    )(*[kept(x) for x in (coeff, *tiles, k, own, w)])


def add_kernel(near_ref, swapped_ref, out_ref):
    def body(row, carry):
        at = pl.ds(pl.multiple_of(row * TILE, TILE), TILE)
        more = pl.ds(pl.multiple_of(row * TILE + PIXELS, TILE), TILE)
        out_ref[at] = near_ref[at] + swapped_ref[more]
        return carry

    lax.fori_loop(0, TILE, body, 0, unroll=4)
    out_ref[PIXELS:, :] = swapped_ref[2 * PIXELS + COMPS :]


def outward(near, swapped):
    vmem = pl.BlockSpec(memory_space=pltpu.VMEM)
    return pl.pallas_call(
        add_kernel,
        out_shape=pltpu.VMEM((PIXELS + COMPS, near.shape[1]), jnp.float32),
        in_specs=[vmem] * 2,
        out_specs=vmem,
        compiler_params=pltpu.CompilerParams(vmem_limit_bytes=VMEM_LIMIT),
        cost_estimate=pl.CostEstimate(flops=100_000, bytes_accessed=1_500_000, transcendentals=0),
        name="outward",
    )(kept(near), kept(swapped))


def model_kernel(amp_ref, index_ref, spread_ref, w_hbm, model_ref, flat_ref, own_ref, w_ref, scale_ref, sem):
    load = pltpu.make_async_copy(w_hbm, w_ref, sem)
    load.start()
    nch, pixels = model_ref.shape
    own_ref[...] = jnp.zeros_like(own_ref)
    for t in range(3):
        for row in range(TILE):
            got = own_row(t, row, amp_ref, index_ref, spread_ref, nch)
            at = (row + 2) * PITCH + 2
            own_ref[t, :, at : at + TILE] = got
            flat_ref[t, :, row * TILE : (row + 1) * TILE] = got
    mu = flat_ref[1] * float(nch)
    inv = 1.0 / flat_ref[2]
    flat_ref[1] = mu
    flat_ref[2] = inv
    scale_ref[...] = (-0.5 * math.log2(math.e)) * inv * inv

    def body(step, carry):
        base = pl.multiple_of(step * 8, 8)
        chan = (lax.broadcasted_iota(jnp.int32, (8, pixels), 0) + base).astype(jnp.float32)
        total = jnp.zeros((8, pixels), jnp.float32)
        for k in range(COMPS):
            diff = chan - flat_ref[1, k : k + 1, :]
            bump = jnp.exp2(diff * diff * scale_ref[k : k + 1, :])
            total += flat_ref[0, k : k + 1, :] * bump
        model_ref[pl.ds(base, 8), :] = total
        return carry

    lax.fori_loop(0, nch // 8, body, 0, unroll=2)
    load.wait()


def model_of(amplitude, centre_index, spread, nch):
    w = jnp.asarray(channel_matrices(nch))
    vmem = pl.BlockSpec(memory_space=pltpu.VMEM)
    pixels = TILE * TILE
    return pl.pallas_call(
        model_kernel,
        out_shape=[
            pltpu.VMEM((nch, pixels), jnp.float32),
            pltpu.VMEM((3, COMPS, pixels), jnp.float32),
            pltpu.VMEM((3, COMPS, EXT), jnp.float32),
            pltpu.VMEM(w.shape, w.dtype),
        ],
        in_specs=[vmem] * 3 + [pl.BlockSpec(memory_space=pl.ANY)],
        out_specs=[vmem] * 4,
        scratch_shapes=[pltpu.VMEM((COMPS, pixels), jnp.float32), pltpu.SemaphoreType.DMA],
        compiler_params=pltpu.CompilerParams(vmem_limit_bytes=VMEM_LIMIT),
        cost_estimate=pl.CostEstimate(flops=10_000_000, bytes_accessed=1_000_000, transcendentals=1_100_000),
        name="gaussian_model",
    )(amplitude, centre_index, spread, pltpu.with_memory_space_constraint(w, pltpu.HBM))


def step_kernel(
    o_0, swapped_ref, far_ref, near_ref, model_ref, flat_ref, ext_ref,
    den_hbm, fit_ref, den_ref, r_ref, sem,
):
    nch, pixels = model_ref.shape
    rows = LANES // TILE
    parts = pixels // LANES
    copies = []
    inner, outer = swapped_ref[2 * PIXELS : 2 * PIXELS + COMPS], near_ref[PIXELS:, :]
    even = lax.rem(lax.axis_index("skyx"), 2) == 0
    left, right = jnp.where(even, outer, inner), jnp.where(even, inner, outer)
    bases = smoothed(with_columns(ext_ref, left, right))
    for part in range(parts):
        at = slice(part * rows, (part + 1) * rows)
        for row in range(part * rows, (part + 1) * rows):
            flat = slice(row * TILE, (row + 1) * TILE)
            den_ref[row] = (o_0[row] + swapped_ref[flat]) + (far_ref[flat] + near_ref[flat])
        copies.append(pltpu.make_async_copy(den_ref.at[at], den_hbm.at[at], sem.at[part]))
        copies[-1].start()

    shape = (COMPS, rows, LANES)
    own_lanes = lax.broadcasted_iota(jnp.int32, shape, 2) // TILE == lax.broadcasted_iota(jnp.int32, shape, 1)
    for part in range(parts):
        block = den_ref[part * rows : (part + 1) * rows].reshape(LANES, nch)
        at = slice(part * LANES, (part + 1) * LANES)
        r_ref[:, at] = model_ref[:, at] - block.T

    for part in range(parts):
        at = slice(part * LANES, (part + 1) * LANES)
        sums = [[] for _ in range(3)]
        for first in range(0, COMPS, 4):
            chosen = range(first, first + 4)
            mus = [jnp.broadcast_to(flat_ref[1, k : k + 1, at], (8, LANES)) for k in chosen]
            inv = [jnp.broadcast_to(flat_ref[2, k : k + 1, at], (8, LANES)) for k in chosen]
            scales = [(-0.5 * math.log2(math.e)) * v * v for v in inv]

            def body(step, carry):
                base = pl.multiple_of(step * 8, 8)
                chan = (lax.broadcasted_iota(jnp.int32, (8, LANES), 0) + base).astype(jnp.float32)
                r = r_ref[pl.ds(base, 8), at]
                out = []
                for mu, scale, (a, b, c) in zip(mus, scales, carry):
                    diff = chan - mu
                    one = r * jnp.exp2(diff * diff * scale)
                    two = one * diff
                    out.append((a + one, b + two, c + two * diff))
                return tuple(out)

            zero = jnp.zeros((8, LANES), jnp.float32)
            done = lax.fori_loop(0, nch // 8, body, ((zero,) * 3,) * 4, unroll=8)
            for four in done:
                for t in range(3):
                    sums[t].append(jnp.sum(four[t], axis=0, keepdims=True))
        amp = flat_ref[0, :, at]
        inv = flat_ref[2, :, at]
        slope = amp * inv * inv
        grads = (
            jnp.concatenate(sums[0], axis=0) * (1.0 / nch),
            jnp.concatenate(sums[1], axis=0) * slope,
            jnp.concatenate(sums[2], axis=0) * (slope * inv * (1.0 / nch)),
        )
        for t in range(3):
            lanes = [(part * rows + i + 2) * PITCH + 2 for i in range(rows)]
            base = jnp.concatenate([bases[t][:, lane : lane + TILE] for lane in lanes], axis=1)
            new = base - STEPS[t] * grads[t]
            spread_out = jnp.where(own_lanes, jnp.broadcast_to(new[:, None, :], own_lanes.shape), 0.0)
            for shift in (LANES // 2, LANES // 4, LANES // 8):
                spread_out = spread_out + pltpu.roll(spread_out, shift, 2)
            fit_ref[t, :, part * rows : (part + 1) * rows, :] = spread_out[:, :, :TILE]

    for copy in copies:
        copy.wait()


def gradient_step(parts, model, flat, ext):
    vmem = pl.BlockSpec(memory_space=pltpu.VMEM)
    shape = parts[0].shape
    return pl.pallas_call(
        step_kernel,
        out_shape=[
            jax.ShapeDtypeStruct(shape, jnp.float32),
            jax.ShapeDtypeStruct((3, COMPS, TILE, TILE), jnp.float32),
        ],
        in_specs=[vmem] * 7,
        out_specs=[pl.BlockSpec(memory_space=pl.ANY), vmem],
        scratch_shapes=[
            pltpu.VMEM(shape, jnp.float32),
            pltpu.VMEM(model.shape, jnp.float32),
            pltpu.SemaphoreType.DMA((2,)),
        ],
        compiler_params=pltpu.CompilerParams(vmem_limit_bytes=VMEM_LIMIT),
        cost_estimate=pl.CostEstimate(flops=15_000_000, bytes_accessed=4_000_000, transcendentals=1_100_000),
        name="gradient_step",
    )(*[kept(x) for x in (*parts, model, flat, ext)])


def on_device(cube, level_table, level_index, amplitude, centre_index, spread):
    nch = cube.shape[2]
    size = lax.axis_size("skyx")
    partner = [(i, i ^ 1) for i in range(size)]

    tile = packed(cube.reshape(PIXELS, nch), amplitude, centre_index, spread)
    up1, down1 = sent(tile, "skyy", 1), sent(tile, "skyy", -1)
    up2, down2 = sent(cube[BEYOND:], "skyy", 2), sent(cube[:-BEYOND], "skyy", -2)

    entries = jnp.arange(level_table.shape[0], dtype=jnp.int32)
    picks = (level_index[:, :, None] == entries).astype(jnp.float32)
    weight = jnp.sum(picks * level_table, axis=2)
    one = jnp.ones((1, nch), jnp.float32)
    coeff = jnp.concatenate([weight, one]) - jnp.concatenate([0.0 * one, weight])
    scale = jnp.array([16.0 ** (-3 * j) for j in range(LEVELS + 1)], jnp.float32)
    coeff = (coeff * scale[:, None])[:, None, :]
    model, flat, own, w = model_of(amplitude, centre_index, spread, nch)
    o_0, swap, near, far, ext = wavelet_parts(coeff, (up1, down1, up2, down2, tile), own, w, nch, size * TILE)

    swapped = lax.ppermute(swap, "skyx", partner)
    far = away(far, "skyx", 2)
    near = away(outward(near, swapped), "skyx", -2)
    return gradient_step((o_0, swapped, far, near), model, flat, ext)


def solution(mesh):
    placed = (
        P("skyy", "skyx", None),
        P(),
        P(),
        P(None, "skyy", "skyx"),
        P(None, "skyy", "skyx"),
        P(None, "skyy", "skyx"),
    )
    return jax.shard_map(
        on_device,
        mesh=mesh,
        in_specs=placed,
        out_specs=(P("skyy", "skyx", None), P(None, None, "skyy", "skyx")),
        check_vma=False,
    )
```

```python
import functools
import math

import jax
import jax.numpy as jnp
import numpy as np
from jax import lax
from jax.experimental import pallas as pl
from jax.experimental.pallas import tpu as pltpu
from jax.sharding import PartitionSpec as P

TILE = 16
LEVELS = 4
COMPS = 8
LANES = 128
TAPS = (1, 4, 6, 4, 1)
BEYOND = 2
VMEM_LIMIT = 20 * 1024 * 1024
ROLES = ((3, 1, 0, 2, 4), (1, 3, 4, 2, 0))
PIXELS = TILE * TILE
PITCH = TILE
EXT = 384
OWN = 2 * PITCH
FIRST_ROWS = 128
STEPS = (0.5, 0.002, 2.0)
LAMS = (0.2, 0.5, 0.05)


def blur_matrix(length, gap):
    out = np.zeros((length, length), np.float64)
    for tap, factor in enumerate(TAPS):
        offset = (tap - 2) * gap
        for i in range(max(0, -offset), min(length, length - offset)):
            out[i, i + offset] = factor
    return out


def composites(length):
    made, now = [], np.eye(length)
    for level in range(LEVELS):
        now = blur_matrix(length, 2**level) @ now
        made.append(now)
    return made


def halves(matrix):
    bf16 = jnp.bfloat16
    high = np.asarray(matrix, np.float32).astype(bf16)
    low = (np.asarray(matrix, np.float32) - high.astype(np.float32)).astype(bf16)
    return high, low


def channel_matrices(nch):
    parts = [halves(m.T) for m in composites(nch)]
    half, quarter = nch // 2, nch // 4
    out = []
    for whole in [p[0] for p in parts] + [p[1] for p in parts[2:]]:
        across = whole[quarter : quarter + half, quarter : quarter + half].copy()
        across[:quarter, :quarter] = 0
        across[quarter:, quarter:] = 0
        out.append(np.stack([whole[:half, :half], across, whole[half:, half:]]))
    return np.stack(out)


def scatter_matrices(length):
    whole = composites(length)
    kinds = []
    for start in (0, TILE * (length // TILE // 2), length - TILE):
        parts = []
        for m in whole:
            block = np.zeros((5 * TILE, TILE))
            for k in range(5 * TILE):
                at = start - 2 * TILE + k
                if 0 <= at < length:
                    block[k] = m[at, start : start + TILE]
            parts.append(halves(block))
        high = np.concatenate([p[0] for p in parts], axis=1)
        low = np.concatenate([p[1] for p in parts[2:]], axis=1)
        columns = np.concatenate([high, high, low], axis=1).reshape(5, TILE, -1)
        for order in ROLES:
            kinds.append(np.concatenate([columns[i] for i in order]))
    return np.stack(kinds)


def sent(values, axis, by):
    size = lax.axis_size(axis)
    if by > 0:
        pairs = [(i, i + by) for i in range(size - by)]
    else:
        pairs = [(i, i + by) for i in range(-by, size)]
    return lax.ppermute(values, axis, pairs)


def away(values, axis, by):
    size = lax.axis_size(axis)
    pairs = [(i, i + by if i % 2 else i - by) for i in range(size)]
    return lax.ppermute(values, axis, [(i, j) for i, j in pairs if 0 <= j < size])


def own_row(t, row, amp_ref, index_ref, spread_ref, nch):
    if t == 0:
        return amp_ref[:, row, :]
    if t == 1:
        return (index_ref[:, row, :].astype(jnp.float32) + 0.5) * (1.0 / nch)
    return spread_ref[:, row, :]


def pack_kernel(cube_hbm, amp_hbm, index_hbm, spread_hbm, out_ref, amp_ref, index_ref, spread_ref, sem):
    pairs = ((amp_hbm, amp_ref), (index_hbm, index_ref), (spread_hbm, spread_ref), (cube_hbm, out_ref.at[0:PIXELS]))
    copies = [pltpu.make_async_copy(a, b, sem.at[i]) for i, (a, b) in enumerate(pairs)]
    for copy in copies:
        copy.start()
    nch = cube_hbm.shape[1]
    out_ref[PIXELS:, :] = jnp.zeros((COMPS, nch), jnp.float32)
    for copy in copies[:3]:
        copy.wait()
    for start, first in ((0, TILE - 2), (FIRST_ROWS, 0)):
        for t in range(3):
            for r in range(2):
                lane = start + (2 * t + r) * PITCH
                got = own_row(t, first + r, amp_ref, index_ref, spread_ref, nch)
                out_ref[PIXELS:, lane : lane + TILE] = got
    copies[3].wait()


def packed(cube, amplitude, centre_index, spread):
    hbm = [pltpu.with_memory_space_constraint(v, pltpu.HBM) for v in (cube, amplitude, centre_index, spread)]
    return pl.pallas_call(
        pack_kernel,
        out_shape=pltpu.VMEM((PIXELS + COMPS, cube.shape[1]), jnp.float32),
        in_specs=[pl.BlockSpec(memory_space=pl.ANY)] * 4,
        out_specs=pl.BlockSpec(memory_space=pltpu.VMEM),
        scratch_shapes=[pltpu.VMEM(v.shape, v.dtype) for v in hbm[1:]] + [pltpu.SemaphoreType.DMA((4,))],
        compiler_params=pltpu.CompilerParams(vmem_limit_bytes=VMEM_LIMIT),
        cost_estimate=pl.CostEstimate(flops=1000, bytes_accessed=1_000_000, transcendentals=0),
        name="pack",
    )(*hbm)


def border_columns(ext_ref, shift):
    lane = lax.broadcasted_iota(jnp.int32, (COMPS, EXT), 1) % PITCH
    total = jnp.zeros((COMPS, EXT), jnp.float32)
    for t in range(3):
        moved = pltpu.roll(ext_ref[t], (2 * t - shift) % EXT, 1)
        total = jnp.where((lane >= 2 * t) & (lane < 2 * t + 2), moved, total)
    return total


def with_rows(own, above, below):
    row = lax.broadcasted_iota(jnp.int32, (COMPS, EXT), 1) // PITCH
    out = []
    for t in range(3):
        p = jnp.where(row < 2, pltpu.roll(above, (EXT - 2 * t * PITCH) % EXT, 1), own[t])
        out.append(jnp.where(row >= TILE + 2, pltpu.roll(below, ((TILE + 2 - 2 * t) * PITCH - FIRST_ROWS) % EXT, 1), p))
    return out


def up_and_down(p):
    return pltpu.roll(p, PITCH, 1) + pltpu.roll(p, EXT - PITCH, 1)


def smoothed(params, left, right):
    lane = lax.broadcasted_iota(jnp.int32, (COMPS, EXT), 1)
    column = lane % PITCH
    at_left, at_right = column == 0, column == TILE - 1
    y = lane // PITCH + (lax.axis_index("skyy") * TILE - 2)
    on_sky = (y >= 0) & (y < lax.axis_size("skyy") * TILE)
    ix = lax.axis_index("skyx")
    beside = on_sky & ((at_left & (ix > 0)) | (at_right & (ix < lax.axis_size("skyx") - 1)))

    def laplacian(p, side):
        before = jnp.where(at_left, side, pltpu.roll(p, 1, 1))
        after = jnp.where(at_right, side, pltpu.roll(p, EXT - 1, 1))
        return 4.0 * p - ((before + after) + up_and_down(p))

    out = []
    for t, p in enumerate(params):
        lefts = [pltpu.roll(left, (EXT - 2 * t - 1 + i) % EXT, 1) for i in range(2)]
        rights = [pltpu.roll(right, (TILE - 1 - 2 * t - i) % EXT, 1) for i in range(2)]
        one, two = [jnp.where(at_left, a, b) for a, b in zip(lefts, rights)]
        first = jnp.where(on_sky, laplacian(p, one), 0.0)
        first_beside = jnp.where(beside, 4.0 * one - ((two + p) + up_and_down(one)), 0.0)
        new = p - (STEPS[t] * LAMS[t]) * laplacian(first, first_beside)
        out.append(pltpu.roll(new, EXT - OWN, 1)[:, :PIXELS])
    return out


def five(v, flag=None):
    total = (v[0] + v[4]) + 4.0 * (v[1] + v[3]) + 6.0 * v[2]
    return total if flag is None else total * flag


def split(v):
    high = v.astype(jnp.bfloat16)
    return high, (v - high.astype(jnp.float32)).astype(jnp.bfloat16)


def column_kind():
    ix = lax.axis_index("skyx")
    kind = jnp.where(ix == 0, 0, jnp.where(ix == lax.axis_size("skyx") - 1, 2, 1))
    return 2 * kind + lax.rem(ix, 2)


def own_kernel(a_ref, x_ref, k_ref, y_ref, _, o_0):
    columns = k_ref[column_kind(), 3 * TILE : 4 * TILE]

    def column_pass(row, carry):
        got = jnp.dot(columns, y_ref[row], preferred_element_type=jnp.float32)
        o_0[row] = got + a_ref[0] * x_ref[pl.ds(pl.multiple_of(row * TILE, TILE), TILE)]
        return carry

    lax.fori_loop(0, TILE, column_pass, 0, unroll=4)


def own_part(coeff, tile, k, y, after, nch):
    vmem = pl.BlockSpec(memory_space=pltpu.VMEM)
    return pl.pallas_call(
        own_kernel,
        out_shape=pltpu.VMEM((TILE, TILE, nch), jnp.float32),
        in_specs=[vmem] * 4 + [pl.BlockSpec(memory_space=pl.ANY)],
        out_specs=vmem,
        compiler_params=pltpu.CompilerParams(vmem_limit_bytes=VMEM_LIMIT),
        cost_estimate=pl.CostEstimate(flops=100_000_000, bytes_accessed=500_000, transcendentals=0),
        name="own_part",
    )(*[kept(x) for x in (coeff, tile, k, y, after)])


def wavelet_kernel(
    a_ref, m1, p1, m2, p2, x_ref, k_ref, own_ref, w_ref,
    swap_ref, far_ref, ext_ref, y_ref, rows_ref,
):
    nch = x_ref.shape[1]
    tiles = (m2, m1, x_ref, p1, p2)
    iy, ix = lax.axis_index("skyy"), lax.axis_index("skyx")
    near = [iy + i for i in (-2, -1, 0, 1, 2)]
    flags = [jnp.where((i >= 0) & (i < lax.axis_size("skyy")), 1.0, 0.0) for i in near]

    lane_tiles = nch // LANES

    def row_pass(step, carry):
        sub = pl.ds(pl.multiple_of((step // lane_tiles) * 8, 8), 8)
        lane = pl.ds(pl.multiple_of((step % lane_tiles) * LANES, LANES), LANES)

        @functools.cache
        def value(level, at):
            tile = (at + 2 * TILE) // TILE
            if level == 0:
                if tile in (1, 2, 3):
                    start = pl.multiple_of(at % TILE * TILE + step // lane_tiles * 8, 8)
                    return tiles[tile][pl.ds(start, 8), lane]
                return tiles[tile][at % TILE - (BEYOND if tile == 0 else 0), sub, lane]
            gap = 2 ** (level - 1)
            taps = [value(level - 1, at + (t - 2) * gap) for t in range(5)]
            return five(taps, None if tile == 2 else flags[tile])

        reach = {1: 28, 2: 24, 3: 16, 4: 0}
        lag = {1: 2, 2: 6, 3: 14, 4: 30}
        for at in range(-30, TILE + 30):
            value(0, at)
            for level in range(1, LEVELS + 1):
                row = at - lag[level]
                if -reach[level] <= row < TILE + reach[level]:
                    got = value(level, row)
                    if 0 <= row < TILE:
                        rows_ref[level - 1, row, sub, lane] = got
        return carry

    lax.fori_loop(0, 2 * lane_tiles, row_pass, 0)

    half, quarter = nch // 2, nch // 4

    def product(v, index):
        blocks = [
            jnp.dot(v[:, at : at + half], w_ref[index, i], preferred_element_type=jnp.float32)
            for i, at in enumerate((0, quarter, half))
        ]
        return blocks

    for level in range(LEVELS):
        high, low = split(rows_ref[level].reshape(PIXELS, nch))
        terms = [product(high, level), product(low, level)]
        if level >= 2:
            terms.append(product(high, level + 2))
        first, middle, last = [functools.reduce(lambda a, b: a + b, v) for v in zip(*terms)]
        pieces = (
            first[:, :quarter],
            first[:, quarter:] + middle[:, :quarter],
            middle[:, quarter:] + last[:, :quarter],
            last[:, quarter:],
        )
        for i, piece in enumerate(pieces):
            lane = slice(i * quarter, (i + 1) * quarter)
            high, low = split(piece * a_ref[level + 1, :, lane])
            high = high.reshape(TILE, TILE, quarter)
            y_ref[:, level * TILE : (level + 1) * TILE, lane] = high
            at = (level + LEVELS) * TILE
            y_ref[:, at : at + TILE, lane] = low.reshape(TILE, TILE, quarter)
            if level >= 2:
                at = (level + 6) * TILE
                y_ref[:, at : at + TILE, lane] = high

    odd = lax.rem(ix, 2)
    columns = k_ref[column_kind(), : 3 * TILE]

    def column_pass(row, carry):
        got = jnp.dot(columns, y_ref[row], preferred_element_type=jnp.float32)
        at = pl.ds(pl.multiple_of(row * TILE, TILE), TILE)
        at_more = pl.ds(pl.multiple_of(row * TILE + PIXELS, TILE), TILE)
        swap_ref[at] = got[:TILE]
        swap_ref[at_more] = got[TILE : 2 * TILE]
        far_ref[at] = got[2 * TILE :]
        return carry

    lax.fori_loop(0, TILE, column_pass, 0, unroll=4)

    params = with_rows(own_ref, m1[PIXELS:, :EXT], p1[PIXELS:, :EXT])
    for t in range(3):
        ext_ref[t] = params[t]
    to_right, to_left = border_columns(ext_ref, TILE - 2), border_columns(ext_ref, 0)
    swap_ref[2 * PIXELS : 2 * PIXELS + COMPS, :EXT] = jnp.where(odd == 0, to_right, to_left)
    swap_ref[2 * PIXELS + COMPS :, :EXT] = jnp.where(odd == 0, to_left, to_right)


def kept(x):
    return pltpu.with_memory_space_constraint(x, pltpu.VMEM)


def wavelet_parts(coeff, tiles, k, own, w, nch):
    vmem = pl.BlockSpec(memory_space=pltpu.VMEM)
    shapes = [(2 * (PIXELS + COMPS), nch), (PIXELS + COMPS, nch), own.shape]
    outs = [pltpu.VMEM(shape, jnp.float32) for shape in shapes]
    return pl.pallas_call(
        wavelet_kernel,
        out_shape=outs + [pltpu.VMEM((TILE, 10 * TILE, nch), jnp.bfloat16)],
        in_specs=[vmem] * 9,
        out_specs=[vmem] * 4,
        scratch_shapes=[pltpu.VMEM((LEVELS, TILE, TILE, nch), jnp.float32)],
        compiler_params=pltpu.CompilerParams(vmem_limit_bytes=VMEM_LIMIT),
        cost_estimate=pl.CostEstimate(flops=4_000_000_000, bytes_accessed=9_000_000, transcendentals=0),
        name="wavelet_parts",
    )(*[kept(x) for x in (coeff, *tiles, k, own, w)])


def outward_kernel(k_ref, y_ref, swapped_ref, out_ref):
    columns = k_ref[column_kind(), 4 * TILE :]

    def column_pass(row, carry):
        got = jnp.dot(columns, y_ref[row], preferred_element_type=jnp.float32)
        at = pl.ds(pl.multiple_of(row * TILE, TILE), TILE)
        more = pl.ds(pl.multiple_of(row * TILE + PIXELS, TILE), TILE)
        out_ref[at] = got + swapped_ref[more]
        return carry

    lax.fori_loop(0, TILE, column_pass, 0, unroll=4)
    out_ref[PIXELS:, :] = swapped_ref[2 * PIXELS + COMPS :]


def outward(k, y, swapped):
    vmem = pl.BlockSpec(memory_space=pltpu.VMEM)
    return pl.pallas_call(
        outward_kernel,
        out_shape=pltpu.VMEM((PIXELS + COMPS, swapped.shape[1]), jnp.float32),
        in_specs=[vmem] * 3,
        out_specs=vmem,
        compiler_params=pltpu.CompilerParams(vmem_limit_bytes=VMEM_LIMIT),
        cost_estimate=pl.CostEstimate(flops=100_000, bytes_accessed=1_500_000, transcendentals=0),
        name="outward",
    )(*[kept(x) for x in (k, y, swapped)])


def model_kernel(amp_ref, index_ref, spread_ref, w_hbm, model_ref, flat_ref, own_ref, w_ref, bump_ref, scale_ref, sem):
    load = pltpu.make_async_copy(w_hbm, w_ref, sem)
    load.start()
    nch, pixels = model_ref.shape
    own_ref[...] = jnp.zeros_like(own_ref)
    for t in range(3):
        for row in range(TILE):
            got = own_row(t, row, amp_ref, index_ref, spread_ref, nch)
            at = (row + 2) * PITCH
            own_ref[t, :, at : at + TILE] = got
            flat_ref[t, :, row * TILE : (row + 1) * TILE] = got
    mu = flat_ref[1] * float(nch)
    inv = 1.0 / flat_ref[2]
    flat_ref[1] = mu
    flat_ref[2] = inv
    scale_ref[...] = (-0.5 * math.log2(math.e)) * inv * inv

    def body(step, carry):
        base = pl.multiple_of(step * 8, 8)
        chan = (lax.broadcasted_iota(jnp.int32, (8, pixels), 0) + base).astype(jnp.float32)
        total = jnp.zeros((8, pixels), jnp.float32)
        for k in range(COMPS):
            diff = chan - flat_ref[1, k : k + 1, :]
            bump = jnp.exp2(diff * diff * scale_ref[k : k + 1, :])
            bump_ref[k, pl.ds(base, 8), :] = bump
            total += flat_ref[0, k : k + 1, :] * bump
        model_ref[pl.ds(base, 8), :] = total
        return carry

    lax.fori_loop(0, nch // 8, body, 0, unroll=2)
    load.wait()


def model_of(amplitude, centre_index, spread, nch):
    w = jnp.asarray(channel_matrices(nch))
    vmem = pl.BlockSpec(memory_space=pltpu.VMEM)
    pixels = TILE * TILE
    return pl.pallas_call(
        model_kernel,
        out_shape=[
            pltpu.VMEM((nch, pixels), jnp.float32),
            pltpu.VMEM((3, COMPS, pixels), jnp.float32),
            pltpu.VMEM((3, COMPS, EXT), jnp.float32),
            pltpu.VMEM(w.shape, w.dtype),
            pltpu.VMEM((COMPS, nch, pixels), jnp.float32),
        ],
        in_specs=[vmem] * 3 + [pl.BlockSpec(memory_space=pl.ANY)],
        out_specs=[vmem] * 5,
        scratch_shapes=[pltpu.VMEM((COMPS, pixels), jnp.float32), pltpu.SemaphoreType.DMA],
        compiler_params=pltpu.CompilerParams(vmem_limit_bytes=VMEM_LIMIT),
        cost_estimate=pl.CostEstimate(flops=10_000_000, bytes_accessed=1_000_000, transcendentals=1_100_000),
        name="gaussian_model",
    )(amplitude, centre_index, spread, pltpu.with_memory_space_constraint(w, pltpu.HBM))


def step_kernel(
    o_0, swapped_ref, far_ref, near_ref, model_ref, bump_ref, flat_ref, ext_ref,
    den_hbm, fit_ref, den_ref, r_ref, sem,
):
    nch, pixels = model_ref.shape
    rows = LANES // TILE
    parts = pixels // LANES
    copies = []
    inner, outer = swapped_ref[2 * PIXELS : 2 * PIXELS + COMPS, :EXT], near_ref[PIXELS:, :EXT]
    even = lax.rem(lax.axis_index("skyx"), 2) == 0
    left, right = jnp.where(even, outer, inner), jnp.where(even, inner, outer)
    bases = smoothed([ext_ref[t] for t in range(3)], left, right)
    for part in range(parts):
        at = slice(part * rows, (part + 1) * rows)
        for row in range(part * rows, (part + 1) * rows):
            flat = slice(row * TILE, (row + 1) * TILE)
            den_ref[row] = (o_0[row] + swapped_ref[flat]) + (far_ref[flat] + near_ref[flat])
        copies.append(pltpu.make_async_copy(den_ref.at[at], den_hbm.at[at], sem.at[part]))
        copies[-1].start()

    shape = (COMPS, rows, LANES)
    own_lanes = lax.broadcasted_iota(jnp.int32, shape, 2) // TILE == lax.broadcasted_iota(jnp.int32, shape, 1)
    for part in range(parts):
        block = den_ref[part * rows : (part + 1) * rows].reshape(LANES, nch)
        at = slice(part * LANES, (part + 1) * LANES)
        r_ref[:, at] = model_ref[:, at] - block.T

    for part in range(parts):
        at = slice(part * LANES, (part + 1) * LANES)
        sums = [[] for _ in range(3)]
        for first in range(0, COMPS, 4):
            chosen = range(first, first + 4)
            mus = [jnp.broadcast_to(flat_ref[1, k : k + 1, at], (8, LANES)) for k in chosen]

            def body(step, carry):
                base = pl.multiple_of(step * 8, 8)
                chan = (lax.broadcasted_iota(jnp.int32, (8, LANES), 0) + base).astype(jnp.float32)
                r = r_ref[pl.ds(base, 8), at]
                out = []
                for k, mu, (a, b, c) in zip(chosen, mus, carry):
                    diff = chan - mu
                    one = r * bump_ref[k, pl.ds(base, 8), at]
                    two = one * diff
                    out.append((a + one, b + two, c + two * diff))
                return tuple(out)

            zero = jnp.zeros((8, LANES), jnp.float32)
            done = lax.fori_loop(0, nch // 8, body, ((zero,) * 3,) * 4, unroll=8)
            for four in done:
                for t in range(3):
                    sums[t].append(jnp.sum(four[t], axis=0, keepdims=True))
        amp = flat_ref[0, :, at]
        inv = flat_ref[2, :, at]
        slope = amp * inv * inv
        grads = (
            jnp.concatenate(sums[0], axis=0) * (1.0 / nch),
            jnp.concatenate(sums[1], axis=0) * slope,
            jnp.concatenate(sums[2], axis=0) * (slope * inv * (1.0 / nch)),
        )
        for t in range(3):
            new = bases[t][:, at] - STEPS[t] * grads[t]
            spread_out = jnp.where(own_lanes, jnp.broadcast_to(new[:, None, :], own_lanes.shape), 0.0)
            for shift in (LANES // 2, LANES // 4, LANES // 8):
                spread_out = spread_out + pltpu.roll(spread_out, shift, 2)
            fit_ref[t, :, part * rows : (part + 1) * rows, :] = spread_out[:, :, :TILE]

    for copy in copies:
        copy.wait()


def gradient_step(parts, model, bump, flat, ext):
    vmem = pl.BlockSpec(memory_space=pltpu.VMEM)
    shape = parts[0].shape
    return pl.pallas_call(
        step_kernel,
        out_shape=[
            jax.ShapeDtypeStruct(shape, jnp.float32),
            jax.ShapeDtypeStruct((3, COMPS, TILE, TILE), jnp.float32),
        ],
        in_specs=[vmem] * 8,
        out_specs=[pl.BlockSpec(memory_space=pl.ANY), vmem],
        scratch_shapes=[
            pltpu.VMEM(shape, jnp.float32),
            pltpu.VMEM(model.shape, jnp.float32),
            pltpu.SemaphoreType.DMA((2,)),
        ],
        compiler_params=pltpu.CompilerParams(vmem_limit_bytes=VMEM_LIMIT),
        cost_estimate=pl.CostEstimate(flops=15_000_000, bytes_accessed=4_000_000, transcendentals=1_100_000),
        name="gradient_step",
    )(*[kept(x) for x in (*parts, model, bump, flat, ext)])


def on_device(cube, level_table, level_index, amplitude, centre_index, spread):
    nch = cube.shape[2]
    size = lax.axis_size("skyx")
    partner = [(i, i ^ 1) for i in range(size)]

    tile = packed(cube.reshape(PIXELS, nch), amplitude, centre_index, spread)
    up1, down1 = sent(tile, "skyy", 1), sent(tile, "skyy", -1)
    up2, down2 = sent(cube[BEYOND:], "skyy", 2), sent(cube[:-BEYOND], "skyy", -2)

    entries = jnp.arange(level_table.shape[0], dtype=jnp.int32)
    picks = (level_index[:, :, None] == entries).astype(jnp.float32)
    weight = jnp.sum(picks * level_table, axis=2)
    one = jnp.ones((1, nch), jnp.float32)
    coeff = jnp.concatenate([weight, one]) - jnp.concatenate([0.0 * one, weight])
    scale = jnp.array([16.0 ** (-3 * j) for j in range(LEVELS + 1)], jnp.float32)
    coeff = (coeff * scale[:, None])[:, None, :]
    model, flat, own, w, bump = model_of(amplitude, centre_index, spread, nch)
    k = jnp.asarray(scatter_matrices(size * TILE))
    swap, far, ext, y = wavelet_parts(coeff, (up1, down1, up2, down2, tile), k, own, w, nch)

    swapped = lax.ppermute(swap, "skyx", partner)
    far = away(far, "skyx", 2)
    total = outward(k, y, swapped)
    near = away(total, "skyx", -2)
    o_0 = own_part(coeff, tile, k, y, total, nch)
    return gradient_step((o_0, swapped, far, near), model, bump, flat, ext)


def solution(mesh):
    placed = (
        P("skyy", "skyx", None),
        P(),
        P(),
        P(None, "skyy", "skyx"),
        P(None, "skyy", "skyx"),
        P(None, "skyy", "skyx"),
    )
    return jax.shard_map(
        on_device,
        mesh=mesh,
        in_specs=placed,
        out_specs=(P("skyy", "skyx", None), P(None, None, "skyy", "skyx")),
        check_vma=False,
    )
```

```python
import functools
import math

import jax
import jax.numpy as jnp
import numpy as np
from jax import lax
from jax.experimental import pallas as pl
from jax.experimental.pallas import tpu as pltpu
from jax.sharding import PartitionSpec as P

TILE = 16
LEVELS = 4
COMPS = 8
LANES = 128
TAPS = (1, 4, 6, 4, 1)
BEYOND = 2
VMEM_LIMIT = 20 * 1024 * 1024
ROLES = ((3, 1, 0, 2, 4), (1, 3, 4, 2, 0))
PIXELS = TILE * TILE
PITCH = TILE
EXT = 384
OWN = 2 * PITCH
FIRST_ROWS = 128
STEPS = (0.5, 0.002, 2.0)
LAMS = (0.2, 0.5, 0.05)


def blur_matrix(length, gap):
    out = np.zeros((length, length), np.float64)
    for tap, factor in enumerate(TAPS):
        offset = (tap - 2) * gap
        for i in range(max(0, -offset), min(length, length - offset)):
            out[i, i + offset] = factor
    return out


def composites(length):
    made, now = [], np.eye(length)
    for level in range(LEVELS):
        now = blur_matrix(length, 2**level) @ now
        made.append(now)
    return made


def halves(matrix):
    bf16 = jnp.bfloat16
    high = np.asarray(matrix, np.float32).astype(bf16)
    low = (np.asarray(matrix, np.float32) - high.astype(np.float32)).astype(bf16)
    return high, low


def channel_matrices(nch):
    parts = [halves(m.T) for m in composites(nch)]
    half, quarter = nch // 2, nch // 4
    out = []
    for whole in [p[0] for p in parts] + [p[1] for p in parts[2:]]:
        across = whole[quarter : quarter + half, quarter : quarter + half].copy()
        across[:quarter, :quarter] = 0
        across[quarter:, quarter:] = 0
        out.append(np.stack([whole[:half, :half], across, whole[half:, half:]]))
    return np.stack(out)


def scatter_matrices(length):
    whole = composites(length)
    kinds = []
    for start in (0, TILE * (length // TILE // 2), length - TILE):
        parts = []
        for m in whole:
            block = np.zeros((5 * TILE, TILE))
            for k in range(5 * TILE):
                at = start - 2 * TILE + k
                if 0 <= at < length:
                    block[k] = m[at, start : start + TILE]
            parts.append(halves(block))
        high = np.concatenate([p[0] for p in parts], axis=1)
        low = np.concatenate([p[1] for p in parts[2:]], axis=1)
        columns = np.concatenate([high, high, low], axis=1).reshape(5, TILE, -1)
        for order in ROLES:
            kinds.append(np.concatenate([columns[i] for i in order]))
    return np.stack(kinds)


def sent(values, axis, by):
    size = lax.axis_size(axis)
    if by > 0:
        pairs = [(i, i + by) for i in range(size - by)]
    else:
        pairs = [(i, i + by) for i in range(-by, size)]
    return lax.ppermute(values, axis, pairs)


def away(values, axis, by):
    size = lax.axis_size(axis)
    pairs = [(i, i + by if i % 2 else i - by) for i in range(size)]
    return lax.ppermute(values, axis, [(i, j) for i, j in pairs if 0 <= j < size])


def own_row(t, row, amp_ref, index_ref, spread_ref, nch):
    if t == 0:
        return amp_ref[:, row, :]
    if t == 1:
        return (index_ref[:, row, :].astype(jnp.float32) + 0.5) * (1.0 / nch)
    return spread_ref[:, row, :]


def pack_kernel(cube_hbm, amp_hbm, index_hbm, spread_hbm, out_ref, amp_ref, index_ref, spread_ref, sem):
    pairs = [(amp_hbm, amp_ref), (index_hbm, index_ref), (spread_hbm, spread_ref)]
    for i in range(4):
        at = slice(i * PIXELS // 4, (i + 1) * PIXELS // 4)
        pairs.append((cube_hbm.at[at], out_ref.at[at]))
    copies = [pltpu.make_async_copy(a, b, sem.at[i]) for i, (a, b) in enumerate(pairs)]
    for copy in copies:
        copy.start()
    nch = cube_hbm.shape[1]
    out_ref[PIXELS:, :] = jnp.zeros((COMPS, nch), jnp.float32)
    for copy in copies[:3]:
        copy.wait()
    for start, first in ((0, TILE - 2), (FIRST_ROWS, 0)):
        for t in range(3):
            for r in range(2):
                lane = start + (2 * t + r) * PITCH
                got = own_row(t, first + r, amp_ref, index_ref, spread_ref, nch)
                out_ref[PIXELS:, lane : lane + TILE] = got
    for copy in copies[3:]:
        copy.wait()


def packed(cube, amplitude, centre_index, spread):
    hbm = [pltpu.with_memory_space_constraint(v, pltpu.HBM) for v in (cube, amplitude, centre_index, spread)]
    return pl.pallas_call(
        pack_kernel,
        out_shape=pltpu.VMEM((PIXELS + COMPS, cube.shape[1]), jnp.float32),
        in_specs=[pl.BlockSpec(memory_space=pl.ANY)] * 4,
        out_specs=pl.BlockSpec(memory_space=pltpu.VMEM),
        scratch_shapes=[pltpu.VMEM(v.shape, v.dtype) for v in hbm[1:]] + [pltpu.SemaphoreType.DMA((7,))],
        compiler_params=pltpu.CompilerParams(vmem_limit_bytes=VMEM_LIMIT),
        cost_estimate=pl.CostEstimate(flops=1000, bytes_accessed=1_000_000, transcendentals=0),
        name="pack",
    )(*hbm)


def border_columns(ext_ref, shift):
    lane = lax.broadcasted_iota(jnp.int32, (COMPS, EXT), 1) % PITCH
    total = jnp.zeros((COMPS, EXT), jnp.float32)
    for t in range(3):
        moved = pltpu.roll(ext_ref[t], (2 * t - shift) % EXT, 1)
        total = jnp.where((lane >= 2 * t) & (lane < 2 * t + 2), moved, total)
    return total


def with_rows(own, above, below):
    row = lax.broadcasted_iota(jnp.int32, (COMPS, EXT), 1) // PITCH
    out = []
    for t in range(3):
        p = jnp.where(row < 2, pltpu.roll(above, (EXT - 2 * t * PITCH) % EXT, 1), own[t])
        out.append(jnp.where(row >= TILE + 2, pltpu.roll(below, ((TILE + 2 - 2 * t) * PITCH - FIRST_ROWS) % EXT, 1), p))
    return out


def up_and_down(p):
    return pltpu.roll(p, PITCH, 1) + pltpu.roll(p, EXT - PITCH, 1)


def smoothed(params, left, right):
    lane = lax.broadcasted_iota(jnp.int32, (COMPS, EXT), 1)
    column = lane % PITCH
    at_left, at_right = column == 0, column == TILE - 1
    y = lane // PITCH + (lax.axis_index("skyy") * TILE - 2)
    on_sky = (y >= 0) & (y < lax.axis_size("skyy") * TILE)
    ix = lax.axis_index("skyx")
    beside = on_sky & ((at_left & (ix > 0)) | (at_right & (ix < lax.axis_size("skyx") - 1)))

    def laplacian(p, side):
        before = jnp.where(at_left, side, pltpu.roll(p, 1, 1))
        after = jnp.where(at_right, side, pltpu.roll(p, EXT - 1, 1))
        return 4.0 * p - ((before + after) + up_and_down(p))

    out = []
    for t, p in enumerate(params):
        lefts = [pltpu.roll(left, (EXT - 2 * t - 1 + i) % EXT, 1) for i in range(2)]
        rights = [pltpu.roll(right, (TILE - 1 - 2 * t - i) % EXT, 1) for i in range(2)]
        one, two = [jnp.where(at_left, a, b) for a, b in zip(lefts, rights)]
        first = jnp.where(on_sky, laplacian(p, one), 0.0)
        first_beside = jnp.where(beside, 4.0 * one - ((two + p) + up_and_down(one)), 0.0)
        new = p - (STEPS[t] * LAMS[t]) * laplacian(first, first_beside)
        out.append(pltpu.roll(new, EXT - OWN, 1)[:, :PIXELS])
    return out


def five(v, flag=None):
    total = (v[0] + v[4]) + 4.0 * (v[1] + v[3]) + 6.0 * v[2]
    return total if flag is None else total * flag


def split(v):
    high = v.astype(jnp.bfloat16)
    return high, (v - high.astype(jnp.float32)).astype(jnp.bfloat16)


def column_kind():
    ix = lax.axis_index("skyx")
    kind = jnp.where(ix == 0, 0, jnp.where(ix == lax.axis_size("skyx") - 1, 2, 1))
    return 2 * kind + lax.rem(ix, 2)


def wavelet_kernel(
    a_ref, m1, p1, m2, p2, x_ref, k_ref, own_ref, w_ref,
    o_0, swap_ref, near_ref, far_ref, ext_ref, rows_ref, y_ref,
):
    nch = x_ref.shape[1]
    tiles = (m2, m1, x_ref, p1, p2)
    iy, ix = lax.axis_index("skyy"), lax.axis_index("skyx")
    near = [iy + i for i in (-2, -1, 0, 1, 2)]
    flags = [jnp.where((i >= 0) & (i < lax.axis_size("skyy")), 1.0, 0.0) for i in near]

    lane_tiles = nch // LANES

    def row_pass(step, carry):
        sub = pl.ds(pl.multiple_of((step // lane_tiles) * 8, 8), 8)
        lane = pl.ds(pl.multiple_of((step % lane_tiles) * LANES, LANES), LANES)

        @functools.cache
        def value(level, at):
            tile = (at + 2 * TILE) // TILE
            if level == 0:
                if tile in (1, 2, 3):
                    start = pl.multiple_of(at % TILE * TILE + step // lane_tiles * 8, 8)
                    return tiles[tile][pl.ds(start, 8), lane]
                return tiles[tile][at % TILE - (BEYOND if tile == 0 else 0), sub, lane]
            gap = 2 ** (level - 1)
            taps = [value(level - 1, at + (t - 2) * gap) for t in range(5)]
            return five(taps, None if tile == 2 else flags[tile])

        reach = {1: 28, 2: 24, 3: 16, 4: 0}
        lag = {1: 2, 2: 6, 3: 14, 4: 30}
        for at in range(-30, TILE + 30):
            value(0, at)
            for level in range(1, LEVELS + 1):
                row = at - lag[level]
                if -reach[level] <= row < TILE + reach[level]:
                    got = value(level, row)
                    if 0 <= row < TILE:
                        rows_ref[level - 1, row, sub, lane] = got
        return carry

    lax.fori_loop(0, 2 * lane_tiles, row_pass, 0)

    half, quarter = nch // 2, nch // 4

    def product(v, index):
        blocks = [
            jnp.dot(v[:, at : at + half], w_ref[index, i], preferred_element_type=jnp.float32)
            for i, at in enumerate((0, quarter, half))
        ]
        return blocks

    for level in range(LEVELS):
        high, low = split(rows_ref[level].reshape(PIXELS, nch))
        terms = [product(high, level), product(low, level)]
        if level >= 2:
            terms.append(product(high, level + 2))
        first, middle, last = [functools.reduce(lambda a, b: a + b, v) for v in zip(*terms)]
        pieces = (
            first[:, :quarter],
            first[:, quarter:] + middle[:, :quarter],
            middle[:, quarter:] + last[:, :quarter],
            last[:, quarter:],
        )
        for i, piece in enumerate(pieces):
            lane = slice(i * quarter, (i + 1) * quarter)
            high, low = split(piece * a_ref[level + 1, :, lane])
            high = high.reshape(TILE, TILE, quarter)
            y_ref[:, level * TILE : (level + 1) * TILE, lane] = high
            at = (level + LEVELS) * TILE
            y_ref[:, at : at + TILE, lane] = low.reshape(TILE, TILE, quarter)
            if level >= 2:
                at = (level + 6) * TILE
                y_ref[:, at : at + TILE, lane] = high

    odd = lax.rem(ix, 2)
    columns = k_ref[column_kind()]

    def column_pass(row, carry):
        got = jnp.dot(columns, y_ref[row], preferred_element_type=jnp.float32)
        at = pl.ds(pl.multiple_of(row * TILE, TILE), TILE)
        at_more = pl.ds(pl.multiple_of(row * TILE + PIXELS, TILE), TILE)
        swap_ref[at] = got[:TILE]
        swap_ref[at_more] = got[TILE : 2 * TILE]
        far_ref[at] = got[2 * TILE : 3 * TILE]
        o_0[row] = got[3 * TILE : 4 * TILE] + a_ref[0] * x_ref[at]
        near_ref[at] = got[4 * TILE :]
        return carry

    lax.fori_loop(0, TILE, column_pass, 0, unroll=4)

    params = with_rows(own_ref, m1[PIXELS:, :EXT], p1[PIXELS:, :EXT])
    for t in range(3):
        ext_ref[t] = params[t]
    to_right, to_left = border_columns(ext_ref, TILE - 2), border_columns(ext_ref, 0)
    swap_ref[2 * PIXELS : 2 * PIXELS + COMPS, :EXT] = jnp.where(odd == 0, to_right, to_left)
    swap_ref[2 * PIXELS + COMPS :, :EXT] = jnp.where(odd == 0, to_left, to_right)


def kept(x):
    return pltpu.with_memory_space_constraint(x, pltpu.VMEM)


def wavelet_parts(coeff, tiles, own, w, nch, length):
    k = jnp.asarray(scatter_matrices(length))
    vmem = pl.BlockSpec(memory_space=pltpu.VMEM)
    heights = (2 * (PIXELS + COMPS), PIXELS, PIXELS + COMPS)
    shapes = [(TILE, TILE, nch)] + [(n, nch) for n in heights] + [own.shape]
    return pl.pallas_call(
        wavelet_kernel,
        out_shape=[pltpu.VMEM(shape, jnp.float32) for shape in shapes],
        in_specs=[vmem] * 9,
        out_specs=[vmem] * 5,
        scratch_shapes=[
            pltpu.VMEM((LEVELS, TILE, TILE, nch), jnp.float32),
            pltpu.VMEM((TILE, 10 * TILE, nch), jnp.bfloat16),
        ],
        compiler_params=pltpu.CompilerParams(vmem_limit_bytes=VMEM_LIMIT),
        cost_estimate=pl.CostEstimate(flops=4_000_000_000, bytes_accessed=9_000_000, transcendentals=0),
        name="wavelet_parts",
    )(*[kept(x) for x in (coeff, *tiles, k, own, w)])


def add_kernel(near_ref, swapped_ref, out_ref):
    def body(row, carry):
        at = pl.ds(pl.multiple_of(row * TILE, TILE), TILE)
        more = pl.ds(pl.multiple_of(row * TILE + PIXELS, TILE), TILE)
        out_ref[at] = near_ref[at] + swapped_ref[more]
        return carry

    lax.fori_loop(0, TILE, body, 0, unroll=4)
    out_ref[PIXELS:, :] = swapped_ref[2 * PIXELS + COMPS :]


def outward(near, swapped):
    vmem = pl.BlockSpec(memory_space=pltpu.VMEM)
    return pl.pallas_call(
        add_kernel,
        out_shape=pltpu.VMEM((PIXELS + COMPS, near.shape[1]), jnp.float32),
        in_specs=[vmem] * 2,
        out_specs=vmem,
        compiler_params=pltpu.CompilerParams(vmem_limit_bytes=VMEM_LIMIT),
        cost_estimate=pl.CostEstimate(flops=100_000, bytes_accessed=1_500_000, transcendentals=0),
        name="outward",
    )(kept(near), kept(swapped))


def model_kernel(amp_ref, index_ref, spread_ref, w_hbm, model_ref, flat_ref, own_ref, w_ref, bump_ref, scale_ref, sem):
    load = pltpu.make_async_copy(w_hbm, w_ref, sem)
    load.start()
    nch, pixels = model_ref.shape
    own_ref[...] = jnp.zeros_like(own_ref)
    for t in range(3):
        for row in range(TILE):
            got = own_row(t, row, amp_ref, index_ref, spread_ref, nch)
            at = (row + 2) * PITCH
            own_ref[t, :, at : at + TILE] = got
            flat_ref[t, :, row * TILE : (row + 1) * TILE] = got
    mu = flat_ref[1] * float(nch)
    inv = 1.0 / flat_ref[2]
    flat_ref[1] = mu
    flat_ref[2] = inv
    scale_ref[...] = (-0.5 * math.log2(math.e)) * inv * inv

    def body(step, carry):
        base = pl.multiple_of(step * 8, 8)
        chan = (lax.broadcasted_iota(jnp.int32, (8, pixels), 0) + base).astype(jnp.float32)
        total = jnp.zeros((8, pixels), jnp.float32)
        for k in range(COMPS):
            diff = chan - flat_ref[1, k : k + 1, :]
            bump = jnp.exp2(diff * diff * scale_ref[k : k + 1, :])
            bump_ref[k, pl.ds(base, 8), :] = bump
            total += flat_ref[0, k : k + 1, :] * bump
        model_ref[pl.ds(base, 8), :] = total
        return carry

    lax.fori_loop(0, nch // 8, body, 0, unroll=2)
    load.wait()


def model_of(amplitude, centre_index, spread, nch):
    w = jnp.asarray(channel_matrices(nch))
    vmem = pl.BlockSpec(memory_space=pltpu.VMEM)
    pixels = TILE * TILE
    return pl.pallas_call(
        model_kernel,
        out_shape=[
            pltpu.VMEM((nch, pixels), jnp.float32),
            pltpu.VMEM((3, COMPS, pixels), jnp.float32),
            pltpu.VMEM((3, COMPS, EXT), jnp.float32),
            pltpu.VMEM(w.shape, w.dtype),
            pltpu.VMEM((COMPS, nch, pixels), jnp.float32),
        ],
        in_specs=[vmem] * 3 + [pl.BlockSpec(memory_space=pl.ANY)],
        out_specs=[vmem] * 5,
        scratch_shapes=[pltpu.VMEM((COMPS, pixels), jnp.float32), pltpu.SemaphoreType.DMA],
        compiler_params=pltpu.CompilerParams(vmem_limit_bytes=VMEM_LIMIT),
        cost_estimate=pl.CostEstimate(flops=10_000_000, bytes_accessed=1_000_000, transcendentals=1_100_000),
        name="gaussian_model",
    )(amplitude, centre_index, spread, pltpu.with_memory_space_constraint(w, pltpu.HBM))


def step_kernel(
    o_0, swapped_ref, far_ref, near_ref, model_ref, bump_ref, flat_ref, ext_ref,
    den_hbm, fit_ref, den_ref, r_ref, sem,
):
    nch, pixels = model_ref.shape
    rows = LANES // TILE
    parts = pixels // LANES
    copies = []
    inner, outer = swapped_ref[2 * PIXELS : 2 * PIXELS + COMPS, :EXT], near_ref[PIXELS:, :EXT]
    even = lax.rem(lax.axis_index("skyx"), 2) == 0
    left, right = jnp.where(even, outer, inner), jnp.where(even, inner, outer)
    bases = smoothed([ext_ref[t] for t in range(3)], left, right)
    for part in range(parts):
        at = slice(part * rows, (part + 1) * rows)
        for row in range(part * rows, (part + 1) * rows):
            flat = slice(row * TILE, (row + 1) * TILE)
            den_ref[row] = (o_0[row] + swapped_ref[flat]) + (far_ref[flat] + near_ref[flat])
        copies.append(pltpu.make_async_copy(den_ref.at[at], den_hbm.at[at], sem.at[part]))
        copies[-1].start()

    shape = (COMPS, rows, LANES)
    own_lanes = lax.broadcasted_iota(jnp.int32, shape, 2) // TILE == lax.broadcasted_iota(jnp.int32, shape, 1)
    for part in range(parts):
        block = den_ref[part * rows : (part + 1) * rows].reshape(LANES, nch)
        at = slice(part * LANES, (part + 1) * LANES)
        r_ref[:, at] = model_ref[:, at] - block.T

    for part in range(parts):
        at = slice(part * LANES, (part + 1) * LANES)
        sums = [[] for _ in range(3)]
        for first in range(0, COMPS, 4):
            chosen = range(first, first + 4)
            mus = [jnp.broadcast_to(flat_ref[1, k : k + 1, at], (8, LANES)) for k in chosen]

            def body(step, carry):
                base = pl.multiple_of(step * 8, 8)
                chan = (lax.broadcasted_iota(jnp.int32, (8, LANES), 0) + base).astype(jnp.float32)
                r = r_ref[pl.ds(base, 8), at]
                out = []
                for k, mu, (a, b, c) in zip(chosen, mus, carry):
                    diff = chan - mu
                    one = r * bump_ref[k, pl.ds(base, 8), at]
                    two = one * diff
                    out.append((a + one, b + two, c + two * diff))
                return tuple(out)

            zero = jnp.zeros((8, LANES), jnp.float32)
            done = lax.fori_loop(0, nch // 8, body, ((zero,) * 3,) * 4, unroll=8)
            for four in done:
                for t in range(3):
                    sums[t].append(jnp.sum(four[t], axis=0, keepdims=True))
        amp = flat_ref[0, :, at]
        inv = flat_ref[2, :, at]
        slope = amp * inv * inv
        grads = (
            jnp.concatenate(sums[0], axis=0) * (1.0 / nch),
            jnp.concatenate(sums[1], axis=0) * slope,
            jnp.concatenate(sums[2], axis=0) * (slope * inv * (1.0 / nch)),
        )
        for t in range(3):
            new = bases[t][:, at] - STEPS[t] * grads[t]
            spread_out = jnp.where(own_lanes, jnp.broadcast_to(new[:, None, :], own_lanes.shape), 0.0)
            for shift in (LANES // 2, LANES // 4, LANES // 8):
                spread_out = spread_out + pltpu.roll(spread_out, shift, 2)
            fit_ref[t, :, part * rows : (part + 1) * rows, :] = spread_out[:, :, :TILE]

    for copy in copies:
        copy.wait()


def gradient_step(parts, model, bump, flat, ext):
    vmem = pl.BlockSpec(memory_space=pltpu.VMEM)
    shape = parts[0].shape
    return pl.pallas_call(
        step_kernel,
        out_shape=[
            jax.ShapeDtypeStruct(shape, jnp.float32),
            jax.ShapeDtypeStruct((3, COMPS, TILE, TILE), jnp.float32),
        ],
        in_specs=[vmem] * 8,
        out_specs=[pl.BlockSpec(memory_space=pl.ANY), vmem],
        scratch_shapes=[
            pltpu.VMEM(shape, jnp.float32),
            pltpu.VMEM(model.shape, jnp.float32),
            pltpu.SemaphoreType.DMA((2,)),
        ],
        compiler_params=pltpu.CompilerParams(vmem_limit_bytes=VMEM_LIMIT),
        cost_estimate=pl.CostEstimate(flops=15_000_000, bytes_accessed=4_000_000, transcendentals=1_100_000),
        name="gradient_step",
    )(*[kept(x) for x in (*parts, model, bump, flat, ext)])


def on_device(cube, level_table, level_index, amplitude, centre_index, spread):
    nch = cube.shape[2]
    size = lax.axis_size("skyx")
    partner = [(i, i ^ 1) for i in range(size)]

    tile = packed(cube.reshape(PIXELS, nch), amplitude, centre_index, spread)
    up1, down1 = sent(tile, "skyy", 1), sent(tile, "skyy", -1)
    up2, down2 = sent(cube[BEYOND:], "skyy", 2), sent(cube[:-BEYOND], "skyy", -2)

    entries = jnp.arange(level_table.shape[0], dtype=jnp.int32)
    picks = (level_index[:, :, None] == entries).astype(jnp.float32)
    weight = jnp.sum(picks * level_table, axis=2)
    one = jnp.ones((1, nch), jnp.float32)
    coeff = jnp.concatenate([weight, one]) - jnp.concatenate([0.0 * one, weight])
    scale = jnp.array([16.0 ** (-3 * j) for j in range(LEVELS + 1)], jnp.float32)
    coeff = (coeff * scale[:, None])[:, None, :]
    model, flat, own, w, bump = model_of(amplitude, centre_index, spread, nch)
    o_0, swap, near, far, ext = wavelet_parts(coeff, (up1, down1, up2, down2, tile), own, w, nch, size * TILE)

    swapped = lax.ppermute(swap, "skyx", partner)
    far = away(far, "skyx", 2)
    near = away(outward(near, swapped), "skyx", -2)
    return gradient_step((o_0, swapped, far, near), model, bump, flat, ext)


def solution(mesh):
    placed = (
        P("skyy", "skyx", None),
        P(),
        P(),
        P(None, "skyy", "skyx"),
        P(None, "skyy", "skyx"),
        P(None, "skyy", "skyx"),
    )
    return jax.shard_map(
        on_device,
        mesh=mesh,
        in_specs=placed,
        out_specs=(P("skyy", "skyx", None), P(None, None, "skyy", "skyx")),
        check_vma=False,
    )
```

```python
import functools
import math

import jax
import jax.numpy as jnp
import numpy as np
from jax import lax
from jax.experimental import pallas as pl
from jax.experimental.pallas import tpu as pltpu
from jax.sharding import PartitionSpec as P

TILE = 16
LEVELS = 4
COMPS = 8
LANES = 128
TAPS = (1, 4, 6, 4, 1)
BEYOND = 2
VMEM_LIMIT = 20 * 1024 * 1024
ROLES = ((3, 1, 0, 2, 4), (1, 3, 4, 2, 0))
PIXELS = TILE * TILE
PITCH = TILE
EXT = 384
OWN = 2 * PITCH
FIRST_ROWS = 128
STEPS = (0.5, 0.002, 2.0)
LAMS = (0.2, 0.5, 0.05)


def blur_matrix(length, gap):
    out = np.zeros((length, length), np.float64)
    for tap, factor in enumerate(TAPS):
        offset = (tap - 2) * gap
        for i in range(max(0, -offset), min(length, length - offset)):
            out[i, i + offset] = factor
    return out


def composites(length):
    made, now = [], np.eye(length)
    for level in range(LEVELS):
        now = blur_matrix(length, 2**level) @ now
        made.append(now)
    return made


def halves(matrix):
    bf16 = jnp.bfloat16
    high = np.asarray(matrix, np.float32).astype(bf16)
    low = (np.asarray(matrix, np.float32) - high.astype(np.float32)).astype(bf16)
    return high, low


def channel_matrices(nch):
    parts = [halves(m.T) for m in composites(nch)]
    half, quarter = nch // 2, nch // 4
    out = []
    for whole in [p[0] for p in parts] + [p[1] for p in parts[2:]]:
        across = whole[quarter : quarter + half, quarter : quarter + half].copy()
        across[:quarter, :quarter] = 0
        across[quarter:, quarter:] = 0
        out.append(np.stack([whole[:half, :half], across, whole[half:, half:]]))
    return np.stack(out)


def scatter_matrices(length):
    whole = composites(length)
    kinds = []
    for start in (0, TILE * (length // TILE // 2), length - TILE):
        parts = []
        for m in whole:
            block = np.zeros((5 * TILE, TILE))
            for k in range(5 * TILE):
                at = start - 2 * TILE + k
                if 0 <= at < length:
                    block[k] = m[at, start : start + TILE]
            parts.append(halves(block))
        high = np.concatenate([p[0] for p in parts], axis=1)
        low = np.concatenate([p[1] for p in parts[2:]], axis=1)
        columns = np.concatenate([high, high, low], axis=1).reshape(5, TILE, -1)
        for order in ROLES:
            kinds.append(np.concatenate([columns[i] for i in order]))
    return np.stack(kinds)


def sent(values, axis, by):
    size = lax.axis_size(axis)
    if by > 0:
        pairs = [(i, i + by) for i in range(size - by)]
    else:
        pairs = [(i, i + by) for i in range(-by, size)]
    return lax.ppermute(values, axis, pairs)


def away(values, axis, by):
    size = lax.axis_size(axis)
    pairs = [(i, i + by if i % 2 else i - by) for i in range(size)]
    return lax.ppermute(values, axis, [(i, j) for i, j in pairs if 0 <= j < size])


def own_row(t, row, amp_ref, index_ref, spread_ref, nch):
    if t == 0:
        return amp_ref[:, row, :]
    if t == 1:
        return (index_ref[:, row, :].astype(jnp.float32) + 0.5) * (1.0 / nch)
    return spread_ref[:, row, :]


def pack_kernel(cube_hbm, amp_hbm, index_hbm, spread_hbm, out_ref, amp_ref, index_ref, spread_ref, sem):
    pairs = ((amp_hbm, amp_ref), (index_hbm, index_ref), (spread_hbm, spread_ref), (cube_hbm, out_ref.at[0:PIXELS]))
    copies = [pltpu.make_async_copy(a, b, sem.at[i]) for i, (a, b) in enumerate(pairs)]
    for copy in copies:
        copy.start()
    nch = cube_hbm.shape[1]
    out_ref[PIXELS:, :] = jnp.zeros((COMPS, nch), jnp.float32)
    for copy in copies[:3]:
        copy.wait()
    for start, first in ((0, TILE - 2), (FIRST_ROWS, 0)):
        for t in range(3):
            for r in range(2):
                lane = start + (2 * t + r) * PITCH
                got = own_row(t, first + r, amp_ref, index_ref, spread_ref, nch)
                out_ref[PIXELS:, lane : lane + TILE] = got
    copies[3].wait()


def packed(cube, amplitude, centre_index, spread):
    hbm = [pltpu.with_memory_space_constraint(v, pltpu.HBM) for v in (cube, amplitude, centre_index, spread)]
    return pl.pallas_call(
        pack_kernel,
        out_shape=pltpu.VMEM((PIXELS + COMPS, cube.shape[1]), jnp.float32),
        in_specs=[pl.BlockSpec(memory_space=pl.ANY)] * 4,
        out_specs=pl.BlockSpec(memory_space=pltpu.VMEM),
        scratch_shapes=[pltpu.VMEM(v.shape, v.dtype) for v in hbm[1:]] + [pltpu.SemaphoreType.DMA((4,))],
        compiler_params=pltpu.CompilerParams(vmem_limit_bytes=VMEM_LIMIT),
        cost_estimate=pl.CostEstimate(flops=1000, bytes_accessed=1_000_000, transcendentals=0),
        name="pack",
    )(*hbm)


def border_columns(ext_ref, shift):
    lane = lax.broadcasted_iota(jnp.int32, (COMPS, EXT), 1) % PITCH
    total = jnp.zeros((COMPS, EXT), jnp.float32)
    for t in range(3):
        moved = pltpu.roll(ext_ref[t], (2 * t - shift) % EXT, 1)
        total = jnp.where((lane >= 2 * t) & (lane < 2 * t + 2), moved, total)
    return total


def with_rows(own, above, below):
    row = lax.broadcasted_iota(jnp.int32, (COMPS, EXT), 1) // PITCH
    out = []
    for t in range(3):
        p = jnp.where(row < 2, pltpu.roll(above, (EXT - 2 * t * PITCH) % EXT, 1), own[t])
        out.append(jnp.where(row >= TILE + 2, pltpu.roll(below, ((TILE + 2 - 2 * t) * PITCH - FIRST_ROWS) % EXT, 1), p))
    return out


def up_and_down(p):
    return pltpu.roll(p, PITCH, 1) + pltpu.roll(p, EXT - PITCH, 1)


def smoothed(params, left, right):
    lane = lax.broadcasted_iota(jnp.int32, (COMPS, EXT), 1)
    column = lane % PITCH
    at_left, at_right = column == 0, column == TILE - 1
    y = lane // PITCH + (lax.axis_index("skyy") * TILE - 2)
    on_sky = (y >= 0) & (y < lax.axis_size("skyy") * TILE)
    ix = lax.axis_index("skyx")
    beside = on_sky & ((at_left & (ix > 0)) | (at_right & (ix < lax.axis_size("skyx") - 1)))

    def laplacian(p, side):
        before = jnp.where(at_left, side, pltpu.roll(p, 1, 1))
        after = jnp.where(at_right, side, pltpu.roll(p, EXT - 1, 1))
        return 4.0 * p - ((before + after) + up_and_down(p))

    out = []
    for t, p in enumerate(params):
        lefts = [pltpu.roll(left, (EXT - 2 * t - 1 + i) % EXT, 1) for i in range(2)]
        rights = [pltpu.roll(right, (TILE - 1 - 2 * t - i) % EXT, 1) for i in range(2)]
        one, two = [jnp.where(at_left, a, b) for a, b in zip(lefts, rights)]
        first = jnp.where(on_sky, laplacian(p, one), 0.0)
        first_beside = jnp.where(beside, 4.0 * one - ((two + p) + up_and_down(one)), 0.0)
        new = p - (STEPS[t] * LAMS[t]) * laplacian(first, first_beside)
        out.append(pltpu.roll(new, EXT - OWN, 1)[:, :PIXELS])
    return out


def five(v, flag=None):
    total = (v[0] + v[4]) + 4.0 * (v[1] + v[3]) + 6.0 * v[2]
    return total if flag is None else total * flag


def split(v):
    high = v.astype(jnp.bfloat16)
    return high, (v - high.astype(jnp.float32)).astype(jnp.bfloat16)


def column_kind():
    ix = lax.axis_index("skyx")
    kind = jnp.where(ix == 0, 0, jnp.where(ix == lax.axis_size("skyx") - 1, 2, 1))
    return 2 * kind + lax.rem(ix, 2)


def wavelet_kernel(
    a_ref, m1, p1, m2, p2, x_ref, k_ref, own_ref, w_ref,
    o_0, swap_ref, near_ref, far_ref, ext_ref, rows_ref, y_ref,
):
    nch = x_ref.shape[1]
    tiles = (m2, m1, x_ref, p1, p2)
    iy, ix = lax.axis_index("skyy"), lax.axis_index("skyx")
    near = [iy + i for i in (-2, -1, 0, 1, 2)]
    flags = [jnp.where((i >= 0) & (i < lax.axis_size("skyy")), 1.0, 0.0) for i in near]

    lane_tiles = nch // LANES

    def row_pass(step, carry):
        sub = pl.ds(pl.multiple_of((step // lane_tiles) * 8, 8), 8)
        lane = pl.ds(pl.multiple_of((step % lane_tiles) * LANES, LANES), LANES)

        @functools.cache
        def value(level, at):
            tile = (at + 2 * TILE) // TILE
            if level == 0:
                if tile in (1, 2, 3):
                    start = pl.multiple_of(at % TILE * TILE + step // lane_tiles * 8, 8)
                    return tiles[tile][pl.ds(start, 8), lane]
                return tiles[tile][at % TILE - (BEYOND if tile == 0 else 0), sub, lane]
            gap = 2 ** (level - 1)
            taps = [value(level - 1, at + (t - 2) * gap) for t in range(5)]
            return five(taps, None if tile == 2 else flags[tile])

        reach = {1: 28, 2: 24, 3: 16, 4: 0}
        lag = {1: 2, 2: 6, 3: 14, 4: 30}
        for at in range(-30, TILE + 30):
            value(0, at)
            for level in range(1, LEVELS + 1):
                row = at - lag[level]
                if -reach[level] <= row < TILE + reach[level]:
                    got = value(level, row)
                    if 0 <= row < TILE:
                        rows_ref[level - 1, row, sub, lane] = got
        return carry

    lax.fori_loop(0, 2 * lane_tiles, row_pass, 0)

    half, quarter = nch // 2, nch // 4

    for level in range(LEVELS):
        high, low = split(rows_ref[level].reshape(PIXELS, nch))
        parts, index = [high, low], [level, level]
        if level >= 2:
            parts, index = parts + [high], index + [level + 2]
        first, middle, last = [
            jnp.dot(
                jnp.concatenate([v[:, at : at + half] for v in parts], axis=1),
                jnp.concatenate([w_ref[j, i] for j in index], axis=0),
                preferred_element_type=jnp.float32,
            )
            for i, at in enumerate((0, quarter, half))
        ]
        pieces = (
            first[:, :quarter],
            first[:, quarter:] + middle[:, :quarter],
            middle[:, quarter:] + last[:, :quarter],
            last[:, quarter:],
        )
        for i, piece in enumerate(pieces):
            lane = slice(i * quarter, (i + 1) * quarter)
            high, low = split(piece * a_ref[level + 1, :, lane])
            high = high.reshape(TILE, TILE, quarter)
            y_ref[:, level * TILE : (level + 1) * TILE, lane] = high
            at = (level + LEVELS) * TILE
            y_ref[:, at : at + TILE, lane] = low.reshape(TILE, TILE, quarter)
            if level >= 2:
                at = (level + 6) * TILE
                y_ref[:, at : at + TILE, lane] = high

    odd = lax.rem(ix, 2)
    columns = k_ref[column_kind()]

    def column_pass(row, carry):
        got = jnp.dot(columns, y_ref[row], preferred_element_type=jnp.float32)
        at = pl.ds(pl.multiple_of(row * TILE, TILE), TILE)
        at_more = pl.ds(pl.multiple_of(row * TILE + PIXELS, TILE), TILE)
        swap_ref[at] = got[:TILE]
        swap_ref[at_more] = got[TILE : 2 * TILE]
        far_ref[at] = got[2 * TILE : 3 * TILE]
        o_0[row] = got[3 * TILE : 4 * TILE] + a_ref[0] * x_ref[at]
        near_ref[at] = got[4 * TILE :]
        return carry

    lax.fori_loop(0, TILE, column_pass, 0, unroll=16)

    params = with_rows(own_ref, m1[PIXELS:, :EXT], p1[PIXELS:, :EXT])
    for t in range(3):
        ext_ref[t] = params[t]
    to_right, to_left = border_columns(ext_ref, TILE - 2), border_columns(ext_ref, 0)
    swap_ref[2 * PIXELS : 2 * PIXELS + COMPS, :EXT] = jnp.where(odd == 0, to_right, to_left)
    swap_ref[2 * PIXELS + COMPS :, :EXT] = jnp.where(odd == 0, to_left, to_right)


def kept(x):
    return pltpu.with_memory_space_constraint(x, pltpu.VMEM)


def wavelet_parts(coeff, tiles, own, w, nch, length):
    k = jnp.asarray(scatter_matrices(length))
    vmem = pl.BlockSpec(memory_space=pltpu.VMEM)
    heights = (2 * (PIXELS + COMPS), PIXELS, PIXELS + COMPS)
    shapes = [(TILE, TILE, nch)] + [(n, nch) for n in heights] + [own.shape]
    return pl.pallas_call(
        wavelet_kernel,
        out_shape=[pltpu.VMEM(shape, jnp.float32) for shape in shapes],
        in_specs=[vmem] * 9,
        out_specs=[vmem] * 5,
        scratch_shapes=[
            pltpu.VMEM((LEVELS, TILE, TILE, nch), jnp.float32),
            pltpu.VMEM((TILE, 10 * TILE, nch), jnp.bfloat16),
        ],
        compiler_params=pltpu.CompilerParams(vmem_limit_bytes=VMEM_LIMIT),
        cost_estimate=pl.CostEstimate(flops=4_000_000_000, bytes_accessed=9_000_000, transcendentals=0),
        name="wavelet_parts",
    )(*[kept(x) for x in (coeff, *tiles, k, own, w)])


def add_kernel(near_ref, swapped_ref, out_ref):
    def body(row, carry):
        at = pl.ds(pl.multiple_of(row * TILE, TILE), TILE)
        more = pl.ds(pl.multiple_of(row * TILE + PIXELS, TILE), TILE)
        out_ref[at] = near_ref[at] + swapped_ref[more]
        return carry

    lax.fori_loop(0, TILE, body, 0, unroll=4)
    out_ref[PIXELS:, :] = swapped_ref[2 * PIXELS + COMPS :]


def outward(near, swapped):
    vmem = pl.BlockSpec(memory_space=pltpu.VMEM)
    return pl.pallas_call(
        add_kernel,
        out_shape=pltpu.VMEM((PIXELS + COMPS, near.shape[1]), jnp.float32),
        in_specs=[vmem] * 2,
        out_specs=vmem,
        compiler_params=pltpu.CompilerParams(vmem_limit_bytes=VMEM_LIMIT),
        cost_estimate=pl.CostEstimate(flops=100_000, bytes_accessed=1_500_000, transcendentals=0),
        name="outward",
    )(kept(near), kept(swapped))


def model_kernel(amp_ref, index_ref, spread_ref, w_hbm, model_ref, flat_ref, own_ref, w_ref, bump_ref, scale_ref, sem):
    load = pltpu.make_async_copy(w_hbm, w_ref, sem)
    load.start()
    nch, pixels = model_ref.shape
    own_ref[...] = jnp.zeros_like(own_ref)
    for t in range(3):
        for row in range(TILE):
            got = own_row(t, row, amp_ref, index_ref, spread_ref, nch)
            at = (row + 2) * PITCH
            own_ref[t, :, at : at + TILE] = got
            flat_ref[t, :, row * TILE : (row + 1) * TILE] = got
    mu = flat_ref[1] * float(nch)
    inv = 1.0 / flat_ref[2]
    flat_ref[1] = mu
    flat_ref[2] = inv
    scale_ref[...] = (-0.5 * math.log2(math.e)) * inv * inv

    def body(step, carry):
        base = pl.multiple_of(step * 8, 8)
        chan = (lax.broadcasted_iota(jnp.int32, (8, pixels), 0) + base).astype(jnp.float32)
        total = jnp.zeros((8, pixels), jnp.float32)
        for k in range(COMPS):
            diff = chan - flat_ref[1, k : k + 1, :]
            bump = jnp.exp2(diff * diff * scale_ref[k : k + 1, :])
            bump_ref[k, pl.ds(base, 8), :] = bump
            total += flat_ref[0, k : k + 1, :] * bump
        model_ref[pl.ds(base, 8), :] = total
        return carry

    lax.fori_loop(0, nch // 8, body, 0, unroll=2)
    load.wait()


def model_of(amplitude, centre_index, spread, nch):
    w = jnp.asarray(channel_matrices(nch))
    vmem = pl.BlockSpec(memory_space=pltpu.VMEM)
    pixels = TILE * TILE
    return pl.pallas_call(
        model_kernel,
        out_shape=[
            pltpu.VMEM((nch, pixels), jnp.float32),
            pltpu.VMEM((3, COMPS, pixels), jnp.float32),
            pltpu.VMEM((3, COMPS, EXT), jnp.float32),
            pltpu.VMEM(w.shape, w.dtype),
            pltpu.VMEM((COMPS, nch, pixels), jnp.float32),
        ],
        in_specs=[vmem] * 3 + [pl.BlockSpec(memory_space=pl.ANY)],
        out_specs=[vmem] * 5,
        scratch_shapes=[pltpu.VMEM((COMPS, pixels), jnp.float32), pltpu.SemaphoreType.DMA],
        compiler_params=pltpu.CompilerParams(vmem_limit_bytes=VMEM_LIMIT),
        cost_estimate=pl.CostEstimate(flops=10_000_000, bytes_accessed=1_000_000, transcendentals=1_100_000),
        name="gaussian_model",
    )(amplitude, centre_index, spread, pltpu.with_memory_space_constraint(w, pltpu.HBM))


def step_kernel(
    o_0, swapped_ref, far_ref, near_ref, model_ref, bump_ref, flat_ref, ext_ref,
    den_hbm, fit_ref, den_ref, r_ref, sem,
):
    nch, pixels = model_ref.shape
    rows = LANES // TILE
    parts = pixels // LANES
    copies = []
    inner, outer = swapped_ref[2 * PIXELS : 2 * PIXELS + COMPS, :EXT], near_ref[PIXELS:, :EXT]
    even = lax.rem(lax.axis_index("skyx"), 2) == 0
    left, right = jnp.where(even, outer, inner), jnp.where(even, inner, outer)
    bases = smoothed([ext_ref[t] for t in range(3)], left, right)
    for part in range(parts):
        at = slice(part * rows, (part + 1) * rows)
        for row in range(part * rows, (part + 1) * rows):
            flat = slice(row * TILE, (row + 1) * TILE)
            den_ref[row] = (o_0[row] + swapped_ref[flat]) + (far_ref[flat] + near_ref[flat])
        copies.append(pltpu.make_async_copy(den_ref.at[at], den_hbm.at[at], sem.at[part]))
        copies[-1].start()

    shape = (COMPS, rows, LANES)
    own_lanes = lax.broadcasted_iota(jnp.int32, shape, 2) // TILE == lax.broadcasted_iota(jnp.int32, shape, 1)
    for part in range(parts):
        block = den_ref[part * rows : (part + 1) * rows].reshape(LANES, nch)
        at = slice(part * LANES, (part + 1) * LANES)
        r_ref[:, at] = model_ref[:, at] - block.T

    for part in range(parts):
        at = slice(part * LANES, (part + 1) * LANES)
        sums = [[] for _ in range(3)]
        for first in range(0, COMPS, 4):
            chosen = range(first, first + 4)
            mus = [jnp.broadcast_to(flat_ref[1, k : k + 1, at], (8, LANES)) for k in chosen]

            def body(step, carry):
                base = pl.multiple_of(step * 8, 8)
                chan = (lax.broadcasted_iota(jnp.int32, (8, LANES), 0) + base).astype(jnp.float32)
                r = r_ref[pl.ds(base, 8), at]
                out = []
                for k, mu, (a, b, c) in zip(chosen, mus, carry):
                    diff = chan - mu
                    one = r * bump_ref[k, pl.ds(base, 8), at]
                    two = one * diff
                    out.append((a + one, b + two, c + two * diff))
                return tuple(out)

            zero = jnp.zeros((8, LANES), jnp.float32)
            done = lax.fori_loop(0, nch // 8, body, ((zero,) * 3,) * 4, unroll=16)
            for four in done:
                for t in range(3):
                    sums[t].append(jnp.sum(four[t], axis=0, keepdims=True))
        amp = flat_ref[0, :, at]
        inv = flat_ref[2, :, at]
        slope = amp * inv * inv
        grads = (
            jnp.concatenate(sums[0], axis=0) * (1.0 / nch),
            jnp.concatenate(sums[1], axis=0) * slope,
            jnp.concatenate(sums[2], axis=0) * (slope * inv * (1.0 / nch)),
        )
        for t in range(3):
            new = bases[t][:, at] - STEPS[t] * grads[t]
            spread_out = jnp.where(own_lanes, jnp.broadcast_to(new[:, None, :], own_lanes.shape), 0.0)
            for shift in (LANES // 2, LANES // 4, LANES // 8):
                spread_out = spread_out + pltpu.roll(spread_out, shift, 2)
            fit_ref[t, :, part * rows : (part + 1) * rows, :] = spread_out[:, :, :TILE]

    for copy in copies:
        copy.wait()


def gradient_step(parts, model, bump, flat, ext):
    vmem = pl.BlockSpec(memory_space=pltpu.VMEM)
    shape = parts[0].shape
    return pl.pallas_call(
        step_kernel,
        out_shape=[
            jax.ShapeDtypeStruct(shape, jnp.float32),
            jax.ShapeDtypeStruct((3, COMPS, TILE, TILE), jnp.float32),
        ],
        in_specs=[vmem] * 8,
        out_specs=[pl.BlockSpec(memory_space=pl.ANY), vmem],
        scratch_shapes=[
            pltpu.VMEM(shape, jnp.float32),
            pltpu.VMEM(model.shape, jnp.float32),
            pltpu.SemaphoreType.DMA((2,)),
        ],
        compiler_params=pltpu.CompilerParams(vmem_limit_bytes=VMEM_LIMIT),
        cost_estimate=pl.CostEstimate(flops=15_000_000, bytes_accessed=4_000_000, transcendentals=1_100_000),
        name="gradient_step",
    )(*[kept(x) for x in (*parts, model, bump, flat, ext)])


def on_device(cube, level_table, level_index, amplitude, centre_index, spread):
    nch = cube.shape[2]
    size = lax.axis_size("skyx")
    partner = [(i, i ^ 1) for i in range(size)]

    tile = packed(cube.reshape(PIXELS, nch), amplitude, centre_index, spread)
    up1, down1 = sent(tile, "skyy", 1), sent(tile, "skyy", -1)
    up2, down2 = sent(cube[BEYOND:], "skyy", 2), sent(cube[:-BEYOND], "skyy", -2)

    entries = jnp.arange(level_table.shape[0], dtype=jnp.int32)
    picks = (level_index[:, :, None] == entries).astype(jnp.float32)
    weight = jnp.sum(picks * level_table, axis=2)
    one = jnp.ones((1, nch), jnp.float32)
    coeff = jnp.concatenate([weight, one]) - jnp.concatenate([0.0 * one, weight])
    scale = jnp.array([16.0 ** (-3 * j) for j in range(LEVELS + 1)], jnp.float32)
    coeff = (coeff * scale[:, None])[:, None, :]
    model, flat, own, w, bump = model_of(amplitude, centre_index, spread, nch)
    o_0, swap, near, far, ext = wavelet_parts(coeff, (up1, down1, up2, down2, tile), own, w, nch, size * TILE)

    swapped = lax.ppermute(swap, "skyx", partner)
    far = away(far, "skyx", 2)
    near = away(outward(near, swapped), "skyx", -2)
    return gradient_step((o_0, swapped, far, near), model, bump, flat, ext)


def solution(mesh):
    placed = (
        P("skyy", "skyx", None),
        P(),
        P(),
        P(None, "skyy", "skyx"),
        P(None, "skyy", "skyx"),
        P(None, "skyy", "skyx"),
    )
    return jax.shard_map(
        on_device,
        mesh=mesh,
        in_specs=placed,
        out_specs=(P("skyy", "skyx", None), P(None, None, "skyy", "skyx")),
        check_vma=False,
    )
```

```python
import functools
import math

import jax
import jax.numpy as jnp
import numpy as np
from jax import lax
from jax.experimental import pallas as pl
from jax.experimental.pallas import tpu as pltpu
from jax.sharding import PartitionSpec as P

TILE = 16
LEVELS = 4
COMPS = 8
LANES = 128
TAPS = (1, 4, 6, 4, 1)
BEYOND = 2
REACHED = TILE - BEYOND
FAR_ROWS = TILE * REACHED + 8
VMEM_LIMIT = 20 * 1024 * 1024
ROLES = ((3, 1, 0, 2, 4), (1, 3, 4, 2, 0))
PIXELS = TILE * TILE
PITCH = TILE
EXT = 384
OWN = 2 * PITCH
FIRST_ROWS = 128
STEPS = (0.5, 0.002, 2.0)
LAMS = (0.2, 0.5, 0.05)


def blur_matrix(length, gap):
    out = np.zeros((length, length), np.float64)
    for tap, factor in enumerate(TAPS):
        offset = (tap - 2) * gap
        for i in range(max(0, -offset), min(length, length - offset)):
            out[i, i + offset] = factor
    return out


def composites(length):
    made, now = [], np.eye(length)
    for level in range(LEVELS):
        now = blur_matrix(length, 2**level) @ now
        made.append(now)
    return made


def halves(matrix):
    bf16 = jnp.bfloat16
    high = np.asarray(matrix, np.float32).astype(bf16)
    low = (np.asarray(matrix, np.float32) - high.astype(np.float32)).astype(bf16)
    return high, low


def channel_matrices(nch):
    parts = [halves(m.T) for m in composites(nch)]
    half, quarter = nch // 2, nch // 4
    out = []
    for whole in [p[0] for p in parts] + [p[1] for p in parts[2:]]:
        across = whole[quarter : quarter + half, quarter : quarter + half].copy()
        across[:quarter, :quarter] = 0
        across[quarter:, quarter:] = 0
        out.append(np.stack([whole[:half, :half], across, whole[half:, half:]]))
    return np.stack(out)


def scatter_matrices(length):
    whole = composites(length)
    kinds = []
    for start in (0, TILE * (length // TILE // 2), length - TILE):
        parts = []
        for m in whole:
            block = np.zeros((5 * TILE, TILE))
            for k in range(5 * TILE):
                at = start - 2 * TILE + k
                if 0 <= at < length:
                    block[k] = m[at, start : start + TILE]
            parts.append(halves(block))
        high = np.concatenate([p[0] for p in parts], axis=1)
        low = np.concatenate([p[1] for p in parts[2:]], axis=1)
        columns = np.concatenate([high, high, low], axis=1).reshape(5, TILE, -1)
        for order in ROLES:
            blocks = [columns[i] for i in order]
            if order[2] == 0:
                blocks[2] = np.roll(blocks[2], -BEYOND, axis=0)
            kinds.append(np.concatenate(blocks))
    return np.stack(kinds)


def sent(values, axis, by):
    size = lax.axis_size(axis)
    if by > 0:
        pairs = [(i, i + by) for i in range(size - by)]
    else:
        pairs = [(i, i + by) for i in range(-by, size)]
    return lax.ppermute(values, axis, pairs)


def away(values, axis, by):
    size = lax.axis_size(axis)
    pairs = [(i, i + by if i % 2 else i - by) for i in range(size)]
    return lax.ppermute(values, axis, [(i, j) for i, j in pairs if 0 <= j < size])


def own_row(t, row, amp_ref, index_ref, spread_ref, nch):
    if t == 0:
        return amp_ref[:, row, :]
    if t == 1:
        return (index_ref[:, row, :].astype(jnp.float32) + 0.5) * (1.0 / nch)
    return spread_ref[:, row, :]


def pack_kernel(cube_hbm, amp_hbm, index_hbm, spread_hbm, out_ref, amp_ref, index_ref, spread_ref, sem):
    pairs = ((amp_hbm, amp_ref), (index_hbm, index_ref), (spread_hbm, spread_ref), (cube_hbm, out_ref.at[0:PIXELS]))
    copies = [pltpu.make_async_copy(a, b, sem.at[i]) for i, (a, b) in enumerate(pairs)]
    for copy in copies:
        copy.start()
    nch = cube_hbm.shape[1]
    out_ref[PIXELS:, :] = jnp.zeros((COMPS, nch), jnp.float32)
    for copy in copies[:3]:
        copy.wait()
    for start, first in ((0, TILE - 2), (FIRST_ROWS, 0)):
        for t in range(3):
            for r in range(2):
                lane = start + (2 * t + r) * PITCH
                got = own_row(t, first + r, amp_ref, index_ref, spread_ref, nch)
                out_ref[PIXELS:, lane : lane + TILE] = got
    copies[3].wait()


def packed(cube, amplitude, centre_index, spread):
    hbm = [pltpu.with_memory_space_constraint(v, pltpu.HBM) for v in (cube, amplitude, centre_index, spread)]
    return pl.pallas_call(
        pack_kernel,
        out_shape=pltpu.VMEM((PIXELS + COMPS, cube.shape[1]), jnp.float32),
        in_specs=[pl.BlockSpec(memory_space=pl.ANY)] * 4,
        out_specs=pl.BlockSpec(memory_space=pltpu.VMEM),
        scratch_shapes=[pltpu.VMEM(v.shape, v.dtype) for v in hbm[1:]] + [pltpu.SemaphoreType.DMA((4,))],
        compiler_params=pltpu.CompilerParams(vmem_limit_bytes=VMEM_LIMIT),
        cost_estimate=pl.CostEstimate(flops=1000, bytes_accessed=1_000_000, transcendentals=0),
        name="pack",
    )(*hbm)


def border_columns(ext_ref, shift):
    lane = lax.broadcasted_iota(jnp.int32, (COMPS, EXT), 1) % PITCH
    total = jnp.zeros((COMPS, EXT), jnp.float32)
    for t in range(3):
        moved = pltpu.roll(ext_ref[t], (2 * t - shift) % EXT, 1)
        total = jnp.where((lane >= 2 * t) & (lane < 2 * t + 2), moved, total)
    return total


def with_rows(own, above, below):
    row = lax.broadcasted_iota(jnp.int32, (COMPS, EXT), 1) // PITCH
    out = []
    for t in range(3):
        p = jnp.where(row < 2, pltpu.roll(above, (EXT - 2 * t * PITCH) % EXT, 1), own[t])
        out.append(jnp.where(row >= TILE + 2, pltpu.roll(below, ((TILE + 2 - 2 * t) * PITCH - FIRST_ROWS) % EXT, 1), p))
    return out


def up_and_down(p):
    return pltpu.roll(p, PITCH, 1) + pltpu.roll(p, EXT - PITCH, 1)


def smoothed(params, left, right):
    lane = lax.broadcasted_iota(jnp.int32, (COMPS, EXT), 1)
    column = lane % PITCH
    at_left, at_right = column == 0, column == TILE - 1
    y = lane // PITCH + (lax.axis_index("skyy") * TILE - 2)
    on_sky = (y >= 0) & (y < lax.axis_size("skyy") * TILE)
    ix = lax.axis_index("skyx")
    beside = on_sky & ((at_left & (ix > 0)) | (at_right & (ix < lax.axis_size("skyx") - 1)))

    def laplacian(p, side):
        before = jnp.where(at_left, side, pltpu.roll(p, 1, 1))
        after = jnp.where(at_right, side, pltpu.roll(p, EXT - 1, 1))
        return 4.0 * p - ((before + after) + up_and_down(p))

    out = []
    for t, p in enumerate(params):
        lefts = [pltpu.roll(left, (EXT - 2 * t - 1 + i) % EXT, 1) for i in range(2)]
        rights = [pltpu.roll(right, (TILE - 1 - 2 * t - i) % EXT, 1) for i in range(2)]
        one, two = [jnp.where(at_left, a, b) for a, b in zip(lefts, rights)]
        first = jnp.where(on_sky, laplacian(p, one), 0.0)
        first_beside = jnp.where(beside, 4.0 * one - ((two + p) + up_and_down(one)), 0.0)
        new = p - (STEPS[t] * LAMS[t]) * laplacian(first, first_beside)
        out.append(pltpu.roll(new, EXT - OWN, 1)[:, :PIXELS])
    return out


def five(v, flag=None):
    total = (v[0] + v[4]) + 4.0 * (v[1] + v[3]) + 6.0 * v[2]
    return total if flag is None else total * flag


def split(v):
    high = v.astype(jnp.bfloat16)
    return high, (v - high.astype(jnp.float32)).astype(jnp.bfloat16)


def column_kind():
    ix = lax.axis_index("skyx")
    kind = jnp.where(ix == 0, 0, jnp.where(ix == lax.axis_size("skyx") - 1, 2, 1))
    return 2 * kind + lax.rem(ix, 2)


def wavelet_kernel(
    a_ref, m1, p1, m2, p2, x_ref, k_ref, own_ref, w_ref,
    o_0, swap_ref, near_ref, far_ref, ext_ref, rows_ref, y_ref,
):
    nch = x_ref.shape[1]
    tiles = (m2, m1, x_ref, p1, p2)
    iy, ix = lax.axis_index("skyy"), lax.axis_index("skyx")
    near = [iy + i for i in (-2, -1, 0, 1, 2)]
    flags = [jnp.where((i >= 0) & (i < lax.axis_size("skyy")), 1.0, 0.0) for i in near]

    lane_tiles = nch // LANES

    def row_pass(step, carry):
        sub = pl.ds(pl.multiple_of((step // lane_tiles) * 8, 8), 8)
        lane = pl.ds(pl.multiple_of((step % lane_tiles) * LANES, LANES), LANES)

        @functools.cache
        def value(level, at):
            tile = (at + 2 * TILE) // TILE
            if level == 0:
                if tile in (1, 2, 3):
                    start = pl.multiple_of(at % TILE * TILE + step // lane_tiles * 8, 8)
                    return tiles[tile][pl.ds(start, 8), lane]
                return tiles[tile][at % TILE - (BEYOND if tile == 0 else 0), sub, lane]
            gap = 2 ** (level - 1)
            taps = [value(level - 1, at + (t - 2) * gap) for t in range(5)]
            return five(taps, None if tile == 2 else flags[tile])

        reach = {1: 28, 2: 24, 3: 16, 4: 0}
        lag = {1: 2, 2: 6, 3: 14, 4: 30}
        for at in range(-30, TILE + 30):
            value(0, at)
            for level in range(1, LEVELS + 1):
                row = at - lag[level]
                if -reach[level] <= row < TILE + reach[level]:
                    got = value(level, row)
                    if 0 <= row < TILE:
                        rows_ref[level - 1, row, sub, lane] = got
        return carry

    lax.fori_loop(0, 2 * lane_tiles, row_pass, 0)

    half, quarter = nch // 2, nch // 4

    for level in range(LEVELS):
        high, low = split(rows_ref[level].reshape(PIXELS, nch))
        parts, index = [high, low], [level, level]
        if level >= 2:
            parts, index = parts + [high], index + [level + 2]
        first, middle, last = [
            jnp.dot(
                jnp.concatenate([v[:, at : at + half] for v in parts], axis=1),
                jnp.concatenate([w_ref[j, i] for j in index], axis=0),
                preferred_element_type=jnp.float32,
            )
            for i, at in enumerate((0, quarter, half))
        ]
        pieces = (
            first[:, :quarter],
            first[:, quarter:] + middle[:, :quarter],
            middle[:, quarter:] + last[:, :quarter],
            last[:, quarter:],
        )
        for i, piece in enumerate(pieces):
            lane = slice(i * quarter, (i + 1) * quarter)
            high, low = split(piece * a_ref[level + 1, :, lane])
            high = high.reshape(TILE, TILE, quarter)
            y_ref[:, level * TILE : (level + 1) * TILE, lane] = high
            at = (level + LEVELS) * TILE
            y_ref[:, at : at + TILE, lane] = low.reshape(TILE, TILE, quarter)
            if level >= 2:
                at = (level + 6) * TILE
                y_ref[:, at : at + TILE, lane] = high

    odd = lax.rem(ix, 2)
    columns = k_ref[column_kind()]

    for row in range(TILE):
        got = jnp.dot(columns, y_ref[row], preferred_element_type=jnp.float32)
        at = slice(row * TILE, (row + 1) * TILE)
        swap_ref[at] = got[:TILE]
        swap_ref[row * TILE + PIXELS : (row + 1) * TILE + PIXELS] = got[TILE : 2 * TILE]
        far_ref[row * REACHED : (row + 1) * REACHED] = got[2 * TILE : 2 * TILE + REACHED]
        o_0[row] = got[3 * TILE : 4 * TILE] + a_ref[0] * x_ref[at]
        near_ref[at] = got[4 * TILE :]

    params = with_rows(own_ref, m1[PIXELS:, :EXT], p1[PIXELS:, :EXT])
    for t in range(3):
        ext_ref[t] = params[t]
    to_right, to_left = border_columns(ext_ref, TILE - 2), border_columns(ext_ref, 0)
    swap_ref[2 * PIXELS : 2 * PIXELS + COMPS, :EXT] = jnp.where(odd == 0, to_right, to_left)
    swap_ref[2 * PIXELS + COMPS :, :EXT] = jnp.where(odd == 0, to_left, to_right)


def kept(x):
    return pltpu.with_memory_space_constraint(x, pltpu.VMEM)


def wavelet_parts(coeff, tiles, own, w, nch, length):
    k = jnp.asarray(scatter_matrices(length))
    vmem = pl.BlockSpec(memory_space=pltpu.VMEM)
    heights = (2 * (PIXELS + COMPS), PIXELS, FAR_ROWS)
    shapes = [(TILE, TILE, nch)] + [(n, nch) for n in heights] + [own.shape]
    return pl.pallas_call(
        wavelet_kernel,
        out_shape=[pltpu.VMEM(shape, jnp.float32) for shape in shapes],
        in_specs=[vmem] * 9,
        out_specs=[vmem] * 5,
        scratch_shapes=[
            pltpu.VMEM((LEVELS, TILE, TILE, nch), jnp.float32),
            pltpu.VMEM((TILE, 10 * TILE, nch), jnp.bfloat16),
        ],
        compiler_params=pltpu.CompilerParams(vmem_limit_bytes=VMEM_LIMIT),
        cost_estimate=pl.CostEstimate(flops=4_000_000_000, bytes_accessed=9_000_000, transcendentals=0),
        name="wavelet_parts",
    )(*[kept(x) for x in (coeff, *tiles, k, own, w)])


def add_kernel(near_ref, swapped_ref, out_ref):
    def body(row, carry):
        at = pl.ds(pl.multiple_of(row * TILE, TILE), TILE)
        more = pl.ds(pl.multiple_of(row * TILE + PIXELS, TILE), TILE)
        out_ref[at] = near_ref[at] + swapped_ref[more]
        return carry

    lax.fori_loop(0, TILE, body, 0, unroll=4)
    out_ref[PIXELS:, :] = swapped_ref[2 * PIXELS + COMPS :]


def outward(near, swapped):
    vmem = pl.BlockSpec(memory_space=pltpu.VMEM)
    return pl.pallas_call(
        add_kernel,
        out_shape=pltpu.VMEM((PIXELS + COMPS, near.shape[1]), jnp.float32),
        in_specs=[vmem] * 2,
        out_specs=vmem,
        compiler_params=pltpu.CompilerParams(vmem_limit_bytes=VMEM_LIMIT),
        cost_estimate=pl.CostEstimate(flops=100_000, bytes_accessed=1_500_000, transcendentals=0),
        name="outward",
    )(kept(near), kept(swapped))


def model_kernel(amp_ref, index_ref, spread_ref, w_hbm, model_ref, flat_ref, own_ref, w_ref, bump_ref, scale_ref, sem):
    load = pltpu.make_async_copy(w_hbm, w_ref, sem)
    load.start()
    nch, pixels = model_ref.shape
    own_ref[...] = jnp.zeros_like(own_ref)
    for t in range(3):
        for row in range(TILE):
            got = own_row(t, row, amp_ref, index_ref, spread_ref, nch)
            at = (row + 2) * PITCH
            own_ref[t, :, at : at + TILE] = got
            flat_ref[t, :, row * TILE : (row + 1) * TILE] = got
    mu = flat_ref[1] * float(nch)
    inv = 1.0 / flat_ref[2]
    flat_ref[1] = mu
    flat_ref[2] = inv
    scale_ref[...] = (-0.5 * math.log2(math.e)) * inv * inv

    def body(step, carry):
        base = pl.multiple_of(step * 8, 8)
        chan = (lax.broadcasted_iota(jnp.int32, (8, pixels), 0) + base).astype(jnp.float32)
        total = jnp.zeros((8, pixels), jnp.float32)
        for k in range(COMPS):
            diff = chan - flat_ref[1, k : k + 1, :]
            bump = jnp.exp2(diff * diff * scale_ref[k : k + 1, :])
            bump_ref[k, pl.ds(base, 8), :] = bump
            total += flat_ref[0, k : k + 1, :] * bump
        model_ref[pl.ds(base, 8), :] = total
        return carry

    lax.fori_loop(0, nch // 8, body, 0, unroll=2)
    load.wait()


def model_of(amplitude, centre_index, spread, nch):
    w = jnp.asarray(channel_matrices(nch))
    vmem = pl.BlockSpec(memory_space=pltpu.VMEM)
    pixels = TILE * TILE
    return pl.pallas_call(
        model_kernel,
        out_shape=[
            pltpu.VMEM((nch, pixels), jnp.float32),
            pltpu.VMEM((3, COMPS, pixels), jnp.float32),
            pltpu.VMEM((3, COMPS, EXT), jnp.float32),
            pltpu.VMEM(w.shape, w.dtype),
            pltpu.VMEM((COMPS, nch, pixels), jnp.float32),
        ],
        in_specs=[vmem] * 3 + [pl.BlockSpec(memory_space=pl.ANY)],
        out_specs=[vmem] * 5,
        scratch_shapes=[pltpu.VMEM((COMPS, pixels), jnp.float32), pltpu.SemaphoreType.DMA],
        compiler_params=pltpu.CompilerParams(vmem_limit_bytes=VMEM_LIMIT),
        cost_estimate=pl.CostEstimate(flops=10_000_000, bytes_accessed=1_000_000, transcendentals=1_100_000),
        name="gaussian_model",
    )(amplitude, centre_index, spread, pltpu.with_memory_space_constraint(w, pltpu.HBM))


def early_kernel(o_0, swapped_ref, far_ref, model_ref, part_ref, r_ref):
    nch, pixels = model_ref.shape
    even = lax.rem(lax.axis_index("skyx"), 2) == 0
    place = lax.broadcasted_iota(jnp.int32, (TILE, nch), 0)
    for row in range(TILE):
        far = far_ref[row * REACHED : row * REACHED + TILE]
        far = jnp.where(place < REACHED, far, 0.0)
        far = jnp.where(even, pltpu.roll(far, BEYOND, 0), far)
        part_ref[row] = (o_0[row] + swapped_ref[row * TILE : (row + 1) * TILE]) + far
    rows = LANES // TILE
    for part in range(pixels // LANES):
        block = part_ref[part * rows : (part + 1) * rows].reshape(LANES, nch)
        at = slice(part * LANES, (part + 1) * LANES)
        r_ref[:, at] = model_ref[:, at] - block.T


def early_part(o_0, swapped, far, model):
    vmem = pl.BlockSpec(memory_space=pltpu.VMEM)
    return pl.pallas_call(
        early_kernel,
        out_shape=[pltpu.VMEM(o_0.shape, jnp.float32), pltpu.VMEM(model.shape, jnp.float32)],
        in_specs=[vmem] * 4,
        out_specs=[vmem] * 2,
        compiler_params=pltpu.CompilerParams(vmem_limit_bytes=VMEM_LIMIT),
        cost_estimate=pl.CostEstimate(flops=2_000_000_000, bytes_accessed=9_000_000, transcendentals=0),
        name="early_part",
    )(*[kept(x) for x in (o_0, swapped, far, model)])


def step_kernel(
    part_ref, early_ref, swapped_ref, near_ref, bump_ref, flat_ref, ext_ref,
    den_hbm, fit_ref, den_ref, r_ref, sem,
):
    nch, pixels = early_ref.shape
    rows = LANES // TILE
    parts = pixels // LANES
    copies = []
    inner, outer = swapped_ref[2 * PIXELS : 2 * PIXELS + COMPS, :EXT], near_ref[PIXELS:, :EXT]
    even = lax.rem(lax.axis_index("skyx"), 2) == 0
    left, right = jnp.where(even, outer, inner), jnp.where(even, inner, outer)
    bases = smoothed([ext_ref[t] for t in range(3)], left, right)
    for part in range(parts):
        at = slice(part * rows, (part + 1) * rows)
        for row in range(part * rows, (part + 1) * rows):
            flat = slice(row * TILE, (row + 1) * TILE)
            den_ref[row] = part_ref[row] + near_ref[flat]
        copies.append(pltpu.make_async_copy(den_ref.at[at], den_hbm.at[at], sem.at[part]))
        copies[-1].start()

    shape = (COMPS, rows, LANES)
    own_lanes = lax.broadcasted_iota(jnp.int32, shape, 2) // TILE == lax.broadcasted_iota(jnp.int32, shape, 1)
    for part in range(parts):
        at = slice(part * LANES, (part + 1) * LANES)
        r_ref[:, at] = early_ref[:, at] - near_ref[at].T

    for part in range(parts):
        at = slice(part * LANES, (part + 1) * LANES)
        sums = [[] for _ in range(3)]
        for first in range(0, COMPS, 4):
            chosen = range(first, first + 4)
            mus = [jnp.broadcast_to(flat_ref[1, k : k + 1, at], (8, LANES)) for k in chosen]

            def body(step, carry):
                base = pl.multiple_of(step * 8, 8)
                chan = (lax.broadcasted_iota(jnp.int32, (8, LANES), 0) + base).astype(jnp.float32)
                r = r_ref[pl.ds(base, 8), at]
                out = []
                for k, mu, (a, b, c) in zip(chosen, mus, carry):
                    diff = chan - mu
                    one = r * bump_ref[k, pl.ds(base, 8), at]
                    two = one * diff
                    out.append((a + one, b + two, c + two * diff))
                return tuple(out)

            zero = jnp.zeros((8, LANES), jnp.float32)
            done = lax.fori_loop(0, nch // 8, body, ((zero,) * 3,) * 4, unroll=16)
            for four in done:
                for t in range(3):
                    sums[t].append(jnp.sum(four[t], axis=0, keepdims=True))
        amp = flat_ref[0, :, at]
        inv = flat_ref[2, :, at]
        slope = amp * inv * inv
        grads = (
            jnp.concatenate(sums[0], axis=0) * (1.0 / nch),
            jnp.concatenate(sums[1], axis=0) * slope,
            jnp.concatenate(sums[2], axis=0) * (slope * inv * (1.0 / nch)),
        )
        for t in range(3):
            new = bases[t][:, at] - STEPS[t] * grads[t]
            spread_out = jnp.where(own_lanes, jnp.broadcast_to(new[:, None, :], own_lanes.shape), 0.0)
            for shift in (LANES // 2, LANES // 4, LANES // 8):
                spread_out = spread_out + pltpu.roll(spread_out, shift, 2)
            fit_ref[t, :, part * rows : (part + 1) * rows, :] = spread_out[:, :, :TILE]

    for copy in copies:
        copy.wait()


def gradient_step(part, early, swapped, near, bump, flat, ext):
    vmem = pl.BlockSpec(memory_space=pltpu.VMEM)
    shape = part.shape
    return pl.pallas_call(
        step_kernel,
        out_shape=[
            jax.ShapeDtypeStruct(shape, jnp.float32),
            jax.ShapeDtypeStruct((3, COMPS, TILE, TILE), jnp.float32),
        ],
        in_specs=[vmem] * 7,
        out_specs=[pl.BlockSpec(memory_space=pl.ANY), vmem],
        scratch_shapes=[
            pltpu.VMEM(shape, jnp.float32),
            pltpu.VMEM(early.shape, jnp.float32),
            pltpu.SemaphoreType.DMA((2,)),
        ],
        compiler_params=pltpu.CompilerParams(vmem_limit_bytes=VMEM_LIMIT),
        cost_estimate=pl.CostEstimate(flops=15_000_000, bytes_accessed=4_000_000, transcendentals=1_100_000),
        name="gradient_step",
    )(*[kept(x) for x in (part, early, swapped, near, bump, flat, ext)])


def on_device(cube, level_table, level_index, amplitude, centre_index, spread):
    nch = cube.shape[2]
    size = lax.axis_size("skyx")
    partner = [(i, i ^ 1) for i in range(size)]

    tile = packed(cube.reshape(PIXELS, nch), amplitude, centre_index, spread)
    up1, down1 = sent(tile, "skyy", 1), sent(tile, "skyy", -1)
    up2, down2 = sent(cube[BEYOND:], "skyy", 2), sent(cube[:-BEYOND], "skyy", -2)

    entries = jnp.arange(level_table.shape[0], dtype=jnp.int32)
    picks = (level_index[:, :, None] == entries).astype(jnp.float32)
    weight = jnp.sum(picks * level_table, axis=2)
    one = jnp.ones((1, nch), jnp.float32)
    coeff = jnp.concatenate([weight, one]) - jnp.concatenate([0.0 * one, weight])
    scale = jnp.array([16.0 ** (-3 * j) for j in range(LEVELS + 1)], jnp.float32)
    coeff = (coeff * scale[:, None])[:, None, :]
    model, flat, own, w, bump = model_of(amplitude, centre_index, spread, nch)
    o_0, swap, near, far, ext = wavelet_parts(coeff, (up1, down1, up2, down2, tile), own, w, nch, size * TILE)

    swapped = lax.ppermute(swap, "skyx", partner)
    far = away(far, "skyx", 2)
    near = away(outward(near, swapped), "skyx", -2)
    part, early = early_part(o_0, swapped, far, model)
    return gradient_step(part, early, swapped, near, bump, flat, ext)


def solution(mesh):
    placed = (
        P("skyy", "skyx", None),
        P(),
        P(),
        P(None, "skyy", "skyx"),
        P(None, "skyy", "skyx"),
        P(None, "skyy", "skyx"),
    )
    return jax.shard_map(
        on_device,
        mesh=mesh,
        in_specs=placed,
        out_specs=(P("skyy", "skyx", None), P(None, None, "skyy", "skyx")),
        check_vma=False,
    )
```

```python
import functools
import math

import jax
import jax.numpy as jnp
import numpy as np
from jax import lax
from jax.experimental import pallas as pl
from jax.experimental.pallas import tpu as pltpu
from jax.sharding import PartitionSpec as P

TILE = 16
LEVELS = 4
COMPS = 8
LANES = 128
TAPS = (1, 4, 6, 4, 1)
BEYOND = 2
REACHED = TILE - BEYOND
FAR_ROWS = TILE * REACHED + 8
VMEM_LIMIT = 20 * 1024 * 1024
ROLES = ((3, 1, 0, 2, 4), (1, 3, 4, 2, 0))
PIXELS = TILE * TILE
PITCH = TILE
EXT = 384
OWN = 2 * PITCH
FIRST_ROWS = 128
STEPS = (0.5, 0.002, 2.0)
LAMS = (0.2, 0.5, 0.05)


def blur_matrix(length, gap):
    out = np.zeros((length, length), np.float64)
    for tap, factor in enumerate(TAPS):
        offset = (tap - 2) * gap
        for i in range(max(0, -offset), min(length, length - offset)):
            out[i, i + offset] = factor
    return out


def composites(length):
    made, now = [], np.eye(length)
    for level in range(LEVELS):
        now = blur_matrix(length, 2**level) @ now
        made.append(now)
    return made


def halves(matrix):
    bf16 = jnp.bfloat16
    high = np.asarray(matrix, np.float32).astype(bf16)
    low = (np.asarray(matrix, np.float32) - high.astype(np.float32)).astype(bf16)
    return high, low


def channel_matrices(nch):
    parts = [halves(m.T) for m in composites(nch)]
    half, quarter = nch // 2, nch // 4
    out = []
    for whole in [p[0] for p in parts] + [p[1] for p in parts[2:]]:
        across = whole[quarter : quarter + half, quarter : quarter + half].copy()
        across[:quarter, :quarter] = 0
        across[quarter:, quarter:] = 0
        out.append(np.stack([whole[:half, :half], across, whole[half:, half:]]))
    return np.stack(out)


def scatter_matrices(length):
    whole = composites(length)
    kinds = []
    for start in (0, TILE * (length // TILE // 2), length - TILE):
        parts = []
        for m in whole:
            block = np.zeros((5 * TILE, TILE))
            for k in range(5 * TILE):
                at = start - 2 * TILE + k
                if 0 <= at < length:
                    block[k] = m[at, start : start + TILE]
            parts.append(halves(block))
        high = np.concatenate([p[0] for p in parts], axis=1)
        low = np.concatenate([p[1] for p in parts[2:]], axis=1)
        columns = np.concatenate([high, high, low], axis=1).reshape(5, TILE, -1)
        for order in ROLES:
            blocks = [columns[i] for i in order]
            if order[2] == 0:
                blocks[2] = np.roll(blocks[2], -BEYOND, axis=0)
            kinds.append(np.concatenate(blocks))
    return np.stack(kinds)


def sent(values, axis, by):
    size = lax.axis_size(axis)
    if by > 0:
        pairs = [(i, i + by) for i in range(size - by)]
    else:
        pairs = [(i, i + by) for i in range(-by, size)]
    return lax.ppermute(values, axis, pairs)


def away(values, axis, by):
    size = lax.axis_size(axis)
    pairs = [(i, i + by if i % 2 else i - by) for i in range(size)]
    return lax.ppermute(values, axis, [(i, j) for i, j in pairs if 0 <= j < size])


def own_row(t, row, amp_ref, index_ref, spread_ref, nch):
    if t == 0:
        return amp_ref[:, row, :]
    if t == 1:
        return (index_ref[:, row, :].astype(jnp.float32) + 0.5) * (1.0 / nch)
    return spread_ref[:, row, :]


def pack_kernel(cube_hbm, amp_hbm, index_hbm, spread_hbm, out_ref, amp_ref, index_ref, spread_ref, sem):
    pairs = ((amp_hbm, amp_ref), (index_hbm, index_ref), (spread_hbm, spread_ref), (cube_hbm, out_ref.at[0:PIXELS]))
    copies = [pltpu.make_async_copy(a, b, sem.at[i]) for i, (a, b) in enumerate(pairs)]
    for copy in copies:
        copy.start()
    nch = cube_hbm.shape[1]
    out_ref[PIXELS:, :] = jnp.zeros((COMPS, nch), jnp.float32)
    for copy in copies[:3]:
        copy.wait()
    for start, first in ((0, TILE - 2), (FIRST_ROWS, 0)):
        for t in range(3):
            for r in range(2):
                lane = start + (2 * t + r) * PITCH
                got = own_row(t, first + r, amp_ref, index_ref, spread_ref, nch)
                out_ref[PIXELS:, lane : lane + TILE] = got
    copies[3].wait()


def packed(cube, amplitude, centre_index, spread):
    hbm = [pltpu.with_memory_space_constraint(v, pltpu.HBM) for v in (cube, amplitude, centre_index, spread)]
    return pl.pallas_call(
        pack_kernel,
        out_shape=pltpu.VMEM((PIXELS + COMPS, cube.shape[1]), jnp.float32),
        in_specs=[pl.BlockSpec(memory_space=pl.ANY)] * 4,
        out_specs=pl.BlockSpec(memory_space=pltpu.VMEM),
        scratch_shapes=[pltpu.VMEM(v.shape, v.dtype) for v in hbm[1:]] + [pltpu.SemaphoreType.DMA((4,))],
        compiler_params=pltpu.CompilerParams(vmem_limit_bytes=VMEM_LIMIT),
        cost_estimate=pl.CostEstimate(flops=1000, bytes_accessed=1_000_000, transcendentals=0),
        name="pack",
    )(*hbm)


def border_columns(ext_ref, shift):
    lane = lax.broadcasted_iota(jnp.int32, (COMPS, EXT), 1) % PITCH
    total = jnp.zeros((COMPS, EXT), jnp.float32)
    for t in range(3):
        moved = pltpu.roll(ext_ref[t], (2 * t - shift) % EXT, 1)
        total = jnp.where((lane >= 2 * t) & (lane < 2 * t + 2), moved, total)
    return total


def with_rows(own, above, below):
    row = lax.broadcasted_iota(jnp.int32, (COMPS, EXT), 1) // PITCH
    out = []
    for t in range(3):
        p = jnp.where(row < 2, pltpu.roll(above, (EXT - 2 * t * PITCH) % EXT, 1), own[t])
        out.append(jnp.where(row >= TILE + 2, pltpu.roll(below, ((TILE + 2 - 2 * t) * PITCH - FIRST_ROWS) % EXT, 1), p))
    return out


def up_and_down(p):
    return pltpu.roll(p, PITCH, 1) + pltpu.roll(p, EXT - PITCH, 1)


def smoothed(params, left, right):
    lane = lax.broadcasted_iota(jnp.int32, (COMPS, EXT), 1)
    column = lane % PITCH
    at_left, at_right = column == 0, column == TILE - 1
    y = lane // PITCH + (lax.axis_index("skyy") * TILE - 2)
    on_sky = (y >= 0) & (y < lax.axis_size("skyy") * TILE)
    ix = lax.axis_index("skyx")
    beside = on_sky & ((at_left & (ix > 0)) | (at_right & (ix < lax.axis_size("skyx") - 1)))

    def laplacian(p, side):
        before = jnp.where(at_left, side, pltpu.roll(p, 1, 1))
        after = jnp.where(at_right, side, pltpu.roll(p, EXT - 1, 1))
        return 4.0 * p - ((before + after) + up_and_down(p))

    out = []
    for t, p in enumerate(params):
        lefts = [pltpu.roll(left, (EXT - 2 * t - 1 + i) % EXT, 1) for i in range(2)]
        rights = [pltpu.roll(right, (TILE - 1 - 2 * t - i) % EXT, 1) for i in range(2)]
        one, two = [jnp.where(at_left, a, b) for a, b in zip(lefts, rights)]
        first = jnp.where(on_sky, laplacian(p, one), 0.0)
        first_beside = jnp.where(beside, 4.0 * one - ((two + p) + up_and_down(one)), 0.0)
        new = p - (STEPS[t] * LAMS[t]) * laplacian(first, first_beside)
        out.append(pltpu.roll(new, EXT - OWN, 1)[:, :PIXELS])
    return out


def five(v, flag=None):
    total = (v[0] + v[4]) + 4.0 * (v[1] + v[3]) + 6.0 * v[2]
    return total if flag is None else total * flag


def split(v):
    high = v.astype(jnp.bfloat16)
    return high, (v - high.astype(jnp.float32)).astype(jnp.bfloat16)


def column_kind():
    ix = lax.axis_index("skyx")
    kind = jnp.where(ix == 0, 0, jnp.where(ix == lax.axis_size("skyx") - 1, 2, 1))
    return 2 * kind + lax.rem(ix, 2)


def wavelet_kernel(
    a_ref, inside_ref, outside_ref, m2, p2, x_ref, k_ref, own_ref, w_ref,
    o_0, swap_ref, near_ref, far_ref, ext_ref, rows_ref, y_ref,
):
    nch = x_ref.shape[1]
    iy, ix = lax.axis_index("skyy"), lax.axis_index("skyx")
    near = [iy + i for i in (-2, -1, 0, 1, 2)]
    flags = [jnp.where((i >= 0) & (i < lax.axis_size("skyy")), 1.0, 0.0) for i in near]

    lane_tiles = nch // LANES

    def row_pass(tiles, step, carry):
        sub = pl.ds(pl.multiple_of((step // lane_tiles) * 8, 8), 8)
        lane = pl.ds(pl.multiple_of((step % lane_tiles) * LANES, LANES), LANES)

        @functools.cache
        def value(level, at):
            tile = (at + 2 * TILE) // TILE
            if level == 0:
                if tile in (1, 2, 3):
                    start = pl.multiple_of(at % TILE * TILE + step // lane_tiles * 8, 8)
                    return tiles[tile][pl.ds(start, 8), lane]
                return tiles[tile][at % TILE - (BEYOND if tile == 0 else 0), sub, lane]
            gap = 2 ** (level - 1)
            taps = [value(level - 1, at + (t - 2) * gap) for t in range(5)]
            return five(taps, None if tile == 2 else flags[tile])

        reach = {1: 28, 2: 24, 3: 16, 4: 0}
        lag = {1: 2, 2: 6, 3: 14, 4: 30}
        for at in range(-30, TILE + 30):
            value(0, at)
            for level in range(1, LEVELS + 1):
                row = at - lag[level]
                if -reach[level] <= row < TILE + reach[level]:
                    got = value(level, row)
                    if 0 <= row < TILE:
                        rows_ref[level - 1, row, sub, lane] = got
        return carry

    even_row = lax.rem(iy, 2) == 0

    @pl.when(even_row)
    def _():
        tiles = (m2, outside_ref, x_ref, inside_ref, p2)
        lax.fori_loop(0, 2 * lane_tiles, functools.partial(row_pass, tiles), 0)

    @pl.when(jnp.logical_not(even_row))
    def _():
        tiles = (m2, inside_ref, x_ref, outside_ref, p2)
        lax.fori_loop(0, 2 * lane_tiles, functools.partial(row_pass, tiles), 0)


    half, quarter = nch // 2, nch // 4

    for level in range(LEVELS):
        high, low = split(rows_ref[level].reshape(PIXELS, nch))
        parts, index = [high, low], [level, level]
        if level >= 2:
            parts, index = parts + [high], index + [level + 2]
        first, middle, last = [
            jnp.dot(
                jnp.concatenate([v[:, at : at + half] for v in parts], axis=1),
                jnp.concatenate([w_ref[j, i] for j in index], axis=0),
                preferred_element_type=jnp.float32,
            )
            for i, at in enumerate((0, quarter, half))
        ]
        pieces = (
            first[:, :quarter],
            first[:, quarter:] + middle[:, :quarter],
            middle[:, quarter:] + last[:, :quarter],
            last[:, quarter:],
        )
        for i, piece in enumerate(pieces):
            lane = slice(i * quarter, (i + 1) * quarter)
            high, low = split(piece * a_ref[level + 1, :, lane])
            high = high.reshape(TILE, TILE, quarter)
            y_ref[:, level * TILE : (level + 1) * TILE, lane] = high
            at = (level + LEVELS) * TILE
            y_ref[:, at : at + TILE, lane] = low.reshape(TILE, TILE, quarter)
            if level >= 2:
                at = (level + 6) * TILE
                y_ref[:, at : at + TILE, lane] = high

    odd = lax.rem(ix, 2)
    columns = k_ref[column_kind()]

    for row in range(TILE):
        got = jnp.dot(columns, y_ref[row], preferred_element_type=jnp.float32)
        at = slice(row * TILE, (row + 1) * TILE)
        swap_ref[at] = got[:TILE]
        swap_ref[row * TILE + PIXELS : (row + 1) * TILE + PIXELS] = got[TILE : 2 * TILE]
        far_ref[row * REACHED : (row + 1) * REACHED] = got[2 * TILE : 2 * TILE + REACHED]
        o_0[row] = got[3 * TILE : 4 * TILE] + a_ref[0] * x_ref[at]
        near_ref[at] = got[4 * TILE :]

    inside, outside = inside_ref[PIXELS:, :EXT], outside_ref[PIXELS:, :EXT]
    above, below = jnp.where(even_row, outside, inside), jnp.where(even_row, inside, outside)
    params = with_rows(own_ref, above, below)
    for t in range(3):
        ext_ref[t] = params[t]
    to_right, to_left = border_columns(ext_ref, TILE - 2), border_columns(ext_ref, 0)
    swap_ref[2 * PIXELS : 2 * PIXELS + COMPS, :EXT] = jnp.where(odd == 0, to_right, to_left)
    swap_ref[2 * PIXELS + COMPS :, :EXT] = jnp.where(odd == 0, to_left, to_right)


def kept(x):
    return pltpu.with_memory_space_constraint(x, pltpu.VMEM)


def wavelet_parts(coeff, tiles, own, w, nch, length):
    k = jnp.asarray(scatter_matrices(length))
    vmem = pl.BlockSpec(memory_space=pltpu.VMEM)
    heights = (2 * (PIXELS + COMPS), PIXELS, FAR_ROWS)
    shapes = [(TILE, TILE, nch)] + [(n, nch) for n in heights] + [own.shape]
    return pl.pallas_call(
        wavelet_kernel,
        out_shape=[pltpu.VMEM(shape, jnp.float32) for shape in shapes],
        in_specs=[vmem] * 9,
        out_specs=[vmem] * 5,
        scratch_shapes=[
            pltpu.VMEM((LEVELS, TILE, TILE, nch), jnp.float32),
            pltpu.VMEM((TILE, 10 * TILE, nch), jnp.bfloat16),
        ],
        compiler_params=pltpu.CompilerParams(vmem_limit_bytes=VMEM_LIMIT),
        cost_estimate=pl.CostEstimate(flops=4_000_000_000, bytes_accessed=9_000_000, transcendentals=0),
        name="wavelet_parts",
    )(*[kept(x) for x in (coeff, *tiles, k, own, w)])


def add_kernel(near_ref, swapped_ref, out_ref):
    def body(row, carry):
        at = pl.ds(pl.multiple_of(row * TILE, TILE), TILE)
        more = pl.ds(pl.multiple_of(row * TILE + PIXELS, TILE), TILE)
        out_ref[at] = near_ref[at] + swapped_ref[more]
        return carry

    lax.fori_loop(0, TILE, body, 0, unroll=4)
    out_ref[PIXELS:, :] = swapped_ref[2 * PIXELS + COMPS :]


def outward(near, swapped):
    vmem = pl.BlockSpec(memory_space=pltpu.VMEM)
    return pl.pallas_call(
        add_kernel,
        out_shape=pltpu.VMEM((PIXELS + COMPS, near.shape[1]), jnp.float32),
        in_specs=[vmem] * 2,
        out_specs=vmem,
        compiler_params=pltpu.CompilerParams(vmem_limit_bytes=VMEM_LIMIT),
        cost_estimate=pl.CostEstimate(flops=100_000, bytes_accessed=1_500_000, transcendentals=0),
        name="outward",
    )(kept(near), kept(swapped))


def model_kernel(amp_ref, index_ref, spread_ref, w_hbm, model_ref, flat_ref, own_ref, w_ref, bump_ref, scale_ref, sem):
    load = pltpu.make_async_copy(w_hbm, w_ref, sem)
    load.start()
    nch, pixels = model_ref.shape
    own_ref[...] = jnp.zeros_like(own_ref)
    for t in range(3):
        for row in range(TILE):
            got = own_row(t, row, amp_ref, index_ref, spread_ref, nch)
            at = (row + 2) * PITCH
            own_ref[t, :, at : at + TILE] = got
            flat_ref[t, :, row * TILE : (row + 1) * TILE] = got
    mu = flat_ref[1] * float(nch)
    inv = 1.0 / flat_ref[2]
    flat_ref[1] = mu
    flat_ref[2] = inv
    scale_ref[...] = (-0.5 * math.log2(math.e)) * inv * inv

    def body(step, carry):
        base = pl.multiple_of(step * 8, 8)
        chan = (lax.broadcasted_iota(jnp.int32, (8, pixels), 0) + base).astype(jnp.float32)
        total = jnp.zeros((8, pixels), jnp.float32)
        for k in range(COMPS):
            diff = chan - flat_ref[1, k : k + 1, :]
            bump = jnp.exp2(diff * diff * scale_ref[k : k + 1, :])
            bump_ref[k, pl.ds(base, 8), :] = bump
            total += flat_ref[0, k : k + 1, :] * bump
        model_ref[pl.ds(base, 8), :] = total
        return carry

    lax.fori_loop(0, nch // 8, body, 0, unroll=2)
    load.wait()


def model_of(amplitude, centre_index, spread, nch):
    w = jnp.asarray(channel_matrices(nch))
    vmem = pl.BlockSpec(memory_space=pltpu.VMEM)
    pixels = TILE * TILE
    return pl.pallas_call(
        model_kernel,
        out_shape=[
            pltpu.VMEM((nch, pixels), jnp.float32),
            pltpu.VMEM((3, COMPS, pixels), jnp.float32),
            pltpu.VMEM((3, COMPS, EXT), jnp.float32),
            pltpu.VMEM(w.shape, w.dtype),
            pltpu.VMEM((COMPS, nch, pixels), jnp.float32),
        ],
        in_specs=[vmem] * 3 + [pl.BlockSpec(memory_space=pl.ANY)],
        out_specs=[vmem] * 5,
        scratch_shapes=[pltpu.VMEM((COMPS, pixels), jnp.float32), pltpu.SemaphoreType.DMA],
        compiler_params=pltpu.CompilerParams(vmem_limit_bytes=VMEM_LIMIT),
        cost_estimate=pl.CostEstimate(flops=10_000_000, bytes_accessed=1_000_000, transcendentals=1_100_000),
        name="gaussian_model",
    )(amplitude, centre_index, spread, pltpu.with_memory_space_constraint(w, pltpu.HBM))


def early_kernel(o_0, swapped_ref, far_ref, model_ref, part_ref, r_ref):
    nch, pixels = model_ref.shape
    even = lax.rem(lax.axis_index("skyx"), 2) == 0
    place = lax.broadcasted_iota(jnp.int32, (TILE, nch), 0)
    for row in range(TILE):
        far = far_ref[row * REACHED : row * REACHED + TILE]
        far = jnp.where(place < REACHED, far, 0.0)
        far = jnp.where(even, pltpu.roll(far, BEYOND, 0), far)
        part_ref[row] = (o_0[row] + swapped_ref[row * TILE : (row + 1) * TILE]) + far
    rows = LANES // TILE
    for part in range(pixels // LANES):
        block = part_ref[part * rows : (part + 1) * rows].reshape(LANES, nch)
        at = slice(part * LANES, (part + 1) * LANES)
        r_ref[:, at] = model_ref[:, at] - block.T


def early_part(o_0, swapped, far, model):
    vmem = pl.BlockSpec(memory_space=pltpu.VMEM)
    return pl.pallas_call(
        early_kernel,
        out_shape=[pltpu.VMEM(o_0.shape, jnp.float32), pltpu.VMEM(model.shape, jnp.float32)],
        in_specs=[vmem] * 4,
        out_specs=[vmem] * 2,
        compiler_params=pltpu.CompilerParams(vmem_limit_bytes=VMEM_LIMIT),
        cost_estimate=pl.CostEstimate(flops=2_000_000_000, bytes_accessed=9_000_000, transcendentals=0),
        name="early_part",
    )(*[kept(x) for x in (o_0, swapped, far, model)])


def step_kernel(
    part_ref, early_ref, swapped_ref, near_ref, bump_ref, flat_ref, ext_ref,
    den_hbm, fit_ref, den_ref, r_ref, sem,
):
    nch, pixels = early_ref.shape
    rows = LANES // TILE
    parts = pixels // LANES
    copies = []
    inner, outer = swapped_ref[2 * PIXELS : 2 * PIXELS + COMPS, :EXT], near_ref[PIXELS:, :EXT]
    even = lax.rem(lax.axis_index("skyx"), 2) == 0
    left, right = jnp.where(even, outer, inner), jnp.where(even, inner, outer)
    bases = smoothed([ext_ref[t] for t in range(3)], left, right)
    for part in range(parts):
        at = slice(part * rows, (part + 1) * rows)
        for row in range(part * rows, (part + 1) * rows):
            flat = slice(row * TILE, (row + 1) * TILE)
            den_ref[row] = part_ref[row] + near_ref[flat]
        copies.append(pltpu.make_async_copy(den_ref.at[at], den_hbm.at[at], sem.at[part]))
        copies[-1].start()

    shape = (COMPS, rows, LANES)
    own_lanes = lax.broadcasted_iota(jnp.int32, shape, 2) // TILE == lax.broadcasted_iota(jnp.int32, shape, 1)
    for part in range(parts):
        at = slice(part * LANES, (part + 1) * LANES)
        r_ref[:, at] = early_ref[:, at] - near_ref[at].T

    for part in range(parts):
        at = slice(part * LANES, (part + 1) * LANES)
        sums = [[] for _ in range(3)]
        for first in range(0, COMPS, 8):
            chosen = range(first, first + 8)
            mus = [jnp.broadcast_to(flat_ref[1, k : k + 1, at], (8, LANES)) for k in chosen]

            def body(step, carry):
                base = pl.multiple_of(step * 8, 8)
                chan = (lax.broadcasted_iota(jnp.int32, (8, LANES), 0) + base).astype(jnp.float32)
                r = r_ref[pl.ds(base, 8), at]
                out = []
                for k, mu, (a, b, c) in zip(chosen, mus, carry):
                    diff = chan - mu
                    one = r * bump_ref[k, pl.ds(base, 8), at]
                    two = one * diff
                    out.append((a + one, b + two, c + two * diff))
                return tuple(out)

            zero = jnp.zeros((8, LANES), jnp.float32)
            done = lax.fori_loop(0, nch // 8, body, ((zero,) * 3,) * 8, unroll=16)
            for sums_of_one in done:
                for t in range(3):
                    sums[t].append(jnp.sum(sums_of_one[t], axis=0, keepdims=True))
        amp = flat_ref[0, :, at]
        inv = flat_ref[2, :, at]
        slope = amp * inv * inv
        grads = (
            jnp.concatenate(sums[0], axis=0) * (1.0 / nch),
            jnp.concatenate(sums[1], axis=0) * slope,
            jnp.concatenate(sums[2], axis=0) * (slope * inv * (1.0 / nch)),
        )
        for t in range(3):
            new = bases[t][:, at] - STEPS[t] * grads[t]
            spread_out = jnp.where(own_lanes, jnp.broadcast_to(new[:, None, :], own_lanes.shape), 0.0)
            for shift in (LANES // 2, LANES // 4, LANES // 8):
                spread_out = spread_out + pltpu.roll(spread_out, shift, 2)
            fit_ref[t, :, part * rows : (part + 1) * rows, :] = spread_out[:, :, :TILE]

    for copy in copies:
        copy.wait()


def gradient_step(part, early, swapped, near, bump, flat, ext):
    vmem = pl.BlockSpec(memory_space=pltpu.VMEM)
    shape = part.shape
    return pl.pallas_call(
        step_kernel,
        out_shape=[
            jax.ShapeDtypeStruct(shape, jnp.float32),
            jax.ShapeDtypeStruct((3, COMPS, TILE, TILE), jnp.float32),
        ],
        in_specs=[vmem] * 7,
        out_specs=[pl.BlockSpec(memory_space=pl.ANY), vmem],
        scratch_shapes=[
            pltpu.VMEM(shape, jnp.float32),
            pltpu.VMEM(early.shape, jnp.float32),
            pltpu.SemaphoreType.DMA((2,)),
        ],
        compiler_params=pltpu.CompilerParams(vmem_limit_bytes=VMEM_LIMIT),
        cost_estimate=pl.CostEstimate(flops=15_000_000, bytes_accessed=4_000_000, transcendentals=1_100_000),
        name="gradient_step",
    )(*[kept(x) for x in (part, early, swapped, near, bump, flat, ext)])


def on_device(cube, level_table, level_index, amplitude, centre_index, spread):
    nch = cube.shape[2]
    size = lax.axis_size("skyx")
    partner = [(i, i ^ 1) for i in range(size)]

    tile = packed(cube.reshape(PIXELS, nch), amplitude, centre_index, spread)
    inside = lax.ppermute(tile, "skyy", [(i, i ^ 1) for i in range(lax.axis_size("skyy"))])
    outside = away(tile, "skyy", 1)
    up2, down2 = sent(cube[BEYOND:], "skyy", 2), sent(cube[:-BEYOND], "skyy", -2)

    entries = jnp.arange(level_table.shape[0], dtype=jnp.int32)
    picks = (level_index[:, :, None] == entries).astype(jnp.float32)
    weight = jnp.sum(picks * level_table, axis=2)
    one = jnp.ones((1, nch), jnp.float32)
    coeff = jnp.concatenate([weight, one]) - jnp.concatenate([0.0 * one, weight])
    scale = jnp.array([16.0 ** (-3 * j) for j in range(LEVELS + 1)], jnp.float32)
    coeff = (coeff * scale[:, None])[:, None, :]
    model, flat, own, w, bump = model_of(amplitude, centre_index, spread, nch)
    o_0, swap, near, far, ext = wavelet_parts(coeff, (inside, outside, up2, down2, tile), own, w, nch, size * TILE)

    swapped = lax.ppermute(swap, "skyx", partner)
    far = away(far, "skyx", 2)
    near = away(outward(near, swapped), "skyx", -2)
    part, early = early_part(o_0, swapped, far, model)
    return gradient_step(part, early, swapped, near, bump, flat, ext)


def solution(mesh):
    placed = (
        P("skyy", "skyx", None),
        P(),
        P(),
        P(None, "skyy", "skyx"),
        P(None, "skyy", "skyx"),
        P(None, "skyy", "skyx"),
    )
    return jax.shard_map(
        on_device,
        mesh=mesh,
        in_specs=placed,
        out_specs=(P("skyy", "skyx", None), P(None, None, "skyy", "skyx")),
        check_vma=False,
    )
```

```python
import functools
import math

import jax
import jax.numpy as jnp
import numpy as np
from jax import lax
from jax.experimental import pallas as pl
from jax.experimental.pallas import tpu as pltpu
from jax.sharding import PartitionSpec as P

TILE = 16
LEVELS = 4
COMPS = 8
LANES = 128
TAPS = (1, 4, 6, 4, 1)
BEYOND = 2
REACHED = TILE - BEYOND
FAR_ROWS = TILE * REACHED + 8
VMEM_LIMIT = 20 * 1024 * 1024
ROLES = ((3, 1, 0, 2, 4), (1, 3, 4, 2, 0))
PIXELS = TILE * TILE
PITCH = TILE
EXT = 384
OWN = 2 * PITCH
FIRST_ROWS = 128
STEPS = (0.5, 0.002, 2.0)
LAMS = (0.2, 0.5, 0.05)


def blur_matrix(length, gap):
    out = np.zeros((length, length), np.float64)
    for tap, factor in enumerate(TAPS):
        offset = (tap - 2) * gap
        for i in range(max(0, -offset), min(length, length - offset)):
            out[i, i + offset] = factor
    return out


def composites(length):
    made, now = [], np.eye(length)
    for level in range(LEVELS):
        now = blur_matrix(length, 2**level) @ now
        made.append(now)
    return made


def halves(matrix):
    bf16 = jnp.bfloat16
    high = np.asarray(matrix, np.float32).astype(bf16)
    low = (np.asarray(matrix, np.float32) - high.astype(np.float32)).astype(bf16)
    return high, low


def channel_matrices(nch):
    parts = [halves(m.T) for m in composites(nch)]
    half, quarter = nch // 2, nch // 4
    out = []
    for whole in [p[0] for p in parts] + [p[1] for p in parts[2:]]:
        across = whole[quarter : quarter + half, quarter : quarter + half].copy()
        across[:quarter, :quarter] = 0
        across[quarter:, quarter:] = 0
        out.append(np.stack([whole[:half, :half], across, whole[half:, half:]]))
    return np.stack(out)


def scatter_matrices(length):
    whole = composites(length)
    kinds = []
    for start in (0, TILE * (length // TILE // 2), length - TILE):
        parts = []
        for m in whole:
            block = np.zeros((5 * TILE, TILE))
            for k in range(5 * TILE):
                at = start - 2 * TILE + k
                if 0 <= at < length:
                    block[k] = m[at, start : start + TILE]
            parts.append(halves(block))
        high = np.concatenate([p[0] for p in parts], axis=1)
        low = np.concatenate([p[1] for p in parts[2:]], axis=1)
        columns = np.concatenate([high, high, low], axis=1).reshape(5, TILE, -1)
        for order in ROLES:
            blocks = [columns[i] for i in order]
            if order[2] == 0:
                blocks[2] = np.roll(blocks[2], -BEYOND, axis=0)
            kinds.append(np.concatenate(blocks))
    return np.stack(kinds)


def sent(values, axis, by):
    size = lax.axis_size(axis)
    if by > 0:
        pairs = [(i, i + by) for i in range(size - by)]
    else:
        pairs = [(i, i + by) for i in range(-by, size)]
    return lax.ppermute(values, axis, pairs)


def away(values, axis, by):
    size = lax.axis_size(axis)
    pairs = [(i, i + by if i % 2 else i - by) for i in range(size)]
    return lax.ppermute(values, axis, [(i, j) for i, j in pairs if 0 <= j < size])


def own_row(t, row, amp_ref, index_ref, spread_ref, nch):
    if t == 0:
        return amp_ref[:, row, :]
    if t == 1:
        return (index_ref[:, row, :].astype(jnp.float32) + 0.5) * (1.0 / nch)
    return spread_ref[:, row, :]


def pack_kernel(cube_hbm, amp_hbm, index_hbm, spread_hbm, out_ref, amp_ref, index_ref, spread_ref, sem):
    pairs = ((amp_hbm, amp_ref), (index_hbm, index_ref), (spread_hbm, spread_ref), (cube_hbm, out_ref.at[0:PIXELS]))
    copies = [pltpu.make_async_copy(a, b, sem.at[i]) for i, (a, b) in enumerate(pairs)]
    for copy in copies:
        copy.start()
    nch = cube_hbm.shape[1]
    out_ref[PIXELS:, :] = jnp.zeros((COMPS, nch), jnp.float32)
    for copy in copies[:3]:
        copy.wait()
    for start, first in ((0, TILE - 2), (FIRST_ROWS, 0)):
        for t in range(3):
            for r in range(2):
                lane = start + (2 * t + r) * PITCH
                got = own_row(t, first + r, amp_ref, index_ref, spread_ref, nch)
                out_ref[PIXELS:, lane : lane + TILE] = got
    copies[3].wait()


def packed(cube, amplitude, centre_index, spread):
    hbm = [pltpu.with_memory_space_constraint(v, pltpu.HBM) for v in (cube, amplitude, centre_index, spread)]
    return pl.pallas_call(
        pack_kernel,
        out_shape=pltpu.VMEM((PIXELS + COMPS, cube.shape[1]), jnp.float32),
        in_specs=[pl.BlockSpec(memory_space=pl.ANY)] * 4,
        out_specs=pl.BlockSpec(memory_space=pltpu.VMEM),
        scratch_shapes=[pltpu.VMEM(v.shape, v.dtype) for v in hbm[1:]] + [pltpu.SemaphoreType.DMA((4,))],
        compiler_params=pltpu.CompilerParams(vmem_limit_bytes=VMEM_LIMIT),
        cost_estimate=pl.CostEstimate(flops=1000, bytes_accessed=1_000_000, transcendentals=0),
        name="pack",
    )(*hbm)


def border_columns(ext_ref, shift):
    lane = lax.broadcasted_iota(jnp.int32, (COMPS, EXT), 1) % PITCH
    total = jnp.zeros((COMPS, EXT), jnp.float32)
    for t in range(3):
        moved = pltpu.roll(ext_ref[t], (2 * t - shift) % EXT, 1)
        total = jnp.where((lane >= 2 * t) & (lane < 2 * t + 2), moved, total)
    return total


def with_rows(own, above, below):
    row = lax.broadcasted_iota(jnp.int32, (COMPS, EXT), 1) // PITCH
    out = []
    for t in range(3):
        p = jnp.where(row < 2, pltpu.roll(above, (EXT - 2 * t * PITCH) % EXT, 1), own[t])
        out.append(jnp.where(row >= TILE + 2, pltpu.roll(below, ((TILE + 2 - 2 * t) * PITCH - FIRST_ROWS) % EXT, 1), p))
    return out


def up_and_down(p):
    return pltpu.roll(p, PITCH, 1) + pltpu.roll(p, EXT - PITCH, 1)


def smoothed(params, left, right):
    lane = lax.broadcasted_iota(jnp.int32, (COMPS, EXT), 1)
    column = lane % PITCH
    at_left, at_right = column == 0, column == TILE - 1
    y = lane // PITCH + (lax.axis_index("skyy") * TILE - 2)
    on_sky = (y >= 0) & (y < lax.axis_size("skyy") * TILE)
    ix = lax.axis_index("skyx")
    beside = on_sky & ((at_left & (ix > 0)) | (at_right & (ix < lax.axis_size("skyx") - 1)))

    def laplacian(p, side):
        before = jnp.where(at_left, side, pltpu.roll(p, 1, 1))
        after = jnp.where(at_right, side, pltpu.roll(p, EXT - 1, 1))
        return 4.0 * p - ((before + after) + up_and_down(p))

    out = []
    for t, p in enumerate(params):
        lefts = [pltpu.roll(left, (EXT - 2 * t - 1 + i) % EXT, 1) for i in range(2)]
        rights = [pltpu.roll(right, (TILE - 1 - 2 * t - i) % EXT, 1) for i in range(2)]
        one, two = [jnp.where(at_left, a, b) for a, b in zip(lefts, rights)]
        first = jnp.where(on_sky, laplacian(p, one), 0.0)
        first_beside = jnp.where(beside, 4.0 * one - ((two + p) + up_and_down(one)), 0.0)
        new = p - (STEPS[t] * LAMS[t]) * laplacian(first, first_beside)
        out.append(pltpu.roll(new, EXT - OWN, 1)[:, :PIXELS])
    return out


def five(v, flag=None):
    total = (v[0] + v[4]) + 4.0 * (v[1] + v[3]) + 6.0 * v[2]
    return total if flag is None else total * flag


def split(v):
    high = v.astype(jnp.bfloat16)
    return high, (v - high.astype(jnp.float32)).astype(jnp.bfloat16)


def column_kind():
    ix = lax.axis_index("skyx")
    kind = jnp.where(ix == 0, 0, jnp.where(ix == lax.axis_size("skyx") - 1, 2, 1))
    return 2 * kind + lax.rem(ix, 2)


def wavelet_kernel(
    a_ref, m1, p1, m2, p2, x_ref, k_ref, own_ref, w_ref,
    o_0, swap_ref, near_ref, far_ref, ext_ref, rows_ref, y_ref,
):
    nch = x_ref.shape[1]
    tiles = (m2, m1, x_ref, p1, p2)
    iy, ix = lax.axis_index("skyy"), lax.axis_index("skyx")
    near = [iy + i for i in (-2, -1, 0, 1, 2)]
    flags = [jnp.where((i >= 0) & (i < lax.axis_size("skyy")), 1.0, 0.0) for i in near]

    lane_tiles = nch // LANES

    def row_pass(step, carry):
        sub = pl.ds(pl.multiple_of((step // lane_tiles) * 8, 8), 8)
        lane = pl.ds(pl.multiple_of((step % lane_tiles) * LANES, LANES), LANES)

        @functools.cache
        def value(level, at):
            tile = (at + 2 * TILE) // TILE
            if level == 0:
                if tile in (1, 2, 3):
                    start = pl.multiple_of(at % TILE * TILE + step // lane_tiles * 8, 8)
                    return tiles[tile][pl.ds(start, 8), lane]
                return tiles[tile][at % TILE - (BEYOND if tile == 0 else 0), sub, lane]
            gap = 2 ** (level - 1)
            taps = [value(level - 1, at + (t - 2) * gap) for t in range(5)]
            return five(taps, None if tile == 2 else flags[tile])

        reach = {1: 28, 2: 24, 3: 16, 4: 0}
        lag = {1: 2, 2: 6, 3: 14, 4: 30}
        for at in range(-30, TILE + 30):
            value(0, at)
            for level in range(1, LEVELS + 1):
                row = at - lag[level]
                if -reach[level] <= row < TILE + reach[level]:
                    got = value(level, row)
                    if 0 <= row < TILE:
                        rows_ref[level - 1, row, sub, lane] = got
        return carry

    lax.fori_loop(0, 2 * lane_tiles, row_pass, 0)

    half, quarter = nch // 2, nch // 4

    for level in range(LEVELS):
        high, low = split(rows_ref[level].reshape(PIXELS, nch))
        parts, index = [high, low], [level, level]
        if level >= 2:
            parts, index = parts + [high], index + [level + 2]
        first, middle, last = [
            jnp.dot(
                jnp.concatenate([v[:, at : at + half] for v in parts], axis=1),
                jnp.concatenate([w_ref[j, i] for j in index], axis=0),
                preferred_element_type=jnp.float32,
            )
            for i, at in enumerate((0, quarter, half))
        ]
        pieces = (
            first[:, :quarter],
            first[:, quarter:] + middle[:, :quarter],
            middle[:, quarter:] + last[:, :quarter],
            last[:, quarter:],
        )
        for i, piece in enumerate(pieces):
            lane = slice(i * quarter, (i + 1) * quarter)
            high, low = split(piece * a_ref[level + 1, :, lane])
            high = high.reshape(TILE, TILE, quarter)
            y_ref[:, level * TILE : (level + 1) * TILE, lane] = high
            at = (level + LEVELS) * TILE
            y_ref[:, at : at + TILE, lane] = low.reshape(TILE, TILE, quarter)
            if level >= 2:
                at = (level + 6) * TILE
                y_ref[:, at : at + TILE, lane] = high

    odd = lax.rem(ix, 2)
    columns = k_ref[column_kind()]

    for row in range(TILE):
        got = jnp.dot(columns, y_ref[row], preferred_element_type=jnp.float32)
        at = slice(row * TILE, (row + 1) * TILE)
        swap_ref[at] = got[:TILE]
        swap_ref[row * TILE + PIXELS : (row + 1) * TILE + PIXELS] = got[TILE : 2 * TILE]
        far_ref[row * REACHED : (row + 1) * REACHED] = got[2 * TILE : 2 * TILE + REACHED]
        o_0[row] = got[3 * TILE : 4 * TILE] + a_ref[0] * x_ref[at]
        near_ref[at] = got[4 * TILE :]

    params = with_rows(own_ref, m1[PIXELS:, :EXT], p1[PIXELS:, :EXT])
    for t in range(3):
        ext_ref[t] = params[t]
    to_right, to_left = border_columns(ext_ref, TILE - 2), border_columns(ext_ref, 0)
    swap_ref[2 * PIXELS : 2 * PIXELS + COMPS, :EXT] = jnp.where(odd == 0, to_right, to_left)
    swap_ref[2 * PIXELS + COMPS :, :EXT] = jnp.where(odd == 0, to_left, to_right)


def kept(x):
    return pltpu.with_memory_space_constraint(x, pltpu.VMEM)


def wavelet_parts(coeff, tiles, own, w, nch, length):
    k = jnp.asarray(scatter_matrices(length))
    vmem = pl.BlockSpec(memory_space=pltpu.VMEM)
    heights = (2 * (PIXELS + COMPS), PIXELS, FAR_ROWS)
    shapes = [(TILE, TILE, nch)] + [(n, nch) for n in heights] + [own.shape]
    return pl.pallas_call(
        wavelet_kernel,
        out_shape=[pltpu.VMEM(shape, jnp.float32) for shape in shapes],
        in_specs=[vmem] * 9,
        out_specs=[vmem] * 5,
        scratch_shapes=[
            pltpu.VMEM((LEVELS, TILE, TILE, nch), jnp.float32),
            pltpu.VMEM((TILE, 10 * TILE, nch), jnp.bfloat16),
        ],
        compiler_params=pltpu.CompilerParams(vmem_limit_bytes=VMEM_LIMIT),
        cost_estimate=pl.CostEstimate(flops=4_000_000_000, bytes_accessed=9_000_000, transcendentals=0),
        name="wavelet_parts",
    )(*[kept(x) for x in (coeff, *tiles, k, own, w)])


def add_kernel(near_ref, swapped_ref, out_ref):
    def body(row, carry):
        at = pl.ds(pl.multiple_of(row * TILE, TILE), TILE)
        more = pl.ds(pl.multiple_of(row * TILE + PIXELS, TILE), TILE)
        out_ref[at] = near_ref[at] + swapped_ref[more]
        return carry

    lax.fori_loop(0, TILE, body, 0, unroll=4)
    out_ref[PIXELS:, :] = swapped_ref[2 * PIXELS + COMPS :]


def outward(near, swapped):
    vmem = pl.BlockSpec(memory_space=pltpu.VMEM)
    return pl.pallas_call(
        add_kernel,
        out_shape=pltpu.VMEM((PIXELS + COMPS, near.shape[1]), jnp.float32),
        in_specs=[vmem] * 2,
        out_specs=vmem,
        compiler_params=pltpu.CompilerParams(vmem_limit_bytes=VMEM_LIMIT),
        cost_estimate=pl.CostEstimate(flops=100_000, bytes_accessed=1_500_000, transcendentals=0),
        name="outward",
    )(kept(near), kept(swapped))


def model_kernel(amp_ref, index_ref, spread_ref, w_hbm, model_ref, flat_ref, own_ref, w_ref, bump_ref, scale_ref, sem):
    load = pltpu.make_async_copy(w_hbm, w_ref, sem)
    load.start()
    nch, pixels = model_ref.shape
    own_ref[...] = jnp.zeros_like(own_ref)
    for t in range(3):
        for row in range(TILE):
            got = own_row(t, row, amp_ref, index_ref, spread_ref, nch)
            at = (row + 2) * PITCH
            own_ref[t, :, at : at + TILE] = got
            flat_ref[t, :, row * TILE : (row + 1) * TILE] = got
    mu = flat_ref[1] * float(nch)
    inv = 1.0 / flat_ref[2]
    flat_ref[1] = mu
    flat_ref[2] = inv
    scale_ref[...] = (-0.5 * math.log2(math.e)) * inv * inv

    def body(step, carry):
        base = pl.multiple_of(step * 8, 8)
        chan = (lax.broadcasted_iota(jnp.int32, (8, pixels), 0) + base).astype(jnp.float32)
        total = jnp.zeros((8, pixels), jnp.float32)
        for k in range(COMPS):
            diff = chan - flat_ref[1, k : k + 1, :]
            bump = jnp.exp2(diff * diff * scale_ref[k : k + 1, :])
            bump_ref[k, pl.ds(base, 8), :] = bump
            total += flat_ref[0, k : k + 1, :] * bump
        model_ref[pl.ds(base, 8), :] = total
        return carry

    lax.fori_loop(0, nch // 8, body, 0, unroll=2)
    load.wait()


def model_of(amplitude, centre_index, spread, nch):
    w = jnp.asarray(channel_matrices(nch))
    vmem = pl.BlockSpec(memory_space=pltpu.VMEM)
    pixels = TILE * TILE
    return pl.pallas_call(
        model_kernel,
        out_shape=[
            pltpu.VMEM((nch, pixels), jnp.float32),
            pltpu.VMEM((3, COMPS, pixels), jnp.float32),
            pltpu.VMEM((3, COMPS, EXT), jnp.float32),
            pltpu.VMEM(w.shape, w.dtype),
            pltpu.VMEM((COMPS, nch, pixels), jnp.float32),
        ],
        in_specs=[vmem] * 3 + [pl.BlockSpec(memory_space=pl.ANY)],
        out_specs=[vmem] * 5,
        scratch_shapes=[pltpu.VMEM((COMPS, pixels), jnp.float32), pltpu.SemaphoreType.DMA],
        compiler_params=pltpu.CompilerParams(vmem_limit_bytes=VMEM_LIMIT),
        cost_estimate=pl.CostEstimate(flops=10_000_000, bytes_accessed=1_000_000, transcendentals=1_100_000),
        name="gaussian_model",
    )(amplitude, centre_index, spread, pltpu.with_memory_space_constraint(w, pltpu.HBM))


def early_kernel(o_0, swapped_ref, far_ref, model_ref, part_ref, r_ref):
    nch, pixels = model_ref.shape
    even = lax.rem(lax.axis_index("skyx"), 2) == 0
    place = lax.broadcasted_iota(jnp.int32, (TILE, nch), 0)
    for row in range(TILE):
        far = far_ref[row * REACHED : row * REACHED + TILE]
        far = jnp.where(place < REACHED, far, 0.0)
        far = jnp.where(even, pltpu.roll(far, BEYOND, 0), far)
        part_ref[row] = (o_0[row] + swapped_ref[row * TILE : (row + 1) * TILE]) + far
    rows = LANES // TILE
    for part in range(pixels // LANES):
        block = part_ref[part * rows : (part + 1) * rows].reshape(LANES, nch)
        at = slice(part * LANES, (part + 1) * LANES)
        r_ref[:, at] = model_ref[:, at] - block.T


def early_part(o_0, swapped, far, model):
    vmem = pl.BlockSpec(memory_space=pltpu.VMEM)
    return pl.pallas_call(
        early_kernel,
        out_shape=[pltpu.VMEM(o_0.shape, jnp.float32), pltpu.VMEM(model.shape, jnp.float32)],
        in_specs=[vmem] * 4,
        out_specs=[vmem] * 2,
        compiler_params=pltpu.CompilerParams(vmem_limit_bytes=VMEM_LIMIT),
        cost_estimate=pl.CostEstimate(flops=2_000_000_000, bytes_accessed=9_000_000, transcendentals=0),
        name="early_part",
    )(*[kept(x) for x in (o_0, swapped, far, model)])


def step_kernel(
    part_ref, early_ref, swapped_ref, near_ref, bump_ref, flat_ref, ext_ref,
    den_hbm, fit_ref, den_ref, r_ref, sem,
):
    nch, pixels = early_ref.shape
    rows = LANES // TILE
    parts = pixels // LANES
    copies = []
    inner, outer = swapped_ref[2 * PIXELS : 2 * PIXELS + COMPS, :EXT], near_ref[PIXELS:, :EXT]
    even = lax.rem(lax.axis_index("skyx"), 2) == 0
    left, right = jnp.where(even, outer, inner), jnp.where(even, inner, outer)
    for part in range(parts):
        at = slice(part * rows, (part + 1) * rows)
        for row in range(part * rows, (part + 1) * rows):
            flat = slice(row * TILE, (row + 1) * TILE)
            den_ref[row] = part_ref[row] + near_ref[flat]
        copies.append(pltpu.make_async_copy(den_ref.at[at], den_hbm.at[at], sem.at[part]))
        copies[-1].start()

    bases = smoothed([ext_ref[t] for t in range(3)], left, right)
    shape = (COMPS, rows, LANES)
    own_lanes = lax.broadcasted_iota(jnp.int32, shape, 2) // TILE == lax.broadcasted_iota(jnp.int32, shape, 1)
    for part in range(parts):
        at = slice(part * LANES, (part + 1) * LANES)
        r_ref[:, at] = early_ref[:, at] - near_ref[at].T

    for part in range(parts):
        at = slice(part * LANES, (part + 1) * LANES)
        sums = [[] for _ in range(3)]
        for first in range(0, COMPS, 8):
            chosen = range(first, first + 8)
            mus = [jnp.broadcast_to(flat_ref[1, k : k + 1, at], (8, LANES)) for k in chosen]

            def body(step, carry):
                base = pl.multiple_of(step * 8, 8)
                chan = (lax.broadcasted_iota(jnp.int32, (8, LANES), 0) + base).astype(jnp.float32)
                r = r_ref[pl.ds(base, 8), at]
                out = []
                for k, mu, (a, b, c) in zip(chosen, mus, carry):
                    diff = chan - mu
                    one = r * bump_ref[k, pl.ds(base, 8), at]
                    two = one * diff
                    out.append((a + one, b + two, c + two * diff))
                return tuple(out)

            zero = jnp.zeros((8, LANES), jnp.float32)
            done = lax.fori_loop(0, nch // 8, body, ((zero,) * 3,) * 8, unroll=16)
            for sums_of_one in done:
                for t in range(3):
                    sums[t].append(jnp.sum(sums_of_one[t], axis=0, keepdims=True))
        amp = flat_ref[0, :, at]
        inv = flat_ref[2, :, at]
        slope = amp * inv * inv
        grads = (
            jnp.concatenate(sums[0], axis=0) * (1.0 / nch),
            jnp.concatenate(sums[1], axis=0) * slope,
            jnp.concatenate(sums[2], axis=0) * (slope * inv * (1.0 / nch)),
        )
        for t in range(3):
            new = bases[t][:, at] - STEPS[t] * grads[t]
            spread_out = jnp.where(own_lanes, jnp.broadcast_to(new[:, None, :], own_lanes.shape), 0.0)
            for shift in (LANES // 2, LANES // 4, LANES // 8):
                spread_out = spread_out + pltpu.roll(spread_out, shift, 2)
            fit_ref[t, :, part * rows : (part + 1) * rows, :] = spread_out[:, :, :TILE]

    for copy in copies:
        copy.wait()


def gradient_step(part, early, swapped, near, bump, flat, ext):
    vmem = pl.BlockSpec(memory_space=pltpu.VMEM)
    shape = part.shape
    return pl.pallas_call(
        step_kernel,
        out_shape=[
            jax.ShapeDtypeStruct(shape, jnp.float32),
            jax.ShapeDtypeStruct((3, COMPS, TILE, TILE), jnp.float32),
        ],
        in_specs=[vmem] * 7,
        out_specs=[pl.BlockSpec(memory_space=pl.ANY), vmem],
        scratch_shapes=[
            pltpu.VMEM(shape, jnp.float32),
            pltpu.VMEM(early.shape, jnp.float32),
            pltpu.SemaphoreType.DMA((2,)),
        ],
        compiler_params=pltpu.CompilerParams(vmem_limit_bytes=VMEM_LIMIT),
        cost_estimate=pl.CostEstimate(flops=15_000_000, bytes_accessed=4_000_000, transcendentals=1_100_000),
        name="gradient_step",
    )(*[kept(x) for x in (part, early, swapped, near, bump, flat, ext)])


def on_device(cube, level_table, level_index, amplitude, centre_index, spread):
    nch = cube.shape[2]
    size = lax.axis_size("skyx")
    partner = [(i, i ^ 1) for i in range(size)]

    tile = packed(cube.reshape(PIXELS, nch), amplitude, centre_index, spread)
    up1, down1 = sent(tile, "skyy", 1), sent(tile, "skyy", -1)
    up2, down2 = sent(cube[BEYOND:], "skyy", 2), sent(cube[:-BEYOND], "skyy", -2)

    entries = jnp.arange(level_table.shape[0], dtype=jnp.int32)
    picks = (level_index[:, :, None] == entries).astype(jnp.float32)
    weight = jnp.sum(picks * level_table, axis=2)
    one = jnp.ones((1, nch), jnp.float32)
    coeff = jnp.concatenate([weight, one]) - jnp.concatenate([0.0 * one, weight])
    scale = jnp.array([16.0 ** (-3 * j) for j in range(LEVELS + 1)], jnp.float32)
    coeff = (coeff * scale[:, None])[:, None, :]
    model, flat, own, w, bump = model_of(amplitude, centre_index, spread, nch)
    o_0, swap, near, far, ext = wavelet_parts(coeff, (up1, down1, up2, down2, tile), own, w, nch, size * TILE)

    swapped = lax.ppermute(swap, "skyx", partner)
    far = away(far, "skyx", 2)
    near = away(outward(near, swapped), "skyx", -2)
    part, early = early_part(o_0, swapped, far, model)
    return gradient_step(part, early, swapped, near, bump, flat, ext)


def solution(mesh):
    placed = (
        P("skyy", "skyx", None),
        P(),
        P(),
        P(None, "skyy", "skyx"),
        P(None, "skyy", "skyx"),
        P(None, "skyy", "skyx"),
    )
    return jax.shard_map(
        on_device,
        mesh=mesh,
        in_specs=placed,
        out_specs=(P("skyy", "skyx", None), P(None, None, "skyy", "skyx")),
        check_vma=False,
    )
```

```python
import functools
import math

import jax
import jax.numpy as jnp
import numpy as np
from jax import lax
from jax.experimental import pallas as pl
from jax.experimental.pallas import tpu as pltpu
from jax.sharding import PartitionSpec as P

TILE = 16
LEVELS = 4
COMPS = 8
LANES = 128
TAPS = (1, 4, 6, 4, 1)
BEYOND = 2
REACHED = TILE - BEYOND
FAR_ROWS = TILE * REACHED + 8
VMEM_LIMIT = 20 * 1024 * 1024
ROLES = ((3, 1, 0, 2, 4), (1, 3, 4, 2, 0))
PIXELS = TILE * TILE
PITCH = TILE
EXT = 384
OWN = 2 * PITCH
FIRST_ROWS = 128
STEPS = (0.5, 0.002, 2.0)
LAMS = (0.2, 0.5, 0.05)


def blur_matrix(length, gap):
    out = np.zeros((length, length), np.float64)
    for tap, factor in enumerate(TAPS):
        offset = (tap - 2) * gap
        for i in range(max(0, -offset), min(length, length - offset)):
            out[i, i + offset] = factor
    return out


def composites(length):
    made, now = [], np.eye(length)
    for level in range(LEVELS):
        now = blur_matrix(length, 2**level) @ now
        made.append(now)
    return made


def halves(matrix):
    bf16 = jnp.bfloat16
    high = np.asarray(matrix, np.float32).astype(bf16)
    low = (np.asarray(matrix, np.float32) - high.astype(np.float32)).astype(bf16)
    return high, low


def channel_matrices(nch):
    parts = [halves(m.T) for m in composites(nch)]
    half, quarter = nch // 2, nch // 4
    out = []
    for whole in [p[0] for p in parts] + [p[1] for p in parts[2:]]:
        across = whole[quarter : quarter + half, quarter : quarter + half].copy()
        across[:quarter, :quarter] = 0
        across[quarter:, quarter:] = 0
        out.append(np.stack([whole[:half, :half], across, whole[half:, half:]]))
    return np.stack(out)


def scatter_matrices(length):
    whole = composites(length)
    kinds = []
    for start in (0, TILE * (length // TILE // 2), length - TILE):
        parts = []
        for m in whole:
            block = np.zeros((5 * TILE, TILE))
            for k in range(5 * TILE):
                at = start - 2 * TILE + k
                if 0 <= at < length:
                    block[k] = m[at, start : start + TILE]
            parts.append(halves(block))
        high = np.concatenate([p[0] for p in parts], axis=1)
        low = np.concatenate([p[1] for p in parts[2:]], axis=1)
        columns = np.concatenate([high, high, low], axis=1).reshape(5, TILE, -1)
        for order in ROLES:
            blocks = [columns[i] for i in order]
            if order[2] == 0:
                blocks[2] = np.roll(blocks[2], -BEYOND, axis=0)
            kinds.append(np.concatenate(blocks))
    return np.stack(kinds)


def sent(values, axis, by):
    size = lax.axis_size(axis)
    if by > 0:
        pairs = [(i, i + by) for i in range(size - by)]
    else:
        pairs = [(i, i + by) for i in range(-by, size)]
    return lax.ppermute(values, axis, pairs)


def away(values, axis, by):
    size = lax.axis_size(axis)
    pairs = [(i, i + by if i % 2 else i - by) for i in range(size)]
    return lax.ppermute(values, axis, [(i, j) for i, j in pairs if 0 <= j < size])


def own_row(t, row, amp_ref, index_ref, spread_ref, nch):
    if t == 0:
        return amp_ref[:, row, :]
    if t == 1:
        return (index_ref[:, row, :].astype(jnp.float32) + 0.5) * (1.0 / nch)
    return spread_ref[:, row, :]


def pack_kernel(cube_hbm, amp_hbm, index_hbm, spread_hbm, out_ref, amp_ref, index_ref, spread_ref, sem):
    pairs = ((amp_hbm, amp_ref), (index_hbm, index_ref), (spread_hbm, spread_ref), (cube_hbm, out_ref.at[0:PIXELS]))
    copies = [pltpu.make_async_copy(a, b, sem.at[i]) for i, (a, b) in enumerate(pairs)]
    for copy in copies:
        copy.start()
    nch = cube_hbm.shape[1]
    out_ref[PIXELS:, :] = jnp.zeros((COMPS, nch), jnp.float32)
    for copy in copies[:3]:
        copy.wait()
    for start, first in ((0, TILE - 2), (FIRST_ROWS, 0)):
        for t in range(3):
            for r in range(2):
                lane = start + (2 * t + r) * PITCH
                got = own_row(t, first + r, amp_ref, index_ref, spread_ref, nch)
                out_ref[PIXELS:, lane : lane + TILE] = got
    copies[3].wait()


def packed(cube, amplitude, centre_index, spread):
    hbm = [pltpu.with_memory_space_constraint(v, pltpu.HBM) for v in (cube, amplitude, centre_index, spread)]
    return pl.pallas_call(
        pack_kernel,
        out_shape=pltpu.VMEM((PIXELS + COMPS, cube.shape[1]), jnp.float32),
        in_specs=[pl.BlockSpec(memory_space=pl.ANY)] * 4,
        out_specs=pl.BlockSpec(memory_space=pltpu.VMEM),
        scratch_shapes=[pltpu.VMEM(v.shape, v.dtype) for v in hbm[1:]] + [pltpu.SemaphoreType.DMA((4,))],
        compiler_params=pltpu.CompilerParams(vmem_limit_bytes=VMEM_LIMIT),
        cost_estimate=pl.CostEstimate(flops=1000, bytes_accessed=1_000_000, transcendentals=0),
        name="pack",
    )(*hbm)


def border_columns(ext_ref, shift):
    lane = lax.broadcasted_iota(jnp.int32, (COMPS, EXT), 1) % PITCH
    total = jnp.zeros((COMPS, EXT), jnp.float32)
    for t in range(3):
        moved = pltpu.roll(ext_ref[t], (2 * t - shift) % EXT, 1)
        total = jnp.where((lane >= 2 * t) & (lane < 2 * t + 2), moved, total)
    return total


def with_rows(own, above, below):
    row = lax.broadcasted_iota(jnp.int32, (COMPS, EXT), 1) // PITCH
    out = []
    for t in range(3):
        p = jnp.where(row < 2, pltpu.roll(above, (EXT - 2 * t * PITCH) % EXT, 1), own[t])
        out.append(jnp.where(row >= TILE + 2, pltpu.roll(below, ((TILE + 2 - 2 * t) * PITCH - FIRST_ROWS) % EXT, 1), p))
    return out


def up_and_down(p):
    return pltpu.roll(p, PITCH, 1) + pltpu.roll(p, EXT - PITCH, 1)


def smoothed(params, left, right):
    lane = lax.broadcasted_iota(jnp.int32, (COMPS, EXT), 1)
    column = lane % PITCH
    at_left, at_right = column == 0, column == TILE - 1
    y = lane // PITCH + (lax.axis_index("skyy") * TILE - 2)
    on_sky = (y >= 0) & (y < lax.axis_size("skyy") * TILE)
    ix = lax.axis_index("skyx")
    beside = on_sky & ((at_left & (ix > 0)) | (at_right & (ix < lax.axis_size("skyx") - 1)))

    def laplacian(p, side):
        before = jnp.where(at_left, side, pltpu.roll(p, 1, 1))
        after = jnp.where(at_right, side, pltpu.roll(p, EXT - 1, 1))
        return 4.0 * p - ((before + after) + up_and_down(p))

    out = []
    for t, p in enumerate(params):
        lefts = [pltpu.roll(left, (EXT - 2 * t - 1 + i) % EXT, 1) for i in range(2)]
        rights = [pltpu.roll(right, (TILE - 1 - 2 * t - i) % EXT, 1) for i in range(2)]
        one, two = [jnp.where(at_left, a, b) for a, b in zip(lefts, rights)]
        first = jnp.where(on_sky, laplacian(p, one), 0.0)
        first_beside = jnp.where(beside, 4.0 * one - ((two + p) + up_and_down(one)), 0.0)
        new = p - (STEPS[t] * LAMS[t]) * laplacian(first, first_beside)
        out.append(pltpu.roll(new, EXT - OWN, 1)[:, :PIXELS])
    return out


def five(v, flag=None):
    total = (v[0] + v[4]) + 4.0 * (v[1] + v[3]) + 6.0 * v[2]
    return total if flag is None else total * flag


def split(v):
    high = v.astype(jnp.bfloat16)
    return high, (v - high.astype(jnp.float32)).astype(jnp.bfloat16)


def column_kind():
    ix = lax.axis_index("skyx")
    kind = jnp.where(ix == 0, 0, jnp.where(ix == lax.axis_size("skyx") - 1, 2, 1))
    return 2 * kind + lax.rem(ix, 2)


def wavelet_kernel(
    a_ref, m1, p1, m2, p2, x_ref, k_ref, own_ref, w_ref,
    o_0, swap_ref, near_ref, far_ref, ext_ref, rows_ref, y_ref,
):
    nch = x_ref.shape[1]
    tiles = (m2, m1, x_ref, p1, p2)
    iy, ix = lax.axis_index("skyy"), lax.axis_index("skyx")
    near = [iy + i for i in (-2, -1, 0, 1, 2)]
    flags = [jnp.where((i >= 0) & (i < lax.axis_size("skyy")), 1.0, 0.0) for i in near]

    lane_tiles = nch // LANES

    def row_pass(step, carry):
        sub = pl.ds(pl.multiple_of((step // lane_tiles) * 8, 8), 8)
        lane = pl.ds(pl.multiple_of((step % lane_tiles) * LANES, LANES), LANES)

        @functools.cache
        def value(level, at):
            tile = (at + 2 * TILE) // TILE
            if level == 0:
                if tile in (1, 2, 3):
                    start = pl.multiple_of(at % TILE * TILE + step // lane_tiles * 8, 8)
                    return tiles[tile][pl.ds(start, 8), lane]
                return tiles[tile][at % TILE - (BEYOND if tile == 0 else 0), sub, lane]
            gap = 2 ** (level - 1)
            taps = [value(level - 1, at + (t - 2) * gap) for t in range(5)]
            return five(taps, None if tile == 2 else flags[tile])

        reach = {1: 28, 2: 24, 3: 16, 4: 0}
        lag = {1: 2, 2: 6, 3: 14, 4: 30}
        for at in range(-30, TILE + 30):
            value(0, at)
            for level in range(1, LEVELS + 1):
                row = at - lag[level]
                if -reach[level] <= row < TILE + reach[level]:
                    got = value(level, row)
                    if 0 <= row < TILE:
                        rows_ref[level - 1, row, sub, lane] = got
        return carry

    lax.fori_loop(0, 2 * lane_tiles, row_pass, 0)

    half, quarter = nch // 2, nch // 4

    for level in range(LEVELS):
        high, low = split(rows_ref[level].reshape(PIXELS, nch))
        parts, index = [high, low], [level, level]
        if level >= 2:
            parts, index = parts + [high], index + [level + 2]
        first, middle, last = [
            jnp.dot(
                jnp.concatenate([v[:, at : at + half] for v in parts], axis=1),
                jnp.concatenate([w_ref[j, i] for j in index], axis=0),
                preferred_element_type=jnp.float32,
            )
            for i, at in enumerate((0, quarter, half))
        ]
        pieces = (
            first[:, :quarter],
            first[:, quarter:] + middle[:, :quarter],
            middle[:, quarter:] + last[:, :quarter],
            last[:, quarter:],
        )
        for i, piece in enumerate(pieces):
            lane = slice(i * quarter, (i + 1) * quarter)
            high, low = split(piece * a_ref[level + 1, :, lane])
            high = high.reshape(TILE, TILE, quarter)
            y_ref[:, level * TILE : (level + 1) * TILE, lane] = high
            at = (level + LEVELS) * TILE
            y_ref[:, at : at + TILE, lane] = low.reshape(TILE, TILE, quarter)
            if level >= 2:
                at = (level + 6) * TILE
                y_ref[:, at : at + TILE, lane] = high

    odd = lax.rem(ix, 2)
    columns = k_ref[column_kind()]

    for row in range(TILE):
        got = jnp.dot(columns, y_ref[row], preferred_element_type=jnp.float32)
        at = slice(row * TILE, (row + 1) * TILE)
        swap_ref[at] = got[:TILE]
        swap_ref[row * TILE + PIXELS : (row + 1) * TILE + PIXELS] = got[TILE : 2 * TILE]
        far_ref[row * REACHED : (row + 1) * REACHED] = got[2 * TILE : 2 * TILE + REACHED]
        o_0[row] = got[3 * TILE : 4 * TILE] + a_ref[0] * x_ref[at]
        near_ref[at] = got[4 * TILE :]

    params = with_rows(own_ref, m1[PIXELS:, :EXT], p1[PIXELS:, :EXT])
    for t in range(3):
        ext_ref[t] = params[t]
    to_right, to_left = border_columns(ext_ref, TILE - 2), border_columns(ext_ref, 0)
    swap_ref[2 * PIXELS : 2 * PIXELS + COMPS, :EXT] = jnp.where(odd == 0, to_right, to_left)
    swap_ref[2 * PIXELS + COMPS :, :EXT] = jnp.where(odd == 0, to_left, to_right)


def kept(x):
    return pltpu.with_memory_space_constraint(x, pltpu.VMEM)


def wavelet_parts(coeff, tiles, own, w, nch, length):
    k = jnp.asarray(scatter_matrices(length))
    vmem = pl.BlockSpec(memory_space=pltpu.VMEM)
    heights = (2 * (PIXELS + COMPS), PIXELS, FAR_ROWS)
    shapes = [(TILE, TILE, nch)] + [(n, nch) for n in heights] + [own.shape]
    return pl.pallas_call(
        wavelet_kernel,
        out_shape=[pltpu.VMEM(shape, jnp.float32) for shape in shapes],
        in_specs=[vmem] * 9,
        out_specs=[vmem] * 5,
        scratch_shapes=[
            pltpu.VMEM((LEVELS, TILE, TILE, nch), jnp.float32),
            pltpu.VMEM((TILE, 10 * TILE, nch), jnp.bfloat16),
        ],
        compiler_params=pltpu.CompilerParams(vmem_limit_bytes=VMEM_LIMIT),
        cost_estimate=pl.CostEstimate(flops=4_000_000_000, bytes_accessed=9_000_000, transcendentals=0),
        name="wavelet_parts",
    )(*[kept(x) for x in (coeff, *tiles, k, own, w)])


def add_kernel(near_ref, swapped_ref, out_ref):
    def body(row, carry):
        at = pl.ds(pl.multiple_of(row * TILE, TILE), TILE)
        more = pl.ds(pl.multiple_of(row * TILE + PIXELS, TILE), TILE)
        out_ref[at] = near_ref[at] + swapped_ref[more]
        return carry

    lax.fori_loop(0, TILE, body, 0, unroll=4)
    out_ref[PIXELS:, :] = swapped_ref[2 * PIXELS + COMPS :]


def outward(near, swapped):
    vmem = pl.BlockSpec(memory_space=pltpu.VMEM)
    return pl.pallas_call(
        add_kernel,
        out_shape=pltpu.VMEM((PIXELS + COMPS, near.shape[1]), jnp.float32),
        in_specs=[vmem] * 2,
        out_specs=vmem,
        compiler_params=pltpu.CompilerParams(vmem_limit_bytes=VMEM_LIMIT),
        cost_estimate=pl.CostEstimate(flops=100_000, bytes_accessed=1_500_000, transcendentals=0),
        name="outward",
    )(kept(near), kept(swapped))


def model_kernel(amp_ref, index_ref, spread_ref, w_hbm, model_ref, flat_ref, own_ref, w_ref, bump_ref, scale_ref, sem):
    load = pltpu.make_async_copy(w_hbm, w_ref, sem)
    load.start()
    nch, pixels = model_ref.shape
    own_ref[...] = jnp.zeros_like(own_ref)
    for t in range(3):
        for row in range(TILE):
            got = own_row(t, row, amp_ref, index_ref, spread_ref, nch)
            at = (row + 2) * PITCH
            own_ref[t, :, at : at + TILE] = got
            flat_ref[t, :, row * TILE : (row + 1) * TILE] = got
    mu = flat_ref[1] * float(nch)
    inv = 1.0 / flat_ref[2]
    flat_ref[1] = mu
    flat_ref[2] = inv
    scale_ref[...] = (-0.5 * math.log2(math.e)) * inv * inv

    def body(step, carry):
        base = pl.multiple_of(step * 8, 8)
        chan = (lax.broadcasted_iota(jnp.int32, (8, pixels), 0) + base).astype(jnp.float32)
        total = jnp.zeros((8, pixels), jnp.float32)
        for k in range(COMPS):
            diff = chan - flat_ref[1, k : k + 1, :]
            bump = jnp.exp2(diff * diff * scale_ref[k : k + 1, :])
            bump_ref[k, pl.ds(base, 8), :] = bump
            total += flat_ref[0, k : k + 1, :] * bump
        model_ref[pl.ds(base, 8), :] = total
        return carry

    lax.fori_loop(0, nch // 8, body, 0, unroll=2)
    load.wait()


def model_of(amplitude, centre_index, spread, nch):
    w = jnp.asarray(channel_matrices(nch))
    vmem = pl.BlockSpec(memory_space=pltpu.VMEM)
    pixels = TILE * TILE
    return pl.pallas_call(
        model_kernel,
        out_shape=[
            pltpu.VMEM((nch, pixels), jnp.float32),
            pltpu.VMEM((3, COMPS, pixels), jnp.float32),
            pltpu.VMEM((3, COMPS, EXT), jnp.float32),
            pltpu.VMEM(w.shape, w.dtype),
            pltpu.VMEM((COMPS, nch, pixels), jnp.float32),
        ],
        in_specs=[vmem] * 3 + [pl.BlockSpec(memory_space=pl.ANY)],
        out_specs=[vmem] * 5,
        scratch_shapes=[pltpu.VMEM((COMPS, pixels), jnp.float32), pltpu.SemaphoreType.DMA],
        compiler_params=pltpu.CompilerParams(vmem_limit_bytes=VMEM_LIMIT),
        cost_estimate=pl.CostEstimate(flops=10_000_000, bytes_accessed=1_000_000, transcendentals=1_100_000),
        name="gaussian_model",
    )(amplitude, centre_index, spread, pltpu.with_memory_space_constraint(w, pltpu.HBM))


def early_kernel(o_0, swapped_ref, far_ref, model_ref, part_ref, r_ref):
    nch, pixels = model_ref.shape
    even = lax.rem(lax.axis_index("skyx"), 2) == 0
    place = lax.broadcasted_iota(jnp.int32, (TILE, nch), 0)
    for row in range(TILE):
        far = far_ref[row * REACHED : row * REACHED + TILE]
        far = jnp.where(place < REACHED, far, 0.0)
        far = jnp.where(even, pltpu.roll(far, BEYOND, 0), far)
        part_ref[row] = (o_0[row] + swapped_ref[row * TILE : (row + 1) * TILE]) + far
    rows = LANES // TILE
    for part in range(pixels // LANES):
        block = part_ref[part * rows : (part + 1) * rows].reshape(LANES, nch)
        at = slice(part * LANES, (part + 1) * LANES)
        r_ref[:, at] = model_ref[:, at] - block.T


def early_part(o_0, swapped, far, model):
    vmem = pl.BlockSpec(memory_space=pltpu.VMEM)
    return pl.pallas_call(
        early_kernel,
        out_shape=[pltpu.VMEM(o_0.shape, jnp.float32), pltpu.VMEM(model.shape, jnp.float32)],
        in_specs=[vmem] * 4,
        out_specs=[vmem] * 2,
        compiler_params=pltpu.CompilerParams(vmem_limit_bytes=VMEM_LIMIT),
        cost_estimate=pl.CostEstimate(flops=2_000_000_000, bytes_accessed=9_000_000, transcendentals=0),
        name="early_part",
    )(*[kept(x) for x in (o_0, swapped, far, model)])


def step_kernel(
    part_ref, early_ref, swapped_ref, near_ref, bump_ref, flat_ref, ext_ref,
    den_hbm, fit_ref, den_ref, r_ref, sem,
):
    nch, pixels = early_ref.shape
    rows = LANES // TILE
    parts = pixels // LANES
    copies = []
    inner, outer = swapped_ref[2 * PIXELS : 2 * PIXELS + COMPS, :EXT], near_ref[PIXELS:, :EXT]
    even = lax.rem(lax.axis_index("skyx"), 2) == 0
    left, right = jnp.where(even, outer, inner), jnp.where(even, inner, outer)
    for part in range(parts):
        at = slice(part * rows, (part + 1) * rows)
        for row in range(part * rows, (part + 1) * rows):
            flat = slice(row * TILE, (row + 1) * TILE)
            den_ref[row] = part_ref[row] + near_ref[flat]
        copies.append(pltpu.make_async_copy(den_ref.at[at], den_hbm.at[at], sem.at[part]))
        copies[-1].start()

    bases = smoothed([ext_ref[t] for t in range(3)], left, right)
    shape = (COMPS, rows, LANES)
    own_lanes = lax.broadcasted_iota(jnp.int32, shape, 2) // TILE == lax.broadcasted_iota(jnp.int32, shape, 1)
    for part in range(parts):
        at = slice(part * LANES, (part + 1) * LANES)
        r_ref[:, at] = early_ref[:, at] - near_ref[at].T

    for part in range(parts):
        at = slice(part * LANES, (part + 1) * LANES)
        sums = [[] for _ in range(3)]
        for first in range(0, COMPS, 8):
            chosen = range(first, first + 8)
            mus = [jnp.broadcast_to(flat_ref[1, k : k + 1, at], (8, LANES)) for k in chosen]

            def body(step, carry):
                base = pl.multiple_of(step * 8, 8)
                chan = (lax.broadcasted_iota(jnp.int32, (8, LANES), 0) + base).astype(jnp.float32)
                r = r_ref[pl.ds(base, 8), at]
                out = []
                for k, mu, (a, b, c) in zip(chosen, mus, carry):
                    diff = chan - mu
                    one = r * bump_ref[k, pl.ds(base, 8), at]
                    two = one * diff
                    out.append((a + one, b + two, c + two * diff))
                return tuple(out)

            zero = jnp.zeros((8, LANES), jnp.float32)
            done = lax.fori_loop(0, nch // 8, body, ((zero,) * 3,) * 8, unroll=32)
            for sums_of_one in done:
                for t in range(3):
                    sums[t].append(jnp.sum(sums_of_one[t], axis=0, keepdims=True))
        amp = flat_ref[0, :, at]
        inv = flat_ref[2, :, at]
        slope = amp * inv * inv
        grads = (
            jnp.concatenate(sums[0], axis=0) * (1.0 / nch),
            jnp.concatenate(sums[1], axis=0) * slope,
            jnp.concatenate(sums[2], axis=0) * (slope * inv * (1.0 / nch)),
        )
        for t in range(3):
            new = bases[t][:, at] - STEPS[t] * grads[t]
            spread_out = jnp.where(own_lanes, jnp.broadcast_to(new[:, None, :], own_lanes.shape), 0.0)
            for shift in (LANES // 2, LANES // 4, LANES // 8):
                spread_out = spread_out + pltpu.roll(spread_out, shift, 2)
            fit_ref[t, :, part * rows : (part + 1) * rows, :] = spread_out[:, :, :TILE]

    for copy in copies:
        copy.wait()


def gradient_step(part, early, swapped, near, bump, flat, ext):
    vmem = pl.BlockSpec(memory_space=pltpu.VMEM)
    shape = part.shape
    return pl.pallas_call(
        step_kernel,
        out_shape=[
            jax.ShapeDtypeStruct(shape, jnp.float32),
            jax.ShapeDtypeStruct((3, COMPS, TILE, TILE), jnp.float32),
        ],
        in_specs=[vmem] * 7,
        out_specs=[pl.BlockSpec(memory_space=pl.ANY), vmem],
        scratch_shapes=[
            pltpu.VMEM(shape, jnp.float32),
            pltpu.VMEM(early.shape, jnp.float32),
            pltpu.SemaphoreType.DMA((2,)),
        ],
        compiler_params=pltpu.CompilerParams(vmem_limit_bytes=VMEM_LIMIT),
        cost_estimate=pl.CostEstimate(flops=15_000_000, bytes_accessed=4_000_000, transcendentals=1_100_000),
        name="gradient_step",
    )(*[kept(x) for x in (part, early, swapped, near, bump, flat, ext)])


def on_device(cube, level_table, level_index, amplitude, centre_index, spread):
    nch = cube.shape[2]
    size = lax.axis_size("skyx")
    partner = [(i, i ^ 1) for i in range(size)]

    tile = packed(cube.reshape(PIXELS, nch), amplitude, centre_index, spread)
    up1, down1 = sent(tile, "skyy", 1), sent(tile, "skyy", -1)
    up2, down2 = sent(cube[BEYOND:], "skyy", 2), sent(cube[:-BEYOND], "skyy", -2)

    entries = jnp.arange(level_table.shape[0], dtype=jnp.int32)
    picks = (level_index[:, :, None] == entries).astype(jnp.float32)
    weight = jnp.sum(picks * level_table, axis=2)
    one = jnp.ones((1, nch), jnp.float32)
    coeff = jnp.concatenate([weight, one]) - jnp.concatenate([0.0 * one, weight])
    scale = jnp.array([16.0 ** (-3 * j) for j in range(LEVELS + 1)], jnp.float32)
    coeff = (coeff * scale[:, None])[:, None, :]
    model, flat, own, w, bump = model_of(amplitude, centre_index, spread, nch)
    o_0, swap, near, far, ext = wavelet_parts(coeff, (up1, down1, up2, down2, tile), own, w, nch, size * TILE)

    swapped = lax.ppermute(swap, "skyx", partner)
    far = away(far, "skyx", 2)
    near = away(outward(near, swapped), "skyx", -2)
    part, early = early_part(o_0, swapped, far, model)
    return gradient_step(part, early, swapped, near, bump, flat, ext)


def solution(mesh):
    placed = (
        P("skyy", "skyx", None),
        P(),
        P(),
        P(None, "skyy", "skyx"),
        P(None, "skyy", "skyx"),
        P(None, "skyy", "skyx"),
    )
    return jax.shard_map(
        on_device,
        mesh=mesh,
        in_specs=placed,
        out_specs=(P("skyy", "skyx", None), P(None, None, "skyy", "skyx")),
        check_vma=False,
    )
```
